128 devices in a mesh: lat: 4 (over x_lo, core), lon: 32 (over y, x_hi, z).
Axes of the slice: x: 4 (x_hi: 2, x_lo: 2; x = x_hi * 2 + x_lo), y: 4, z: 4, core: 2. Of those that a mesh axis runs over, the one named last changes fastest.
Arguments:
- feature: bfloat16 [64, 1024, 256], P('lat', 'lon'), may hold values from -6 to 6
- filters: bfloat16 [64, 9, 25], P('lat'), may hold values from -1.25 to 1.25
- start: int32 [64], P('lat'), may hold values from 0 to 63, as said below
- length: int32 [64], P('lat'), may hold values from 1 to 5, as said below
- weight: bfloat16 [9, 256, 256], replicated, may hold values from -0.125 to 0.125
- cotangent: bfloat16 [64, 1024, 256], P('lat', 'lon'), may hold values from -6 to 6
Outputs:
- mixed: bfloat16 [64, 1024, 256], P('lat', 'lon')
- grad_feature: bfloat16 [64, 1024, 256], P('lat', 'lon')
- grad_weight: float32 [9, 256, 256], replicated
The draws below stay inside these ranges and needn't reach their ends.
Inputs may be any that keep to these rules, and one draw needn't show every extreme that they name: start[i] >= max(i - 2, 0) and start[i] + length[i] <= min(i + 3, 64). `length`: some row's support has the full 5 rows.
All inputs are finite; a program needn't handle non-finite values.
Results may differ from the reference program's by a relative error of at most 0.0049.
Values may be sent and summed in bfloat16 or wider, within the bound.
No kernel may reach another device: no remote copies, remote signals or barrier semaphores. Data moves between devices by JAX's collectives and lax.ppermute only.
A program may use at most 128 MiB of HBM per device.

```python
import math
import jax
import jax.numpy as jnp
from jax import lax

CHAN = 256
BASIS = 9
LAT_REACH = 2
LON_REACH = 2
TAPS = 25
NLAT = 64
NLON = 1024


def support_pair(key):
    row_global = jnp.arange(NLAT, dtype=jnp.int32)
    lowest = jnp.maximum(row_global - LAT_REACH, 0)
    highest = jnp.minimum(row_global + LAT_REACH + 1, NLAT)
    key_head, key_tail = jax.random.split(key)
    head_cut = jax.random.randint(key_head, (NLAT,), 0, LAT_REACH + 1)
    tail_cut = jax.random.randint(key_tail, (NLAT,), 0, LAT_REACH + 1 - head_cut)
    full_row = row_global == LAT_REACH
    head_cut = jnp.where(full_row, 0, head_cut)
    tail_cut = jnp.where(full_row, 0, tail_cut)
    return ((lowest + head_cut).astype(jnp.int32), (highest - lowest - head_cut - tail_cut).astype(jnp.int32))


def draw_start(key, part):
    return support_pair(key)[0]


def draw_length(key, part):
    return support_pair(key)[1]


def steps_of(own_key, dims, shards, low, high):
    def one(position, parts):
        draws = jax.random.uniform(jax.random.fold_in(jax.random.fold_in(own_key, 6), position), (parts,), jnp.float32, low / len(shards), high / len(shards))
        return jnp.repeat(jnp.exp(draws), dims[position] // parts).reshape((-1,) + (1,) * (len(dims) - position - 1))

    level = one(*shards[0])
    for cut in shards[1:]:
        level = level * one(*cut)
    return level


def gaussian(key, extent, width, reach, cuts=(), kind=jnp.bfloat16):
    array = jax.random.normal(key, extent, jnp.float32) * width
    if len(cuts) > 0:
        array = steps_of(key, extent, cuts, -0.22, 0.18) * array
    return jnp.clip(array, min=-reach, max=reach).astype(kind)


def setup_inputs(seed: int = 0) -> dict:
    streams_of = jax.random.split(jax.random.key(seed), 7)
    return {
        "feature": gaussian(streams_of[0], (NLAT, NLON, CHAN), 1.0, 6.0, ((0, 4), (1, 32))),
        "filters": gaussian(streams_of[1], (NLAT, BASIS, TAPS), 0.22, 1.25, ((0, 4),)),
        "start": draw_start(jax.random.fold_in(streams_of[6], 71), 0),
        "length": draw_length(jax.random.fold_in(streams_of[6], 71), 0),
        "weight": gaussian(streams_of[4], (BASIS, CHAN, CHAN), (BASIS * CHAN) ** -0.5, 0.125),
        "cotangent": gaussian(streams_of[5], (NLAT, NLON, CHAN), 1.0, 6.0, ((0, 4), (1, 32))),
    }


def support_mask(start, length):
    row_global = jnp.arange(NLAT, dtype=jnp.int32)
    source = row_global[:, None] - LAT_REACH + jnp.arange(2 * LAT_REACH + 1, dtype=jnp.int32)[None, :]
    return (source >= start[:, None]) & (source < (start + length)[:, None])

def reference(feature, filters, start, length, weight, cotangent):
    band_rows = 2 * LAT_REACH + 1
    lon_taps = 2 * LON_REACH + 1
    inside = support_mask(start, length).astype(jnp.float32)
    masked = filters.astype(jnp.float32).reshape(NLAT, BASIS, band_rows, lon_taps) * inside[:, None, :, None]
    masked = masked.reshape(NLAT, BASIS, band_rows * lon_taps)
    widened = jnp.concatenate([feature[:, NLON - LON_REACH:], feature, feature[:, :LON_REACH]], axis=1)
    padded = jnp.pad(widened, ((LAT_REACH, LAT_REACH), (0, 0), (0, 0)))
    mixing = weight.reshape(BASIS * CHAN, CHAN)

    def row_step(grad_total, row_index):
        rows_in = lax.dynamic_slice_in_dim(padded, row_index, band_rows, 0)
        window = jnp.stack([rows_in[lat_tap, lon_tap:lon_tap + NLON] for lat_tap in range(band_rows) for lon_tap in range(lon_taps)], axis=0).astype(jnp.float32)
        taps_row = lax.dynamic_index_in_dim(masked, row_index, 0, keepdims=False)
        basis_out = jnp.einsum('kq,qlc->lkc', taps_row, window, precision=lax.Precision.HIGHEST).astype(jnp.bfloat16)
        flat = basis_out.reshape(NLON, BASIS * CHAN)
        output = jnp.dot(flat, mixing, preferred_element_type=jnp.float32).astype(jnp.bfloat16)
        upstream = lax.dynamic_index_in_dim(cotangent, row_index, 0, keepdims=False)
        grad_back = lax.dot_general(upstream, mixing, (((1,), (1,)), ((), ())), preferred_element_type=jnp.float32).astype(jnp.bfloat16)
        grad_total = grad_total + lax.dot_general(flat, upstream, (((0,), (0,)), ((), ())), preferred_element_type=jnp.float32)
        return (grad_total, (output, grad_back.reshape(NLON, BASIS, CHAN)))
    grad_total, (mixed, grad_basis) = lax.scan(row_step, jnp.zeros((BASIS * CHAN, CHAN), jnp.float32), jnp.arange(NLAT, dtype=jnp.int32))
    grad_weight = (grad_total * (1.0 / math.sqrt(NLAT * NLON))).reshape(BASIS, CHAN, CHAN)
    grad_wide = jnp.concatenate([grad_basis[:, NLON - LON_REACH:], grad_basis, grad_basis[:, :LON_REACH]], axis=1)
    grad_pad = jnp.pad(grad_wide, ((LAT_REACH, LAT_REACH), (0, 0), (0, 0), (0, 0)))
    taps_pad = jnp.pad(masked, ((LAT_REACH, LAT_REACH), (0, 0), (0, 0)))

    def grad_row(row_index):
        accum = jnp.zeros((NLON, CHAN), jnp.float32)
        for lat_tap in range(band_rows):
            source_row = row_index + 2 * LAT_REACH - lat_tap
            taps_here = lax.dynamic_index_in_dim(taps_pad, source_row, 0, keepdims=False)
            grads_row = lax.dynamic_index_in_dim(grad_pad, source_row, 0, keepdims=False).astype(jnp.float32)
            for lon_tap in range(lon_taps):
                tap_index = lat_tap * lon_taps + lon_tap
                offset = 2 * LON_REACH - lon_tap
                accum = accum + jnp.einsum('k,lkc->lc', taps_here[:, tap_index], grads_row[offset:offset + NLON], precision=lax.Precision.HIGHEST)
        return accum.astype(jnp.bfloat16)
    grad_feature = lax.map(grad_row, jnp.arange(NLAT, dtype=jnp.int32))
    return (mixed, grad_feature, grad_weight)
```

```python
import functools
import math

import jax
import numpy as np
import jax.numpy as jnp
from jax import lax
from jax.experimental import pallas as pl
from jax.experimental.pallas import tpu as pltpu
from jax.sharding import Mesh, PartitionSpec as P

AXES = ("xl", "core", "y", "xh", "z")
SIZES = (2, 2, 4, 2, 4)
RING = ("xl", "y", "xh", "z")

ROWS = 16
CELLS = 32
SLOTS = 48
BASIS = 9
CHAN = 256
HALF = 128
BAND = 5
KEEP = 40
bf16 = jnp.bfloat16
f32 = jnp.float32


def moves(lat=False, core=False, lon=0):
    pairs = []
    for xl in range(2):
        for c in range(2):
            for cell in range(32):
                source = (xl * 2 + c) * 32 + cell
                row = (xl ^ int(lat)) * 2 + (c ^ int(core))
                pairs.append((source, row * 32 + (cell + lon) % 32))
    return pairs


def send(x, **way):
    return lax.ppermute(x, AXES, moves(**way))


def vmem(count):
    return [pl.BlockSpec(memory_space=pltpu.VMEM)] * count


SMEM = pl.BlockSpec(memory_space=pltpu.SMEM)


def call(kernel, outs, operands, scratch=(), place=None, flops=0, traffic=0, limit=40):
    shapes = [jax.ShapeDtypeStruct(*o) for o in outs]
    specs = vmem(len(operands))
    args = tuple(operands)
    if place is not None:
        specs = [SMEM] + specs
        args = (place,) + args
    return pl.pallas_call(
        kernel,
        out_shape=shapes,
        in_specs=specs,
        out_specs=vmem(len(outs)),
        scratch_shapes=list(scratch),
        compiler_params=pltpu.CompilerParams(vmem_limit_bytes=limit * 1024 * 1024),
        cost_estimate=pl.CostEstimate(flops=flops, bytes_accessed=traffic, transcendentals=0),
    )(*args)


def edge_kernel(place, fo, fx, co, cx, right, left, rows, corner_r, corner_l):
    xl, core = place[0], place[1]
    for f, (own, other) in enumerate(((fo, fx), (co, cx))):
        for part, ref in enumerate((own, other)):
            span = slice(part * ROWS, (part + 1) * ROWS)
            right[f, span] = ref[:, CELLS - 2 : CELLS, :]
            left[f, span] = ref[:, 0:2, :]
            for side in range(2):
                holder = 1 - side

                @pl.when((xl == side) & (core == (holder if part == 0 else 1 - holder)))
                def _():
                    first = ROWS - 2 if side == 0 else 0
                    rows[f] = ref[first : first + 2]
                    corner_r[f] = ref[first : first + 2, CELLS - 2 : CELLS, :]
                    corner_l[f] = ref[first : first + 2, 0:2, :]


def padded(dst, f, xl, core, own, other, right, left, rows, corner_r, corner_l, lanes):
    width = dst.shape[-1]
    dst[:, CELLS:SLOTS, :] = jnp.zeros((36, SLOTS - CELLS, width), bf16)
    for part, ref in enumerate((own, other)):
        at = pl.ds(2 + ROWS * (core if part == 0 else 1 - core), ROWS)
        span = slice(part * ROWS, (part + 1) * ROWS)
        dst[at, 0:CELLS, :] = ref[:, :, lanes]
        dst[at, CELLS : CELLS + 2, :] = right[f, span, :, lanes]
        dst[at, CELLS + 2 : CELLS + 4, :] = left[f, span, :, lanes]
    edge = pl.ds(34 * (1 - xl), 2)
    dst[edge, 0:CELLS, :] = rows[f, :, :, lanes]
    dst[edge, CELLS : CELLS + 2, :] = corner_r[f, :, :, lanes]
    dst[edge, CELLS + 2 : CELLS + 4, :] = corner_l[f, :, :, lanes]
    dst[pl.ds(34 * xl, 2)] = jnp.zeros((2, SLOTS, width), bf16)


def band_masks(lanes):
    cell = lax.broadcasted_iota(jnp.int32, (CELLS, lanes), 0)
    slot = lax.broadcasted_iota(jnp.int32, (CELLS, lanes), 1) % SLOTS
    place = jnp.where(slot < CELLS + 2, slot, jnp.where(slot < CELLS + 4, slot - 36, 1000))
    return [(place - cell + 2) == s for s in range(BAND)]


def spread(inner, lanes):
    table = np.zeros((inner, BAND, BAND, lanes), np.float32)
    for o in range(inner):
        for s in range(BAND):
            table[o, s, s, o * SLOTS : (o + 1) * SLOTS] = 1.0
    return jnp.asarray(table.reshape(inner * BAND, BAND * lanes), bf16)


def band(block, masks, lanes, row):
    total = jnp.zeros((CELLS, lanes), f32)
    for s in range(BAND):
        line = block[pl.ds(row, 1), s * lanes : (s + 1) * lanes]
        total = jnp.where(masks[s], jnp.broadcast_to(line, (CELLS, lanes)), total)
    return total.astype(bf16)


def forward_band_kernel(taps, table, co, cx, bands, cot_t, lines):
    lines[...] = jnp.dot(taps[...], table[...], preferred_element_type=f32)
    masks = band_masks(CHAN)

    def row(n, carry):
        for k in range(BASIS):
            bands[n, k * CELLS : (k + 1) * CELLS, :] = band(lines, masks, CHAN, n * 16 + k)
        return carry

    lax.fori_loop(0, 2 * ROWS, row, 0)
    cot_t[:, 0:512] = co[...].reshape(512, CHAN).T
    cot_t[:, 512:1024] = cx[...].reshape(512, CHAN).T


def weight_kernel(
    place, fo, fx, right, left, rows, corner_r, corner_l, bands, cot_t, parts, field, basis
):
    xl, core = place[0], place[1]
    lanes = pl.ds(pl.multiple_of(core * HALF, HALF), HALF)
    padded(field, 0, xl, core, fo, fx, right, left, rows, corner_r, corner_l, lanes)

    def row(n, carry):
        first = jnp.where(n < ROWS, core * ROWS + n, (1 - core) * ROWS + n - ROWS)
        window = field[pl.ds(first, BAND)].reshape(BAND * SLOTS, HALF)
        out = jnp.dot(
            bands[n, :, 0 : BAND * SLOTS], window, preferred_element_type=f32
        ).astype(bf16)
        at = pl.ds(pl.multiple_of(n * CELLS, CELLS), CELLS)
        for k in range(BASIS):
            basis[at, k * HALF : (k + 1) * HALF] = out[k * CELLS : (k + 1) * CELLS]
        return carry

    lax.fori_loop(0, 2 * ROWS, row, 0)
    parts[:, 32:KEEP, :] = jnp.zeros((64, 8, HALF), bf16)
    for k in range(BASIS):
        grad = jnp.dot(
            cot_t[...], basis[:, k * HALF : (k + 1) * HALF], preferred_element_type=f32
        ).T
        for side in range(2):
            tiles = grad[:, side * HALF : (side + 1) * HALF].reshape(16, 8, HALF).astype(bf16)
            begin = side * 144 + k * 16
            while_at = 0
            while while_at < 16:
                s, j = divmod(begin + while_at, 64)
                count = min(16 - while_at, 64 - j)
                parts[j : j + count, s * 8 : (s + 1) * 8, :] = tiles[while_at : while_at + count]
                while_at += count


def sum_kernel(scale, parts, out):
    total = jnp.sum(parts[...].astype(f32), axis=0) * scale
    out[...] = jnp.broadcast_to(total.astype(bf16)[None], out.shape)


def place_kernel(place, mine, theirs, out):
    core = place[1]
    for half in range(2):
        for ref, is_mine in ((mine, True), (theirs, False)):

            @pl.when(core == (half if is_mine else 1 - half))
            def _():
                for side in range(2):
                    for k in range(BASIS):
                        begin = side * 144 + k * 16
                        at = 0
                        while at < 16:
                            s, j = divmod(begin + at, 64)
                            count = min(16 - at, 64 - j)
                            tiles = ref[j : j + count, s * 8 : (s + 1) * 8, :].astype(f32)
                            first = half * HALF + at * 8
                            out[
                                k, first : first + count * 8, side * HALF : (side + 1) * HALF
                            ] = tiles.reshape(count * 8, HALF)
                            at += count


def mixed_kernel(
    place, fo, fx, right, left, rows, corner_r, corner_l, bands, weight, out, field, basis
):
    xl, core = place[0], place[1]
    padded(field, 0, xl, core, fo, fx, right, left, rows, corner_r, corner_l, slice(None))

    def row(n, carry):
        window = field[pl.ds(core * ROWS + n, BAND)].reshape(BAND * SLOTS, CHAN)
        part = jnp.dot(
            bands[n, :, 0 : BAND * SLOTS], window, preferred_element_type=f32
        ).astype(bf16)
        at = pl.ds(pl.multiple_of(n * CELLS, CELLS), CELLS)
        for k in range(BASIS):
            basis[at, k * CHAN : (k + 1) * CHAN] = part[k * CELLS : (k + 1) * CELLS]
        return carry

    lax.fori_loop(0, ROWS, row, 0)
    out[...] = (
        jnp.dot(basis[...], weight[...], preferred_element_type=f32)
        .astype(bf16)
        .reshape(ROWS, CELLS, CHAN)
    )


def feature_kernel(
    place,
    co,
    cx,
    right,
    left,
    rows,
    corner_r,
    corner_l,
    taps,
    table,
    weight,
    out,
    field,
    lines,
    grads,
    bands,
    total,
):
    xl, core = place[0], place[1]
    lanes = 512
    near = ROWS + 4
    padded(field, 1, xl, core, co, cx, right, left, rows, corner_r, corner_l, slice(None))
    lines[...] = jnp.dot(taps[...], table[...], preferred_element_type=f32)
    masks = band_masks(lanes)
    for k in range(BASIS):
        for h in range(2):
            upstream = field[pl.ds(core * ROWS + h * 10, 10)].reshape(10 * SLOTS, CHAN)
            back = lax.dot_general(
                upstream,
                weight[k * CHAN : (k + 1) * CHAN, :],
                (((1,), (1,)), ((), ())),
                preferred_element_type=f32,
            )
            grads[h * 10 : (h + 1) * 10, k * SLOTS : (k + 1) * SLOTS, :] = back.astype(
                bf16
            ).reshape(10, SLOTS, CHAN)
    total[...] = jnp.zeros_like(total)

    def row(i, carry):
        for b in range(BAND):
            bands[b * CELLS : (b + 1) * CELLS, :] = band(lines, masks, lanes, i * 8 + b)
        part = jnp.dot(
            bands[:, 0 : BASIS * SLOTS], grads[i], preferred_element_type=f32
        ).reshape(BAND, CELLS, CHAN)
        total[pl.ds(i, BAND)] += part
        return carry

    lax.fori_loop(0, near, row, 0)
    out[...] = total[4 : 4 + ROWS].astype(bf16)


def shards(feature, filters, start, length, weight, cotangent):
    xl, core = lax.axis_index("xl"), lax.axis_index("core")
    place = jnp.stack([xl, core]).astype(jnp.int32)
    lat = xl * 2 + core

    source = (
        lat * ROWS
        + jnp.arange(ROWS, dtype=jnp.int32)[:, None]
        - 2
        + jnp.arange(BAND, dtype=jnp.int32)[None, :]
    )
    inside = (source >= start[:, None]) & (source < (start + length)[:, None])
    masked = filters.reshape(ROWS, BASIS, BAND, BAND) * inside.astype(bf16)[:, None, :, None]

    f_other = send(feature, core=True)
    c_other = send(cotangent, core=True)
    m_other = send(masked, core=True)

    edge = [
        ((2, 32, 2, CHAN), bf16),
        ((2, 32, 2, CHAN), bf16),
        ((2, 2, CELLS, CHAN), bf16),
        ((2, 2, 2, CHAN), bf16),
        ((2, 2, 2, CHAN), bf16),
    ]
    to_right, to_left, rows, corner_r, corner_l = call(
        edge_kernel, edge, (feature, f_other, cotangent, c_other), place=place, traffic=2**20
    )
    left = send(to_right, lon=1)
    right = send(to_left, lon=-1)
    rows = send(rows, lat=True)
    corner_l, corner_r = (
        send(corner_r, lat=True, lon=1),
        send(corner_l, lat=True, lon=-1),
    )
    halo = (right, left, rows, corner_r, corner_l)

    both = jnp.concatenate([masked, m_other], 0)
    flat = jnp.pad(both.reshape(32, BASIS, 25), ((0, 0), (0, 7), (0, 0))).reshape(512, 25)
    bands, cot_t = call(
        forward_band_kernel,
        [((32, BASIS * CELLS, CHAN), bf16), ((CHAN, 1024), bf16)],
        (flat, spread(BAND, CHAN), cotangent, c_other),
        scratch=[pltpu.VMEM((512, BAND * CHAN), f32)],
        flops=2 * 512 * 32 * 1280,
        traffic=6 * 2**20,
    )
    (parts,) = call(
        weight_kernel,
        [((64, KEEP, HALF), bf16)],
        (feature, f_other, *halo, bands, cot_t),
        scratch=[
            pltpu.VMEM((36, SLOTS, HALF), bf16),
            pltpu.VMEM((1024, BASIS * HALF), bf16),
        ],
        place=place,
        flops=2 * 32 * 288 * 256 * 256 + 2 * 1024 * 1152 * 256,
        traffic=7 * 2**20,
    )
    swapped = lax.all_to_all(parts, RING, 0, 0, tiled=True)
    (shared,) = call(
        functools.partial(sum_kernel, 1.0 / math.sqrt(64 * 1024)),
        [((64, KEEP, HALF), bf16)],
        (swapped,),
        traffic=2**20,
    )
    mine = lax.all_to_all(shared, RING, 0, 0, tiled=True)
    theirs = send(mine, core=True)
    (grad_weight,) = call(
        place_kernel, [((BASIS, CHAN, CHAN), f32)], (mine, theirs), place=place, traffic=4 * 2**20
    )

    mixing = weight.reshape(BASIS * CHAN, CHAN)
    (mixed,) = call(
        mixed_kernel,
        [((ROWS, CELLS, CHAN), bf16)],
        (feature, f_other, *halo, bands, mixing),
        scratch=[
            pltpu.VMEM((36, SLOTS, CHAN), bf16),
            pltpu.VMEM((512, BASIS * CHAN), bf16),
        ],
        place=place,
        flops=2 * 16 * 288 * 256 * 256 + 2 * 512 * 2304 * 256,
        traffic=8 * 2**20,
    )

    lowest = jnp.where(core == 0, masked, m_other)
    highest = jnp.where(core == 0, m_other, masked)
    beyond = send(jnp.where(xl == 0, highest[ROWS - 2 :], lowest[:2]), lat=True)
    none = jnp.zeros_like(beyond)
    chip = jnp.concatenate(
        [
            jnp.where(xl == 0, none, beyond),
            lowest,
            highest,
            jnp.where(xl == 0, beyond, none),
        ],
        0,
    )
    near = lax.dynamic_slice_in_dim(chip, core * ROWS, ROWS + 4, 0)[..., ::-1]
    near = jnp.pad(near.transpose(0, 2, 1, 3), ((0, 0), (0, 3), (0, 0), (0, 0)))
    (grad_feature,) = call(
        feature_kernel,
        [((ROWS, CELLS, CHAN), bf16)],
        (
            cotangent,
            c_other,
            *halo,
            near.reshape((ROWS + 4) * 8, BASIS * BAND),
            spread(BASIS, 512),
            mixing,
        ),
        scratch=[
            pltpu.VMEM((36, SLOTS, CHAN), bf16),
            pltpu.VMEM(((ROWS + 4) * 8, BAND * 512), f32),
            pltpu.VMEM((ROWS + 4, BASIS * SLOTS, CHAN), bf16),
            pltpu.VMEM((BAND * CELLS, 512), bf16),
            pltpu.VMEM((ROWS + 8, CELLS, CHAN), f32),
        ],
        place=place,
        flops=2 * 960 * 2304 * 256 + 2 * 20 * 160 * 512 * 256,
        traffic=8 * 2**20,
    )
    return (mixed, grad_feature, grad_weight)


def solution(mesh):
    fine = Mesh(mesh.devices.reshape(SIZES), AXES)
    lat, lon = ("xl", "core"), ("y", "xh", "z")
    return jax.shard_map(
        shards,
        mesh=fine,
        in_specs=(P(lat, lon, None), P(lat, None, None), P(lat), P(lat), P(), P(lat, lon, None)),
        out_specs=(P(lat, lon, None), P(lat, lon, None), P()),
        check_vma=False,
    )
```

```python
import functools
import math

import jax
import jax.numpy as jnp
from jax import lax
from jax.experimental import pallas as pl
from jax.experimental.pallas import tpu as pltpu
from jax.sharding import Mesh, PartitionSpec as P

AXES = ("xl", "core", "y", "xh", "z")
SIZES = (2, 2, 4, 2, 4)
RING = ("xl", "y", "xh", "z")

ROWS = 16
CELLS = 32
SLOTS = 48
BASIS = 9
CHAN = 256
HALF = 128
BAND = 5
KEEP = 40
bf16 = jnp.bfloat16
f32 = jnp.float32


def moves(lat=False, core=False, lon=0):
    pairs = []
    for xl in range(2):
        for c in range(2):
            for cell in range(32):
                source = (xl * 2 + c) * 32 + cell
                row = (xl ^ int(lat)) * 2 + (c ^ int(core))
                pairs.append((source, row * 32 + (cell + lon) % 32))
    return pairs


def send(x, **way):
    return lax.ppermute(x, AXES, moves(**way))


def vmem(count):
    return [pl.BlockSpec(memory_space=pltpu.VMEM)] * count


SMEM = pl.BlockSpec(memory_space=pltpu.SMEM)


def call(kernel, outs, operands, scratch=(), place=None, flops=0, traffic=0, limit=40):
    shapes = [jax.ShapeDtypeStruct(*o) for o in outs]
    specs = vmem(len(operands))
    args = tuple(operands)
    if place is not None:
        specs = [SMEM] + specs
        args = (place,) + args
    return pl.pallas_call(
        kernel,
        out_shape=shapes,
        in_specs=specs,
        out_specs=vmem(len(outs)),
        scratch_shapes=list(scratch),
        compiler_params=pltpu.CompilerParams(vmem_limit_bytes=limit * 1024 * 1024),
        cost_estimate=pl.CostEstimate(flops=flops, bytes_accessed=traffic, transcendentals=0),
    )(*args)


def column_kernel(fo, co, right, left):
    for f, ref in enumerate((fo, co)):
        right[f] = ref[:, CELLS - 2 : CELLS, :]
        left[f] = ref[:, 0:2, :]


def boundary(xl, core):
    return [
        ((xl == side) & (core == (1 - side if part == 0 else side)), part, 14 * (1 - side))
        for side in range(2)
        for part in range(2)
    ]


def row_kernel(place, fo, fx, co, cx, ro, rx, lo, lx, to, tx, rows):
    xl, core = place[0], place[1]
    rows[:, :, 36:SLOTS, :] = jnp.zeros((2, 2, SLOTS - 36, CHAN), bf16)
    for chosen, part, first in boundary(xl, core):

        @pl.when(chosen)
        def _():
            span = slice(first, first + 2)
            for f, pair in enumerate(((fo, fx), (co, cx))):
                rows[f, :, 0:CELLS, :] = pair[part][span]
                rows[f, :, CELLS : CELLS + 2, :] = (ro, rx)[part][f, span]
                rows[f, :, CELLS + 2 : CELLS + 4, :] = (lo, lx)[part][f, span]
            rows[1, 0, SLOTS - 2 : SLOTS, :] = (to, tx)[part][span]


def padded(dst, f, xl, core, own, other, ro, rx, lo, lx, rows, lanes):
    width = dst.shape[-1]
    dst[:, 36:SLOTS, :] = jnp.zeros((36, SLOTS - 36, width), bf16)
    for part, (ref, right, left) in enumerate(((own, ro, lo), (other, rx, lx))):
        at = pl.ds(2 + ROWS * (core if part == 0 else 1 - core), ROWS)
        dst[at, 0:CELLS, :] = ref[:, :, lanes]
        dst[at, CELLS : CELLS + 2, :] = right[f, :, :, lanes]
        dst[at, CELLS + 2 : CELLS + 4, :] = left[f, :, :, lanes]
    if rows is None:
        dst[0:2] = jnp.zeros((2, SLOTS, width), bf16)
        dst[34:36] = jnp.zeros((2, SLOTS, width), bf16)
    else:
        dst[pl.ds(34 * (1 - xl), 2), 0:36, :] = rows[f, :, 0:36, lanes]
        dst[pl.ds(34 * xl, 2)] = jnp.zeros((2, SLOTS, width), bf16)


def over(index, divisor):
    return ((index.astype(f32) + 0.5) * (1.0 / divisor)).astype(jnp.int32)


def split_taps(index):
    k = over(index, 25)
    tap = index - 25 * k
    b = over(tap, 5)
    return k, b, tap - 5 * b


def iota(shape, axis):
    return lax.broadcasted_iota(jnp.int32, shape, axis)


def band_masks(lanes):
    cell = iota((CELLS, lanes), 0)
    lane = iota((CELLS, lanes), 1)
    slot = lane - SLOTS * over(lane, SLOTS)
    place = jnp.where(slot < CELLS + 2, slot, jnp.where(slot < CELLS + 4, slot - 36, 1000))
    return [(place - cell + 2) == s for s in range(BAND)]


def band(block, masks, lanes, row):
    total = jnp.zeros((CELLS, lanes), f32)
    for s in range(BAND):
        line = block[pl.ds(row, 1), s * lanes : (s + 1) * lanes]
        total = jnp.where(masks[s], jnp.broadcast_to(line, (CELLS, lanes)), total)
    return total.astype(bf16)


def one_hot(row, group, offset, count, total):
    column = iota((total, count), 1)
    return (over(row, group) == column + offset).astype(f32).astype(bf16)


def spread(rep, keep, row_key, lanes, inner):
    lane = iota((1, BAND * lanes), 1)
    s = over(lane, lanes)
    o = over(lane - lanes * s, SLOTS)
    lane_key = jnp.where(o < inner, o * BAND + s, -2)
    table = jnp.where(row_key == lane_key, 1.0, 0.0).astype(bf16)
    kept = jnp.where(keep, rep, 0.0).astype(bf16)
    return jnp.dot(kept, table, preferred_element_type=f32)


def forward_band_kernel(to, tx, co, cx, bands, cot_t, lines):
    row = iota((512, 1), 0)
    rep = jnp.dot(one_hot(row, 16, 0, 16, 512), to[...], preferred_element_type=f32)
    rep += jnp.dot(one_hot(row, 16, 16, 16, 512), tx[...], preferred_element_type=f32)
    k, _, _ = split_taps(iota((1, CHAN), 1))
    _, b, s = split_taps(iota((CHAN, 1), 0))
    lines[...] = spread(rep, k == row - 16 * over(row, 16), b * BAND + s, CHAN, BAND)
    masks = band_masks(CHAN)

    def step(n, carry):
        for k in range(BASIS):
            bands[n, k * CELLS : (k + 1) * CELLS, :] = band(lines, masks, CHAN, n * 16 + k)
        return carry

    lax.fori_loop(0, 2 * ROWS, step, 0)
    cot_t[:, 0:512] = co[...].reshape(512, CHAN).T
    cot_t[:, 512:1024] = cx[...].reshape(512, CHAN).T


def weight_kernel(place, fo, fx, ro, rx, lo, lx, bands, cot_t, grad, field, basis):
    xl, core = place[0], place[1]
    lanes = pl.ds(pl.multiple_of(core * HALF, HALF), HALF)
    padded(field, 0, xl, core, fo, fx, ro, rx, lo, lx, None, lanes)

    def step(n, carry):
        first = jnp.where(n < ROWS, core * ROWS + n, (1 - core) * ROWS + n - ROWS)
        window = field[pl.ds(first, BAND)].reshape(BAND * SLOTS, HALF)
        out = jnp.dot(
            bands[n, :, 0 : BAND * SLOTS], window, preferred_element_type=f32
        ).astype(bf16)
        at = pl.ds(pl.multiple_of(n * CELLS, CELLS), CELLS)
        for k in range(BASIS):
            basis[at, k * HALF : (k + 1) * HALF] = out[k * CELLS : (k + 1) * CELLS]
        return carry

    lax.fori_loop(0, 2 * ROWS, step, 0)
    for chosen, part, first in boundary(xl, core):

        @pl.when(chosen)
        def _():
            at = (part * ROWS + first) * CELLS
            basis[at : at + 2 * CELLS, :] = jnp.zeros((2 * CELLS, BASIS * HALF), bf16)

    for k in range(BASIS):
        grad[k] = jnp.dot(
            cot_t[...], basis[:, k * HALF : (k + 1) * HALF], preferred_element_type=f32
        )


def runs(k, side):
    begin, at = side * 144 + k * 16, 0
    while at < 16:
        s, j = divmod(begin + at, 64)
        count = min(16 - at, 64 - j)
        yield at, s * 8, j, count
        at += count


def weight_end_kernel(
    place, fo, fx, co, cx, ro, rx, lo, lx, rows, bands, grad, parts, field, cot, tile
):
    xl, core = place[0], place[1]
    lanes = pl.ds(pl.multiple_of(core * HALF, HALF), HALF)
    field[:, 36:SLOTS, :] = jnp.zeros((6, SLOTS - 36, HALF), bf16)
    field[pl.ds(4 * (1 - xl), 2), 0:36, :] = rows[0, :, 0:36, lanes]
    for chosen, part, first in boundary(xl, core):

        @pl.when(chosen)
        def _():
            ref, right, left = ((fo, ro, lo), (fx, rx, lx))[part]
            at = 2 if first == 0 else 0
            span = slice(0, 4) if first == 0 else slice(12, 16)
            field[at : at + 4, 0:CELLS, :] = ref[span, :, lanes]
            field[at : at + 4, CELLS : CELLS + 2, :] = right[0, span, :, lanes]
            field[at : at + 4, CELLS + 2 : CELLS + 4, :] = left[0, span, :, lanes]
            cot[...] = (co, cx)[part][first : first + 2].reshape(2 * CELLS, CHAN).T
            tile[...] = bands[part * ROWS + first : part * ROWS + first + 2]

    basis = []
    for r in range(2):
        window = field[r : r + BAND].reshape(BAND * SLOTS, HALF)
        basis.append(
            jnp.dot(tile[r, :, 0 : BAND * SLOTS], window, preferred_element_type=f32).astype(bf16)
        )
    parts[:, 32:KEEP, :] = jnp.zeros((64, 8, HALF), bf16)
    for k in range(BASIS):
        cells = jnp.concatenate([x[k * CELLS : (k + 1) * CELLS] for x in basis], 0)
        total = (grad[k] + jnp.dot(cot[...], cells, preferred_element_type=f32)).T
        for side in range(2):
            tiles = total[:, side * HALF : (side + 1) * HALF].reshape(16, 8, HALF).astype(bf16)
            for at, s, j, count in runs(k, side):
                parts[j : j + count, s : s + 8, :] = tiles[at : at + count]


def sum_kernel(scale, parts, out):
    total = jnp.sum(parts[...].astype(f32), axis=0) * scale
    out[...] = jnp.broadcast_to(total.astype(bf16)[None], out.shape)


def place_kernel(place, mine, theirs, out):
    core = place[1]
    for half in range(2):
        for ref, is_mine in ((mine, True), (theirs, False)):

            @pl.when(core == (half if is_mine else 1 - half))
            def _():
                for side in range(2):
                    for k in range(BASIS):
                        for at, s, j, count in runs(k, side):
                            tiles = ref[j : j + count, s : s + 8, :].astype(f32)
                            first = half * HALF + at * 8
                            out[
                                k, first : first + count * 8, side * HALF : (side + 1) * HALF
                            ] = tiles.reshape(count * 8, HALF)


def mixed_kernel(place, fo, fx, ro, rx, lo, lx, rows, bands, weight, out, field, basis):
    xl, core = place[0], place[1]
    padded(field, 0, xl, core, fo, fx, ro, rx, lo, lx, rows, slice(None))

    def step(n, carry):
        window = field[pl.ds(core * ROWS + n, BAND)].reshape(BAND * SLOTS, CHAN)
        part = jnp.dot(
            bands[n, :, 0 : BAND * SLOTS], window, preferred_element_type=f32
        ).astype(bf16)
        at = pl.ds(pl.multiple_of(n * CELLS, CELLS), CELLS)
        for k in range(BASIS):
            basis[at, k * CHAN : (k + 1) * CHAN] = part[k * CELLS : (k + 1) * CELLS]
        return carry

    lax.fori_loop(0, ROWS, step, 0)
    out[...] = (
        jnp.dot(basis[...], weight[...], preferred_element_type=f32)
        .astype(bf16)
        .reshape(ROWS, CELLS, CHAN)
    )


def feature_kernel(
    place, co, cx, ro, rx, lo, lx, rows, to, tx, weight, out, field, lines, grads, bands, total
):
    xl, core = place[0], place[1]
    lanes = 512
    near = ROWS + 4
    padded(field, 1, xl, core, co, cx, ro, rx, lo, lx, rows, slice(None))

    count = near * 8
    row = iota((count, 1), 0)
    beyond = 34 * (1 - xl) - core * ROWS
    other = 2 + (1 - 2 * core) * ROWS
    rep = jnp.dot(one_hot(row, 8, 2, 16, count), to[...], preferred_element_type=f32)
    rep += jnp.dot(one_hot(row, 8, other, 16, count), tx[...], preferred_element_type=f32)
    rep += jnp.dot(
        one_hot(row, 8, beyond, 2, count),
        rows[1, 0, SLOTS - 2 : SLOTS, :],
        preferred_element_type=f32,
    )
    _, b, _ = split_taps(iota((1, CHAN), 1))
    k, _, s = split_taps(iota((CHAN, 1), 0))
    lines[...] = spread(rep, b == row - 8 * over(row, 8), k * BAND + 4 - s, lanes, BASIS)
    masks = band_masks(lanes)
    for k in range(BASIS):
        for h in range(2):
            upstream = field[pl.ds(core * ROWS + h * 10, 10)].reshape(10 * SLOTS, CHAN)
            back = lax.dot_general(
                upstream,
                weight[k * CHAN : (k + 1) * CHAN, :],
                (((1,), (1,)), ((), ())),
                preferred_element_type=f32,
            )
            grads[h * 10 : (h + 1) * 10, k * SLOTS : (k + 1) * SLOTS, :] = back.astype(
                bf16
            ).reshape(10, SLOTS, CHAN)
    total[...] = jnp.zeros_like(total)

    def step(i, carry):
        for b in range(BAND):
            bands[b * CELLS : (b + 1) * CELLS, :] = band(lines, masks, lanes, i * 8 + b)
        part = jnp.dot(
            bands[:, 0 : BASIS * SLOTS], grads[i], preferred_element_type=f32
        ).reshape(BAND, CELLS, CHAN)
        total[pl.ds(i, BAND)] += part
        return carry

    lax.fori_loop(0, near, step, 0)
    out[...] = total[4 : 4 + ROWS].astype(bf16)


def shards(feature, filters, start, length, weight, cotangent):
    xl, core = lax.axis_index("xl"), lax.axis_index("core")
    place = jnp.stack([xl, core]).astype(jnp.int32)
    lat = xl * 2 + core

    column = ((2, ROWS, 2, CHAN), bf16)
    to_right, to_left = call(
        column_kernel, [column, column], (feature, cotangent), traffic=2**19
    )
    lo = send(to_right, lon=1)
    ro = send(to_left, lon=-1)

    band_row = (jnp.arange(225, dtype=jnp.int32) % 25) // 5
    source = lat * ROWS + jnp.arange(ROWS, dtype=jnp.int32)[:, None] - 2 + band_row[None, :]
    inside = (source >= start[:, None]) & (source < (start + length)[:, None])
    masked = jnp.pad(filters.reshape(ROWS, 225) * inside.astype(bf16), ((0, 0), (0, 31)))

    fx = send(feature, core=True)
    cx = send(cotangent, core=True)
    tx = send(masked, core=True)
    bands, cot_t = call(
        forward_band_kernel,
        [((32, BASIS * CELLS, CHAN), bf16), ((CHAN, 1024), bf16)],
        (masked, tx, cotangent, cx),
        scratch=[pltpu.VMEM((512, BAND * CHAN), f32)],
        flops=2 * 512 * 256 * 1280,
        traffic=6 * 2**20,
    )
    lo, ro, bands = lax.optimization_barrier((lo, ro, bands))
    lx = send(lo, core=True)
    rx = send(ro, core=True)
    halo = (ro, rx, lo, lx)

    (rows,) = call(
        row_kernel,
        [((2, 2, SLOTS, CHAN), bf16)],
        (feature, fx, cotangent, cx, *halo, masked, tx),
        place=place,
        traffic=2**20,
    )
    rows = send(rows, lat=True)
    (grad,) = call(
        weight_kernel,
        [((BASIS, CHAN, HALF), f32)],
        (feature, fx, *halo, bands, cot_t),
        scratch=[
            pltpu.VMEM((36, SLOTS, HALF), bf16),
            pltpu.VMEM((1024, BASIS * HALF), bf16),
        ],
        place=place,
        flops=2 * 32 * 288 * 256 * 256 + 2 * 1024 * 1152 * 256,
        traffic=7 * 2**20,
    )
    rows, grad = lax.optimization_barrier((rows, grad))
    (parts,) = call(
        weight_end_kernel,
        [((64, KEEP, HALF), bf16)],
        (feature, fx, cotangent, cx, *halo, rows, bands, grad),
        scratch=[
            pltpu.VMEM((6, SLOTS, HALF), bf16),
            pltpu.VMEM((CHAN, 2 * CELLS), bf16),
            pltpu.VMEM((2, BASIS * CELLS, CHAN), bf16),
        ],
        place=place,
        flops=2 * 64 * 1152 * 256,
        traffic=3 * 2**20,
    )
    mixing = weight.reshape(BASIS * CHAN, CHAN)

    swapped = lax.all_to_all(parts, RING, 0, 0, tiled=True)
    _, mixing_after = lax.optimization_barrier((parts, mixing))
    (mixed,) = call(
        mixed_kernel,
        [((ROWS, CELLS, CHAN), bf16)],
        (feature, fx, *halo, rows, bands, mixing_after),
        scratch=[
            pltpu.VMEM((36, SLOTS, CHAN), bf16),
            pltpu.VMEM((512, BASIS * CHAN), bf16),
        ],
        place=place,
        flops=2 * 16 * 288 * 256 * 256 + 2 * 512 * 2304 * 256,
        traffic=8 * 2**20,
    )
    swapped, mixed = lax.optimization_barrier((swapped, mixed))
    (shared,) = call(
        functools.partial(sum_kernel, 1.0 / math.sqrt(64 * 1024)),
        [((64, KEEP, HALF), bf16)],
        (swapped,),
        traffic=2**20,
    )

    mine = lax.all_to_all(shared, RING, 0, 0, tiled=True)
    _, mixing_later = lax.optimization_barrier((shared, mixing))
    (grad_feature,) = call(
        feature_kernel,
        [((ROWS, CELLS, CHAN), bf16)],
        (cotangent, cx, *halo, rows, masked, tx, mixing_later),
        scratch=[
            pltpu.VMEM((36, SLOTS, CHAN), bf16),
            pltpu.VMEM(((ROWS + 4) * 8, BAND * 512), f32),
            pltpu.VMEM((ROWS + 4, BASIS * SLOTS, CHAN), bf16),
            pltpu.VMEM((BAND * CELLS, 512), bf16),
            pltpu.VMEM((ROWS + 8, CELLS, CHAN), f32),
        ],
        place=place,
        flops=2 * 960 * 2304 * 256 + 2 * 20 * 160 * 512 * 256,
        traffic=8 * 2**20,
    )
    mine, grad_feature = lax.optimization_barrier((mine, grad_feature))
    theirs = send(mine, core=True)
    (grad_weight,) = call(
        place_kernel, [((BASIS, CHAN, CHAN), f32)], (mine, theirs), place=place, traffic=4 * 2**20
    )
    return (mixed, grad_feature, grad_weight)


def solution(mesh):
    fine = Mesh(mesh.devices.reshape(SIZES), AXES)
    lat, lon = ("xl", "core"), ("y", "xh", "z")
    return jax.shard_map(
        shards,
        mesh=fine,
        in_specs=(P(lat, lon, None), P(lat, None, None), P(lat), P(lat), P(), P(lat, lon, None)),
        out_specs=(P(lat, lon, None), P(lat, lon, None), P()),
        check_vma=False,
    )
```

```python
import functools
import math

import jax
import jax.numpy as jnp
from jax import lax
from jax.experimental import pallas as pl
from jax.experimental.pallas import tpu as pltpu
from jax.sharding import Mesh, PartitionSpec as P

AXES = ("xl", "core", "y", "xh", "z")
SIZES = (2, 2, 4, 2, 4)
RING = ("xl", "y", "xh", "z")

ROWS = 16
CELLS = 32
SLOTS = 48
BASIS = 9
CHAN = 256
HALF = 128
BAND = 5
KEEP = 40
bf16 = jnp.bfloat16
f32 = jnp.float32


def moves(lat=False, core=False, lon=(0, 0)):
    pairs = []
    for xl in range(2):
        for c in range(2):
            for cell in range(32):
                source = (xl * 2 + c) * 32 + cell
                row = (xl ^ int(lat)) * 2 + (c ^ int(core))
                pairs.append((source, row * 32 + (cell + lon[c]) % 32))
    return pairs


def send(x, **way):
    return lax.ppermute(x, AXES, moves(**way))


def vmem(count):
    return [pl.BlockSpec(memory_space=pltpu.VMEM)] * count


HBM = pl.BlockSpec(memory_space=pltpu.HBM)


def mark(token):
    token[...] = jnp.zeros(token.shape, f32)


TOKEN = ((8, 128), jnp.float32)


def here():
    return lax.axis_index("xl"), lax.axis_index("core")


def call(kernel, outs, operands, scratch=(), flops=0, traffic=0, limit=24, hbm=(), to=(), alias=None):
    return pl.pallas_call(
        kernel,
        out_shape=[jax.ShapeDtypeStruct(*o) for o in outs],
        in_specs=[HBM if i in hbm else vmem(1)[0] for i in range(len(operands))],
        out_specs=[HBM if i in to else vmem(1)[0] for i in range(len(outs))],
        scratch_shapes=list(scratch),
        input_output_aliases=alias or {},
        compiler_params=pltpu.CompilerParams(vmem_limit_bytes=limit * 1024 * 1024),
        cost_estimate=pl.CostEstimate(flops=flops, bytes_accessed=traffic, transcendentals=0),
    )(*operands)


def column_kernel(f_in, fx, c_in, cx, fo, co, edge):
    _, core = here()
    fo[...] = f_in[...]
    co[...] = c_in[...]
    for side in range(2):

        @pl.when(core == side)
        def _():
            cells = slice(CELLS - 2, CELLS) if side == 0 else slice(0, 2)
            for f, pair in enumerate(((f_in, fx), (c_in, cx))):
                for part, ref in enumerate(pair):
                    edge[f, part * ROWS : (part + 1) * ROWS] = ref[:, cells, :]


def boundary(xl, core):
    return [
        ((xl == side) & (core == (1 - side if part == 0 else side)), part, 14 * (1 - side))
        for side in range(2)
        for part in range(2)
    ]


def rows_of(part, first, count):
    return [slice(p * ROWS + first, p * ROWS + first + count) for p in (part, 1 - part)]


def row_kernel(fo, fx, co, cx, near, far, to, tx, after, rows):
    xl, core = here()
    rows[:, :, 36:SLOTS, :] = jnp.zeros((2, 2, SLOTS - 36, CHAN), bf16)
    for chosen, part, first in boundary(xl, core):

        @pl.when(chosen)
        def _():
            span = slice(first, first + 2)
            side, cross = rows_of(part, first, 2)
            for f, pair in enumerate(((fo, fx), (co, cx))):
                rows[f, :, 0:CELLS, :] = pair[part][span]
                rows[f, :, CELLS : CELLS + 2, :] = near[f, side]
                rows[f, :, CELLS + 2 : CELLS + 4, :] = far[f, cross]
            rows[1, 0, SLOTS - 2 : SLOTS, :] = (to, tx)[part][span]


def padded(dst, f, xl, core, own, other, near, far, rows, lanes):
    width = dst.shape[-1]
    dst[:, 36:SLOTS, :] = jnp.zeros((36, SLOTS - 36, width), bf16)
    for part, ref in enumerate((own, other)):
        at = pl.ds(2 + ROWS * (core if part == 0 else 1 - core), ROWS)
        side, cross = rows_of(part, 0, ROWS)
        dst[at, 0:CELLS, :] = ref[:, :, lanes]
        dst[at, CELLS : CELLS + 2, :] = near[f, side, :, lanes]
        dst[at, CELLS + 2 : CELLS + 4, :] = far[f, cross, :, lanes]
    if rows is None:
        dst[0:2] = jnp.zeros((2, SLOTS, width), bf16)
        dst[34:36] = jnp.zeros((2, SLOTS, width), bf16)
    else:
        dst[pl.ds(34 * (1 - xl), 2), 0:36, :] = rows[f, :, 0:36, lanes]
        dst[pl.ds(34 * xl, 2)] = jnp.zeros((2, SLOTS, width), bf16)


def over(index, divisor):
    return ((index.astype(f32) + 0.5) * (1.0 / divisor)).astype(jnp.int32)


def split_taps(index):
    k = over(index, 25)
    tap = index - 25 * k
    b = over(tap, 5)
    return k, b, tap - 5 * b


def iota(shape, axis):
    return lax.broadcasted_iota(jnp.int32, shape, axis)


def band_masks(lanes):
    _, core = here()
    cell = iota((CELLS, lanes), 0)
    lane = iota((CELLS, lanes), 1)
    slot = lane - SLOTS * over(lane, SLOTS)
    side = jnp.where(slot < CELLS + 2, slot - 34 * (1 - core), slot - 2 - 34 * core)
    place = jnp.where(slot < CELLS, slot, jnp.where(slot < CELLS + 4, side, 1000))
    return [(place - cell + 2) == s for s in range(BAND)]


def band(block, masks, lanes, row):
    total = jnp.zeros((CELLS, lanes), f32)
    for s in range(BAND):
        line = block[pl.ds(row, 1), s * lanes : (s + 1) * lanes]
        total = jnp.where(masks[s], jnp.broadcast_to(line, (CELLS, lanes)), total)
    return total.astype(bf16)


def one_hot(row, group, offset, count, total):
    column = iota((total, count), 1)
    return (over(row, group) == column + offset).astype(f32).astype(bf16)


def spread(rep, keep, row_key, lanes, inner):
    lane = iota((1, BAND * lanes), 1)
    s = over(lane, lanes)
    o = over(lane - lanes * s, SLOTS)
    lane_key = jnp.where(o < inner, o * BAND + s, -2)
    table = jnp.where(row_key == lane_key, 1.0, 0.0).astype(bf16)
    kept = jnp.where(keep, rep, 0.0).astype(bf16)
    return jnp.dot(kept, table, preferred_element_type=f32)


def band_table():
    lane = iota((1, BAND * CHAN), 1)
    s = over(lane, CHAN)
    b = over(lane - CHAN * s, SLOTS)
    key = jnp.where(b < BAND, b * BAND + s, -1)
    return jnp.where(iota((25, 1), 0) == key, 1.0, 0.0).astype(bf16)


def tap_lines(taps, lines):
    lines[...] = jnp.dot(
        taps[...].reshape(BASIS * ROWS, 25), band_table(), preferred_element_type=f32
    )


def all_bands(taps, bands, lines):
    tap_lines(taps, lines)
    masks = band_masks(CHAN)

    def step(n, carry):
        for k in range(BASIS):
            line = band(lines, masks, CHAN, k * ROWS + n)
            bands[n, k * CELLS : (k + 1) * CELLS, :] = line
        return carry

    lax.fori_loop(0, ROWS, step, 0, unroll=4)


def own_kernel(start, length, taps, after, masked, flat, bands, lines):
    xl, core = here()
    square = iota((ROWS, ROWS), 0) == iota((ROWS, ROWS), 1)

    def upright(line):
        spread = jnp.where(square, jnp.broadcast_to(line.astype(f32), (ROWS, ROWS)), 0.0)
        return jnp.sum(spread, axis=1, keepdims=True)

    low = upright(start[...])
    high = low + upright(length[...])
    source = (xl * 2 + core) * ROWS + iota((ROWS, 25), 0) - 2 + over(iota((ROWS, 25), 1), BAND)
    source = source.astype(f32)
    inside = (source >= low) & (source < high)
    total = jnp.zeros((ROWS, CHAN), f32)
    for k in range(BASIS):
        part = jnp.where(inside, taps[k].astype(f32), 0.0).astype(bf16)
        masked[k] = part
        at = iota((25, CHAN), 1) == iota((25, CHAN), 0) + 25 * k
        total += jnp.dot(part, at.astype(f32).astype(bf16), preferred_element_type=f32)
    flat[...] = total.astype(bf16)
    all_bands(masked, bands, lines)


def other_kernel(mx, co, cx, after, bands, cot_t, token, lines):
    mark(token)
    all_bands(mx, bands, lines)
    cot_t[:, 0:512] = co[...].reshape(512, CHAN).T
    cot_t[:, 512:1024] = cx[...].reshape(512, CHAN).T


def weight_kernel(fo, fx, near, far, bo, bx, cot_t, grad, field, basis):
    xl, core = here()
    lanes = pl.ds(pl.multiple_of(core * HALF, HALF), HALF)
    padded(field, 0, xl, core, fo, fx, near, far, None, lanes)

    for part, bands in enumerate((bo, bx)):
        begin = ROWS * (core if part == 0 else 1 - core)

        def step(n, carry):
            window = field[pl.ds(begin + n, BAND)].reshape(BAND * SLOTS, HALF)
            out = jnp.dot(
                bands[n, :, 0 : BAND * SLOTS], window, preferred_element_type=f32
            ).astype(bf16)
            at = pl.ds(pl.multiple_of((part * ROWS + n) * CELLS, CELLS), CELLS)
            for k in range(BASIS):
                basis[at, k * HALF : (k + 1) * HALF] = out[k * CELLS : (k + 1) * CELLS]
            return carry

        lax.fori_loop(0, ROWS, step, 0, unroll=16)
    for chosen, part, first in boundary(xl, core):

        @pl.when(chosen)
        def _():
            at = (part * ROWS + first) * CELLS
            basis[at : at + 2 * CELLS, :] = jnp.zeros((2 * CELLS, BASIS * HALF), bf16)

    total = jnp.dot(cot_t[...], basis[...], preferred_element_type=f32)
    for k in range(BASIS):
        grad[k] = total[:, k * HALF : (k + 1) * HALF]


def runs(k, side):
    begin, at = side * 144 + k * 16, 0
    while at < 16:
        s, j = divmod(begin + at, 64)
        count = min(16 - at, 64 - j)
        yield at, s * 8, j, count
        at += count


def weight_end_kernel(
    fo, fx, co, cx, near, far, rows, bo, bx, grad, parts, token, field, cot, tile
):
    mark(token)
    xl, core = here()
    lanes = pl.ds(pl.multiple_of(core * HALF, HALF), HALF)
    field[:, 36:SLOTS, :] = jnp.zeros((6, SLOTS - 36, HALF), bf16)
    field[pl.ds(4 * (1 - xl), 2), 0:36, :] = rows[0, :, 0:36, lanes]
    for chosen, part, first in boundary(xl, core):

        @pl.when(chosen)
        def _():
            ref = (fo, fx)[part]
            at = 2 if first == 0 else 0
            begin = 0 if first == 0 else 12
            side, cross = rows_of(part, begin, 4)
            field[at : at + 4, 0:CELLS, :] = ref[begin : begin + 4, :, lanes]
            field[at : at + 4, CELLS : CELLS + 2, :] = near[0, side, :, lanes]
            field[at : at + 4, CELLS + 2 : CELLS + 4, :] = far[0, cross, :, lanes]
            cot[...] = (co, cx)[part][first : first + 2].reshape(2 * CELLS, CHAN).T
            tile[...] = (bo, bx)[part][first : first + 2]

    basis = []
    for r in range(2):
        window = field[r : r + BAND].reshape(BAND * SLOTS, HALF)
        basis.append(
            jnp.dot(tile[r, :, 0 : BAND * SLOTS], window, preferred_element_type=f32).astype(bf16)
        )
    parts[:, 32:KEEP, :] = jnp.zeros((64, 8, HALF), bf16)
    for k in range(BASIS):
        cells = jnp.concatenate([x[k * CELLS : (k + 1) * CELLS] for x in basis], 0)
        total = (grad[k] + jnp.dot(cot[...], cells, preferred_element_type=f32)).T
        for side in range(2):
            tiles = total[:, side * HALF : (side + 1) * HALF].reshape(16, 8, HALF).astype(bf16)
            for at, s, j, count in runs(k, side):
                parts[j : j + count, s : s + 8, :] = tiles[at : at + count]


def sum_kernel(scale, parts, after, out, token):
    mark(token)
    total = jnp.sum(parts[...].astype(f32), axis=0) * scale
    out[...] = jnp.broadcast_to(total.astype(bf16)[None], out.shape)


def half_kernel(half_of, tiles_ref, out, stage, sems):
    first = pl.multiple_of(half_of() * HALF, HALF)
    copies = []
    for k in range(BASIS):
        for side in range(2):
            for at, s, j, count in runs(k, side):
                tiles = tiles_ref[j : j + count, s : s + 8, :].astype(f32)
                stage[k, at * 8 : (at + count) * 8, side * HALF : (side + 1) * HALF] = (
                    tiles.reshape(count * 8, HALF)
                )
        copies.append(
            pltpu.make_async_copy(stage.at[k], out.at[k, pl.ds(first, HALF), :], sems.at[k])
        )
        copies[-1].start()
    for copy in copies:
        copy.wait()


def own_half_kernel(mine, out, stage, sems):
    half_kernel(lambda: here()[1], mine, out, stage, sems)


def other_half_kernel(theirs, before, out, stage, sems):
    half_kernel(lambda: 1 - here()[1], theirs, out, stage, sems)


def mixed_kernel(
    fo, fx, near, far, rows, mo, w_hbm, after, out, token, field, basis, weight, bands, lines, sems
):
    mark(token)
    xl, core = here()
    copy = pltpu.make_async_copy(w_hbm, weight, sems)
    copy.start()
    padded(field, 0, xl, core, fo, fx, near, far, rows, slice(None))
    tap_lines(mo, lines)
    masks = band_masks(CHAN)
    for n in range(ROWS):
        for k in range(BASIS):
            line = band(lines, masks, CHAN, k * ROWS + n)
            bands[n, k * CELLS : (k + 1) * CELLS, :] = line
        window = field[pl.ds(core * ROWS + n, BAND)].reshape(BAND * SLOTS, CHAN)
        part = jnp.dot(
            bands[n, :, 0 : BAND * SLOTS], window, preferred_element_type=f32
        ).astype(bf16)
        for k in range(BASIS):
            basis[n * CELLS : (n + 1) * CELLS, k * CHAN : (k + 1) * CHAN] = part[
                k * CELLS : (k + 1) * CELLS
            ]
    copy.wait()
    out[...] = (
        jnp.dot(basis[...], weight[...], preferred_element_type=f32)
        .astype(bf16)
        .reshape(ROWS, CELLS, CHAN)
    )


def feature_kernel(
    co, cx, near, far, rows, to, tx, w_hbm, after, out, token, field, lines, grads, bands, total,
    weight, sems
):
    mark(token)
    copy = pltpu.make_async_copy(w_hbm, weight, sems)
    copy.start()
    xl, core = here()
    lanes = 512
    around = ROWS + 4
    padded(field, 1, xl, core, co, cx, near, far, rows, slice(None))

    count = around * 8
    row = iota((count, 1), 0)
    beyond = 34 * (1 - xl) - core * ROWS
    other = 2 + (1 - 2 * core) * ROWS
    rep = jnp.dot(one_hot(row, 8, 2, 16, count), to[...], preferred_element_type=f32)
    rep += jnp.dot(one_hot(row, 8, other, 16, count), tx[...], preferred_element_type=f32)
    rep += jnp.dot(
        one_hot(row, 8, beyond, 2, count),
        rows[1, 0, SLOTS - 2 : SLOTS, :],
        preferred_element_type=f32,
    )
    _, b, _ = split_taps(iota((1, CHAN), 1))
    k, _, s = split_taps(iota((CHAN, 1), 0))
    lines[...] = spread(rep, b == row - 8 * over(row, 8), k * BAND + 4 - s, lanes, BASIS)
    masks = band_masks(lanes)
    copy.wait()
    for k in range(BASIS):
        for h in range(2):
            upstream = field[pl.ds(core * ROWS + h * 10, 10)].reshape(10 * SLOTS, CHAN)
            back = lax.dot_general(
                upstream,
                weight[k * CHAN : (k + 1) * CHAN, :],
                (((1,), (1,)), ((), ())),
                preferred_element_type=f32,
            )
            grads[h * 10 : (h + 1) * 10, k * SLOTS : (k + 1) * SLOTS, :] = back.astype(
                bf16
            ).reshape(10, SLOTS, CHAN)
    total[...] = jnp.zeros_like(total)

    def step(i, carry):
        for b in range(BAND):
            bands[b * CELLS : (b + 1) * CELLS, :] = band(lines, masks, lanes, i * 8 + b)
        part = jnp.dot(
            bands[:, 0 : BASIS * SLOTS], grads[i], preferred_element_type=f32
        ).reshape(BAND, CELLS, CHAN)
        total[pl.ds(i, BAND)] += part
        return carry

    lax.fori_loop(0, around, step, 0, unroll=4)
    out[...] = total[4 : 4 + ROWS].astype(bf16)


def shards(feature, filters, start, length, weight, cotangent):
    fx = send(feature, core=True)
    cx = send(cotangent, core=True)
    block = ((ROWS, CELLS, CHAN), bf16)
    taps = ((BASIS, ROWS, 25), bf16)
    tiles = ((ROWS, BASIS * CELLS, CHAN), bf16)
    lines = pltpu.VMEM((BASIS * ROWS, BAND * CHAN), f32)
    fo, co, edge = call(
        column_kernel,
        [block, block, ((2, 2 * ROWS, 2, CHAN), bf16)],
        (feature, fx, cotangent, cx),
        traffic=2**20,
        limit=8,
    )
    near = send(edge, lon=(1, -1))

    mo, to, bo = call(
        own_kernel,
        [taps, ((ROWS, CHAN), bf16), tiles],
        (start.reshape(1, ROWS), length.reshape(1, ROWS), filters.transpose(1, 0, 2), edge),
        scratch=[lines],
        flops=2 * 144 * 256 * 1280,
        traffic=4 * 2**20,
        limit=16,
    )
    mx = send(mo, core=True)
    tx = send(to, core=True)
    bx, cot_t, after = call(
        other_kernel,
        [tiles, ((CHAN, 1024), bf16), TOKEN],
        (mx, co, cx, edge),
        scratch=[lines],
        flops=2 * 144 * 256 * 1280,
        traffic=4 * 2**20,
        limit=16,
    )
    near, bx = lax.optimization_barrier((near, bx))
    far = send(near, core=True)
    halo = (near, far)

    (rows,) = call(
        row_kernel,
        [((2, 2, SLOTS, CHAN), bf16)],
        (fo, fx, co, cx, *halo, to, tx, after),
        traffic=2**20,
    )
    rows = send(rows, lat=True)
    (grad,) = call(
        weight_kernel,
        [((BASIS, CHAN, HALF), f32)],
        (fo, fx, *halo, bo, bx, cot_t),
        scratch=[
            pltpu.VMEM((36, SLOTS, HALF), bf16),
            pltpu.VMEM((1024, BASIS * HALF), bf16),
        ],
        flops=2 * 32 * 288 * 256 * 256 + 2 * 1024 * 1152 * 256,
        traffic=7 * 2**20,
    )
    parts, after = call(
        weight_end_kernel,
        [((64, KEEP, HALF), bf16), TOKEN],
        (fo, fx, co, cx, *halo, rows, bo, bx, grad),
        scratch=[
            pltpu.VMEM((6, SLOTS, HALF), bf16),
            pltpu.VMEM((CHAN, 2 * CELLS), bf16),
            pltpu.VMEM((2, BASIS * CELLS, CHAN), bf16),
        ],
        flops=2 * 64 * 1152 * 256,
        traffic=3 * 2**20,
    )
    mixing = weight.reshape(BASIS * CHAN, CHAN)

    swapped = lax.all_to_all(parts, RING, 0, 0, tiled=True)
    mixed, after = call(
        mixed_kernel,
        [block, TOKEN],
        (feature, fx, *halo, rows, mo, mixing, after),
        scratch=[
            pltpu.VMEM((36, SLOTS, CHAN), bf16),
            pltpu.VMEM((512, BASIS * CHAN), bf16),
            pltpu.VMEM((BASIS * CHAN, CHAN), bf16),
            pltpu.VMEM((ROWS, BASIS * CELLS, CHAN), bf16),
            lines,
            pltpu.SemaphoreType.DMA,
        ],
        hbm=(6,),
        flops=2 * 16 * 288 * 256 * 256 + 2 * 512 * 2304 * 256,
        traffic=8 * 2**20,
    )
    shared, after = call(
        functools.partial(sum_kernel, 1.0 / math.sqrt(64 * 1024)),
        [((64, KEEP, HALF), bf16), TOKEN],
        (swapped, after),
        traffic=2**20,
    )

    mine = lax.all_to_all(shared, RING, 0, 0, tiled=True)
    grad_feature, after = call(
        feature_kernel,
        [block, TOKEN],
        (cotangent, cx, *halo, rows, to, tx, mixing, after),
        scratch=[
            pltpu.VMEM((36, SLOTS, CHAN), bf16),
            pltpu.VMEM(((ROWS + 4) * 8, BAND * 512), f32),
            pltpu.VMEM((ROWS + 4, BASIS * SLOTS, CHAN), bf16),
            pltpu.VMEM((BAND * CELLS, 512), bf16),
            pltpu.VMEM((ROWS + 8, CELLS, CHAN), f32),
            pltpu.VMEM((BASIS * CHAN, CHAN), bf16),
            pltpu.SemaphoreType.DMA,
        ],
        hbm=(7,),
        flops=2 * 960 * 2304 * 256 + 2 * 20 * 160 * 512 * 256,
        traffic=8 * 2**20,
    )
    mine, grad_feature = lax.optimization_barrier((mine, grad_feature))
    theirs = send(mine, core=True)
    whole = ((BASIS, CHAN, CHAN), f32)
    stage = [pltpu.VMEM((BASIS, HALF, CHAN), f32), pltpu.SemaphoreType.DMA((BASIS,))]
    (grad_weight,) = call(
        own_half_kernel, [whole], (mine,), scratch=stage, to=(0,), traffic=2 * 2**20, limit=8
    )
    (grad_weight,) = call(
        other_half_kernel,
        [whole],
        (theirs, grad_weight),
        scratch=stage,
        hbm=(1,),
        to=(0,),
        alias={1: 0},
        traffic=2 * 2**20,
        limit=8,
    )
    return (mixed, grad_feature, grad_weight)


def solution(mesh):
    fine = Mesh(mesh.devices.reshape(SIZES), AXES)
    lat, lon = ("xl", "core"), ("y", "xh", "z")
    return jax.shard_map(
        shards,
        mesh=fine,
        in_specs=(P(lat, lon, None), P(lat, None, None), P(lat), P(lat), P(), P(lat, lon, None)),
        out_specs=(P(lat, lon, None), P(lat, lon, None), P()),
        check_vma=False,
    )
```

```python
import functools
import math

import jax
import jax.numpy as jnp
from jax import lax
from jax.experimental import pallas as pl
from jax.experimental.pallas import tpu as pltpu
from jax.sharding import Mesh, PartitionSpec as P

AXES = ("xl", "core", "y", "xh", "z")
SIZES = (2, 2, 4, 2, 4)
RING = ("xl", "y", "xh", "z")

ROWS = 16
CELLS = 32
SLOTS = 48
BASIS = 9
CHAN = 256
HALF = 128
BAND = 5
KEEP = 40
bf16 = jnp.bfloat16
f32 = jnp.float32


def moves(lat=False, core=False, lon=(0, 0)):
    pairs = []
    for xl in range(2):
        for c in range(2):
            for cell in range(32):
                source = (xl * 2 + c) * 32 + cell
                row = (xl ^ int(lat)) * 2 + (c ^ int(core))
                pairs.append((source, row * 32 + (cell + lon[c]) % 32))
    return pairs


def send(x, **way):
    return lax.ppermute(x, AXES, moves(**way))


def vmem(count):
    return [pl.BlockSpec(memory_space=pltpu.VMEM)] * count


HBM = pl.BlockSpec(memory_space=pltpu.HBM)


def mark(token):
    token[...] = jnp.zeros(token.shape, f32)


TOKEN = ((8, 128), jnp.float32)


def here():
    return lax.axis_index("xl"), lax.axis_index("core")


def call(kernel, outs, operands, scratch=(), flops=0, traffic=0, limit=24, hbm=(), to=(), alias=None):
    return pl.pallas_call(
        kernel,
        out_shape=[jax.ShapeDtypeStruct(*o) for o in outs],
        in_specs=[HBM if i in hbm else vmem(1)[0] for i in range(len(operands))],
        out_specs=[HBM if i in to else vmem(1)[0] for i in range(len(outs))],
        scratch_shapes=list(scratch),
        input_output_aliases=alias or {},
        compiler_params=pltpu.CompilerParams(vmem_limit_bytes=limit * 1024 * 1024),
        cost_estimate=pl.CostEstimate(flops=flops, bytes_accessed=traffic, transcendentals=0),
    )(*operands)


def column_kernel(own, fx, cx, edge):
    _, core = here()
    for side in range(2):

        @pl.when(core == side)
        def _():
            cells = slice(CELLS - 2, CELLS) if side == 0 else slice(0, 2)
            for f, other in enumerate((fx, cx)):
                edge[f, 0:ROWS] = own[f, :, cells, :]
                edge[f, ROWS : 2 * ROWS] = other[:, cells, :]


def boundary(xl, core):
    return [
        ((xl == side) & (core == (1 - side if part == 0 else side)), part, 14 * (1 - side))
        for side in range(2)
        for part in range(2)
    ]


def rows_of(part, first, count):
    return [slice(p * ROWS + first, p * ROWS + first + count) for p in (part, 1 - part)]


def row_kernel(own, fx, cx, near, far, to, tx, rows):
    xl, core = here()
    rows[:, :, 36:40, :] = jnp.zeros((2, 2, 4, CHAN), bf16)
    for chosen, part, first in boundary(xl, core):

        @pl.when(chosen)
        def _():
            span = slice(first, first + 2)
            side, cross = rows_of(part, first, 2)
            for f, pair in enumerate(((own.at[0], fx), (own.at[1], cx))):
                rows[f, :, 0:CELLS, :] = pair[part][span]
                rows[f, :, CELLS : CELLS + 2, :] = near[f, side]
                rows[f, :, CELLS + 2 : CELLS + 4, :] = far[f, cross]
            rows[1, 0, 38:40, :] = (to, tx)[part][span]


def padded(dst, f, xl, core, own, other, near, far, rows, lanes):
    width = dst.shape[-1]
    dst[:, 36:SLOTS, :] = jnp.zeros((36, SLOTS - 36, width), bf16)
    for part, ref in enumerate((own, other)):
        at = pl.ds(2 + ROWS * (core if part == 0 else 1 - core), ROWS)
        side, cross = rows_of(part, 0, ROWS)
        dst[at, 0:CELLS, :] = ref[:, :, lanes]
        dst[at, CELLS : CELLS + 2, :] = near[f, side, :, lanes]
        dst[at, CELLS + 2 : CELLS + 4, :] = far[f, cross, :, lanes]
    if rows is None:
        dst[0:2] = jnp.zeros((2, SLOTS, width), bf16)
        dst[34:36] = jnp.zeros((2, SLOTS, width), bf16)
    else:
        dst[pl.ds(34 * (1 - xl), 2), 0:36, :] = rows[f, :, 0:36, lanes]
        dst[pl.ds(34 * xl, 2)] = jnp.zeros((2, SLOTS, width), bf16)


def over(index, divisor):
    return ((index.astype(f32) + 0.5) * (1.0 / divisor)).astype(jnp.int32)


def split_taps(index):
    k = over(index, 25)
    tap = index - 25 * k
    b = over(tap, 5)
    return k, b, tap - 5 * b


def iota(shape, axis):
    return lax.broadcasted_iota(jnp.int32, shape, axis)


def band_masks(lanes):
    _, core = here()
    cell = iota((CELLS, lanes), 0)
    lane = iota((CELLS, lanes), 1)
    slot = lane - SLOTS * over(lane, SLOTS)
    side = jnp.where(slot < CELLS + 2, slot - 34 * (1 - core), slot - 2 - 34 * core)
    place = jnp.where(slot < CELLS, slot, jnp.where(slot < CELLS + 4, side, 1000))
    return [(place - cell + 2) == s for s in range(BAND)]


def band(block, masks, lanes, row):
    total = jnp.zeros((CELLS, lanes), f32)
    for s in range(BAND):
        line = block[pl.ds(row, 1), s * lanes : (s + 1) * lanes]
        total = jnp.where(masks[s], jnp.broadcast_to(line, (CELLS, lanes)), total)
    return total.astype(bf16)


def one_hot(row, group, offset, count, total):
    column = iota((total, count), 1)
    return (over(row, group) == column + offset).astype(f32).astype(bf16)


def spread(rep, keep, row_key, lanes, inner):
    lane = iota((1, BAND * lanes), 1)
    s = over(lane, lanes)
    o = over(lane - lanes * s, SLOTS)
    lane_key = jnp.where(o < inner, o * BAND + s, -2)
    table = jnp.where(row_key == lane_key, 1.0, 0.0).astype(bf16)
    kept = jnp.where(keep, rep, 0.0).astype(bf16)
    return jnp.dot(kept, table, preferred_element_type=f32)


def band_table():
    lane = iota((1, BAND * CHAN), 1)
    s = over(lane, CHAN)
    b = over(lane - CHAN * s, SLOTS)
    key = jnp.where(b < BAND, b * BAND + s, -1)
    return jnp.where(iota((25, 1), 0) == key, 1.0, 0.0).astype(bf16)


def tap_lines(taps, lines):
    lines[...] = jnp.dot(
        taps[...].reshape(BASIS * ROWS, 25), band_table(), preferred_element_type=f32
    )


def all_bands(taps, bands, lines):
    tap_lines(taps, lines)
    masks = band_masks(CHAN)

    def step(n, carry):
        for k in range(BASIS):
            line = band(lines, masks, CHAN, k * ROWS + n)
            bands[n, k * CELLS : (k + 1) * CELLS, :] = line
        return carry

    lax.fori_loop(0, ROWS, step, 0, unroll=4)


def band_kernel(mo, mx, own, cx, after, bo, bx, cot_t, to, tx, lines):
    to[...] = flat_taps(mo)
    tx[...] = flat_taps(mx)
    all_bands(mo, bo, lines)
    all_bands(mx, bx, lines)
    cot_t[:, 0:512] = own[1].reshape(512, CHAN).T
    cot_t[:, 512:1024] = cx[...].reshape(512, CHAN).T


def flat_taps(taps):
    total = jnp.zeros((ROWS, CHAN), f32)
    for k in range(BASIS):
        at = iota((25, CHAN), 1) == iota((25, CHAN), 0) + 25 * k
        total += jnp.dot(taps[k], at.astype(f32).astype(bf16), preferred_element_type=f32)
    return total.astype(bf16)


def weight_kernel(own, fx, near, far, bo, bx, cot_t, grad, field, basis):
    xl, core = here()
    lanes = pl.ds(pl.multiple_of(core * HALF, HALF), HALF)
    padded(field, 0, xl, core, own.at[0], fx, near, far, None, lanes)

    for part, bands in enumerate((bo, bx)):
        begin = ROWS * (core if part == 0 else 1 - core)

        def step(n, carry):
            window = field[pl.ds(begin + n, BAND)].reshape(BAND * SLOTS, HALF)
            out = jnp.dot(
                bands[n, :, 0 : BAND * SLOTS], window, preferred_element_type=f32
            ).astype(bf16)
            at = pl.ds(pl.multiple_of((part * ROWS + n) * CELLS, CELLS), CELLS)
            for k in range(BASIS):
                basis[at, k * HALF : (k + 1) * HALF] = out[k * CELLS : (k + 1) * CELLS]
            return carry

        lax.fori_loop(0, ROWS, step, 0, unroll=16)
    for chosen, part, first in boundary(xl, core):

        @pl.when(chosen)
        def _():
            at = (part * ROWS + first) * CELLS
            basis[at : at + 2 * CELLS, :] = jnp.zeros((2 * CELLS, BASIS * HALF), bf16)

    total = jnp.dot(cot_t[...], basis[...], preferred_element_type=f32)
    for k in range(BASIS):
        grad[k] = total[:, k * HALF : (k + 1) * HALF]


def runs(k, side):
    begin, at = side * 144 + k * 16, 0
    while at < 16:
        s, j = divmod(begin + at, 64)
        count = min(16 - at, 64 - j)
        yield at, s * 8, j, count
        at += count


def weight_end_kernel(
    own, fx, cx, near, far, rows, bo, bx, grad, parts, token, field, cot, tile
):
    mark(token)
    xl, core = here()
    lanes = pl.ds(pl.multiple_of(core * HALF, HALF), HALF)
    field[:, 36:SLOTS, :] = jnp.zeros((6, SLOTS - 36, HALF), bf16)
    field[pl.ds(4 * (1 - xl), 2), 0:36, :] = rows[0, :, 0:36, lanes]
    for chosen, part, first in boundary(xl, core):

        @pl.when(chosen)
        def _():
            ref = (own.at[0], fx)[part]
            at = 2 if first == 0 else 0
            begin = 0 if first == 0 else 12
            side, cross = rows_of(part, begin, 4)
            field[at : at + 4, 0:CELLS, :] = ref[begin : begin + 4, :, lanes]
            field[at : at + 4, CELLS : CELLS + 2, :] = near[0, side, :, lanes]
            field[at : at + 4, CELLS + 2 : CELLS + 4, :] = far[0, cross, :, lanes]
            cot[...] = (own.at[1], cx)[part][first : first + 2].reshape(2 * CELLS, CHAN).T
            tile[...] = (bo, bx)[part][first : first + 2]

    basis = []
    for r in range(2):
        window = field[r : r + BAND].reshape(BAND * SLOTS, HALF)
        basis.append(
            jnp.dot(tile[r, :, 0 : BAND * SLOTS], window, preferred_element_type=f32).astype(bf16)
        )
    parts[:, 32:KEEP, :] = jnp.zeros((64, 8, HALF), bf16)
    for k in range(BASIS):
        cells = jnp.concatenate([x[k * CELLS : (k + 1) * CELLS] for x in basis], 0)
        total = (grad[k] + jnp.dot(cot[...], cells, preferred_element_type=f32)).T
        for side in range(2):
            tiles = total[:, side * HALF : (side + 1) * HALF].reshape(16, 8, HALF).astype(bf16)
            for at, s, j, count in runs(k, side):
                parts[j : j + count, s : s + 8, :] = tiles[at : at + count]


def sum_kernel(scale, parts, after, out, token):
    mark(token)
    total = jnp.sum(parts[...].astype(f32), axis=0) * scale
    out[...] = jnp.broadcast_to(total.astype(bf16)[None], out.shape)


def half_kernel(half_of, tiles_ref, out, stage, sems):
    first = pl.multiple_of(half_of() * HALF, HALF)
    copies = []
    for k in range(BASIS):
        for side in range(2):
            for at, s, j, count in runs(k, side):
                tiles = tiles_ref[j : j + count, s : s + 8, :].astype(f32)
                stage[k, at * 8 : (at + count) * 8, side * HALF : (side + 1) * HALF] = (
                    tiles.reshape(count * 8, HALF)
                )
        copies.append(
            pltpu.make_async_copy(stage.at[k], out.at[k, pl.ds(first, HALF), :], sems.at[k])
        )
        copies[-1].start()
    for copy in copies:
        copy.wait()


def own_half_kernel(mine, out, stage, sems):
    half_kernel(lambda: here()[1], mine, out, stage, sems)


def other_half_kernel(theirs, before, out, stage, sems):
    half_kernel(lambda: 1 - here()[1], theirs, out, stage, sems)


def mixed_kernel(
    fo, fx, near, far, rows, mo, w_hbm, after, out, token,
    field, basis, weight, bands, lines, sems
):
    mark(token)
    xl, core = here()
    copy = pltpu.make_async_copy(w_hbm, weight, sems)
    copy.start()
    padded(field, 0, xl, core, fo, fx, near, far, rows, slice(None))
    tap_lines(mo, lines)
    masks = band_masks(CHAN)
    for n in range(ROWS):
        for k in range(BASIS):
            line = band(lines, masks, CHAN, k * ROWS + n)
            bands[n, k * CELLS : (k + 1) * CELLS, :] = line
        window = field[pl.ds(core * ROWS + n, BAND)].reshape(BAND * SLOTS, CHAN)
        part = jnp.dot(
            bands[n, :, 0 : BAND * SLOTS], window, preferred_element_type=f32
        ).astype(bf16)
        for k in range(BASIS):
            basis[n * CELLS : (n + 1) * CELLS, k * CHAN : (k + 1) * CHAN] = part[
                k * CELLS : (k + 1) * CELLS
            ]
    copy.wait()
    out[...] = (
        jnp.dot(basis[...], weight[...], preferred_element_type=f32)
        .astype(bf16)
        .reshape(ROWS, CELLS, CHAN)
    )


def feature_kernel(
    co, cx, near, far, rows, to, tx, w_hbm, after, out, token, field, lines, grads, bands, total,
    weight, sems
):
    mark(token)
    copy = pltpu.make_async_copy(w_hbm, weight, sems)
    copy.start()
    xl, core = here()
    lanes = 512
    around = ROWS + 4
    padded(field, 1, xl, core, co, cx, near, far, rows, slice(None))

    count = around * 8
    row = iota((count, 1), 0)
    beyond = 34 * (1 - xl) - core * ROWS
    other = 2 + (1 - 2 * core) * ROWS
    rep = jnp.dot(one_hot(row, 8, 2, 16, count), to[...], preferred_element_type=f32)
    rep += jnp.dot(one_hot(row, 8, other, 16, count), tx[...], preferred_element_type=f32)
    rep += jnp.dot(
        one_hot(row, 8, beyond, 2, count), rows[1, 0, 38:40, :], preferred_element_type=f32
    )
    _, b, _ = split_taps(iota((1, CHAN), 1))
    k, _, s = split_taps(iota((CHAN, 1), 0))
    lines[...] = spread(rep, b == row - 8 * over(row, 8), k * BAND + 4 - s, lanes, BASIS)
    masks = band_masks(lanes)
    copy.wait()
    for k in range(BASIS):
        for h in range(2):
            upstream = field[pl.ds(core * ROWS + h * 10, 10)].reshape(10 * SLOTS, CHAN)
            back = lax.dot_general(
                upstream,
                weight[k * CHAN : (k + 1) * CHAN, :],
                (((1,), (1,)), ((), ())),
                preferred_element_type=f32,
            )
            grads[h * 10 : (h + 1) * 10, k * SLOTS : (k + 1) * SLOTS, :] = back.astype(
                bf16
            ).reshape(10, SLOTS, CHAN)
    total[...] = jnp.zeros_like(total)

    def step(i, carry):
        for b in range(BAND):
            bands[b * CELLS : (b + 1) * CELLS, :] = band(lines, masks, lanes, i * 8 + b)
        part = jnp.dot(
            bands[:, 0 : BASIS * SLOTS], grads[i], preferred_element_type=f32
        ).reshape(BAND, CELLS, CHAN)
        total[pl.ds(i, BAND)] += part
        return carry

    lax.fori_loop(0, around, step, 0, unroll=4)
    out[...] = total[4 : 4 + ROWS].astype(bf16)


def shards(feature, filters, start, length, weight, cotangent):
    fx = send(feature, core=True)
    cx = send(cotangent, core=True)
    lat = lax.axis_index("xl") * 2 + lax.axis_index("core")
    source = lat * ROWS + jnp.arange(ROWS, dtype=jnp.int32)[:, None] - 2
    source = source + jnp.arange(25, dtype=jnp.int32)[None, :] // BAND - start[:, None]
    inside = (source >= 0) & (source < length[:, None])
    mo = jnp.where(inside[None], filters.transpose(1, 0, 2), jnp.zeros((), bf16))
    mx = send(mo, core=True)
    own = jnp.stack([feature, cotangent])

    block = ((ROWS, CELLS, CHAN), bf16)
    tiles = ((ROWS, BASIS * CELLS, CHAN), bf16)
    flat = ((ROWS, CHAN), bf16)
    lines = pltpu.VMEM((BASIS * ROWS, BAND * CHAN), f32)
    (edge,) = call(
        column_kernel,
        [((2, 2 * ROWS, 2, CHAN), bf16)],
        (own, fx, cx),
        traffic=2**20,
        limit=8,
    )
    near = send(edge, lon=(1, -1))

    bo, bx, cot_t, to, tx = call(
        band_kernel,
        [tiles, tiles, ((CHAN, 1024), bf16), flat, flat],
        (mo, mx, own, cx, edge),
        scratch=[lines],
        flops=4 * 144 * 256 * 1280,
        traffic=8 * 2**20,
        limit=16,
    )
    near, bx = lax.optimization_barrier((near, bx))
    far = send(near, core=True)
    halo = (near, far)

    (rows,) = call(
        row_kernel,
        [((2, 2, 40, CHAN), bf16)],
        (own, fx, cx, *halo, to, tx),
        traffic=2**20,
    )
    rows = send(rows, lat=True)
    (grad,) = call(
        weight_kernel,
        [((BASIS, CHAN, HALF), f32)],
        (own, fx, *halo, bo, bx, cot_t),
        scratch=[
            pltpu.VMEM((36, SLOTS, HALF), bf16),
            pltpu.VMEM((1024, BASIS * HALF), bf16),
        ],
        flops=2 * 32 * 288 * 256 * 256 + 2 * 1024 * 1152 * 256,
        traffic=7 * 2**20,
    )
    parts, after = call(
        weight_end_kernel,
        [((64, KEEP, HALF), bf16), TOKEN],
        (own, fx, cx, *halo, rows, bo, bx, grad),
        scratch=[
            pltpu.VMEM((6, SLOTS, HALF), bf16),
            pltpu.VMEM((CHAN, 2 * CELLS), bf16),
            pltpu.VMEM((2, BASIS * CELLS, CHAN), bf16),
        ],
        flops=2 * 64 * 1152 * 256,
        traffic=3 * 2**20,
    )
    mixing = weight.reshape(BASIS * CHAN, CHAN)

    swapped = lax.all_to_all(parts, RING, 0, 0, tiled=True)
    mixed, after = call(
        mixed_kernel,
        [block, TOKEN],
        (feature, fx, *halo, rows, mo, mixing, after),
        scratch=[
            pltpu.VMEM((36, SLOTS, CHAN), bf16),
            pltpu.VMEM((512, BASIS * CHAN), bf16),
            pltpu.VMEM((BASIS * CHAN, CHAN), bf16),
            pltpu.VMEM((ROWS, BASIS * CELLS, CHAN), bf16),
            lines,
            pltpu.SemaphoreType.DMA,
        ],
        hbm=(6,),
        flops=2 * 16 * 288 * 256 * 256 + 2 * 512 * 2304 * 256,
        traffic=8 * 2**20,
    )
    shared, after = call(
        functools.partial(sum_kernel, 1.0 / math.sqrt(64 * 1024)),
        [((64, KEEP, HALF), bf16), TOKEN],
        (swapped, after),
        traffic=2**20,
    )

    mine = lax.all_to_all(shared, RING, 0, 0, tiled=True)
    grad_feature, after = call(
        feature_kernel,
        [block, TOKEN],
        (cotangent, cx, *halo, rows, to, tx, mixing, after),
        scratch=[
            pltpu.VMEM((36, SLOTS, CHAN), bf16),
            pltpu.VMEM(((ROWS + 4) * 8, BAND * 512), f32),
            pltpu.VMEM((ROWS + 4, BASIS * SLOTS, CHAN), bf16),
            pltpu.VMEM((BAND * CELLS, 512), bf16),
            pltpu.VMEM((ROWS + 8, CELLS, CHAN), f32),
            pltpu.VMEM((BASIS * CHAN, CHAN), bf16),
            pltpu.SemaphoreType.DMA,
        ],
        hbm=(7,),
        flops=2 * 960 * 2304 * 256 + 2 * 20 * 160 * 512 * 256,
        traffic=8 * 2**20,
    )
    mine, grad_feature = lax.optimization_barrier((mine, grad_feature))
    theirs = send(mine, core=True)
    whole = ((BASIS, CHAN, CHAN), f32)
    stage = [pltpu.VMEM((BASIS, HALF, CHAN), f32), pltpu.SemaphoreType.DMA((BASIS,))]
    (grad_weight,) = call(
        own_half_kernel, [whole], (mine,), scratch=stage, to=(0,), traffic=2 * 2**20, limit=8
    )
    (grad_weight,) = call(
        other_half_kernel,
        [whole],
        (theirs, grad_weight),
        scratch=stage,
        hbm=(1,),
        to=(0,),
        alias={1: 0},
        traffic=2 * 2**20,
        limit=8,
    )
    return (mixed, grad_feature, grad_weight)


def solution(mesh):
    fine = Mesh(mesh.devices.reshape(SIZES), AXES)
    lat, lon = ("xl", "core"), ("y", "xh", "z")
    return jax.shard_map(
        shards,
        mesh=fine,
        in_specs=(P(lat, lon, None), P(lat, None, None), P(lat), P(lat), P(), P(lat, lon, None)),
        out_specs=(P(lat, lon, None), P(lat, lon, None), P()),
        check_vma=False,
    )
```

```python
import functools
import math

import jax
import jax.numpy as jnp
from jax import lax
from jax.experimental import pallas as pl
from jax.experimental.pallas import tpu as pltpu
from jax.sharding import Mesh, PartitionSpec as P

AXES = ("xl", "core", "y", "xh", "z")
SIZES = (2, 2, 4, 2, 4)
RING = ("xl", "y", "xh", "z")

ROWS = 16
CELLS = 32
SLOTS = 48
BASIS = 9
CHAN = 256
HALF = 128
BAND = 5
CHUNK = (9, 4, 128)
bf16 = jnp.bfloat16
f32 = jnp.float32


def moves(lat=False, core=False, lon=(0, 0)):
    pairs = []
    for xl in range(2):
        for c in range(2):
            for cell in range(32):
                source = (xl * 2 + c) * 32 + cell
                row = (xl ^ int(lat)) * 2 + (c ^ int(core))
                pairs.append((source, row * 32 + (cell + lon[c]) % 32))
    return pairs


def send(x, **way):
    return lax.ppermute(x, AXES, moves(**way))


def vmem(count):
    return [pl.BlockSpec(memory_space=pltpu.VMEM)] * count


HBM = pl.BlockSpec(memory_space=pltpu.HBM)


def mark(token):
    token[...] = jnp.zeros(token.shape, f32)


TOKEN = ((8, 128), jnp.float32)


def here():
    return lax.axis_index("xl"), lax.axis_index("core")


def call(kernel, outs, operands, scratch=(), flops=0, traffic=0, limit=24, hbm=(), to=(), alias=None):
    return pl.pallas_call(
        kernel,
        out_shape=[jax.ShapeDtypeStruct(*o) for o in outs],
        in_specs=[HBM if i in hbm else vmem(1)[0] for i in range(len(operands))],
        out_specs=[HBM if i in to else vmem(1)[0] for i in range(len(outs))],
        scratch_shapes=list(scratch),
        input_output_aliases=alias or {},
        compiler_params=pltpu.CompilerParams(vmem_limit_bytes=limit * 1024 * 1024),
        cost_estimate=pl.CostEstimate(flops=flops, bytes_accessed=traffic, transcendentals=0),
    )(*operands)


def column_kernel(own, fx, cx, edge):
    _, core = here()
    for side in range(2):

        @pl.when(core == side)
        def _():
            cells = slice(CELLS - 2, CELLS) if side == 0 else slice(0, 2)
            for f, other in enumerate((fx, cx)):
                edge[f, 0:ROWS] = own[f, :, cells, :]
                edge[f, ROWS : 2 * ROWS] = other[:, cells, :]


def boundary(xl, core):
    return [
        ((xl == side) & (core == (1 - side if part == 0 else side)), part, 14 * (1 - side))
        for side in range(2)
        for part in range(2)
    ]


def rows_of(part, first, count):
    return [slice(p * ROWS + first, p * ROWS + first + count) for p in (part, 1 - part)]


def row_kernel(own, fx, cx, near, far, to, tx, rows):
    xl, core = here()
    rows[:, :, 36:40, :] = jnp.zeros((2, 2, 4, CHAN), bf16)
    for chosen, part, first in boundary(xl, core):

        @pl.when(chosen)
        def _():
            span = slice(first, first + 2)
            side, cross = rows_of(part, first, 2)
            for f, pair in enumerate(((own.at[0], fx), (own.at[1], cx))):
                rows[f, :, 0:CELLS, :] = pair[part][span]
                rows[f, :, CELLS : CELLS + 2, :] = near[f, side]
                rows[f, :, CELLS + 2 : CELLS + 4, :] = far[f, cross]
            rows[1, 0, 38:40, :] = (to, tx)[part][span]


def padded(dst, f, xl, core, own, other, near, far, rows, lanes):
    width = dst.shape[-1]
    dst[:, 36:SLOTS, :] = jnp.zeros((36, SLOTS - 36, width), bf16)
    for part, ref in enumerate((own, other)):
        at = pl.ds(2 + ROWS * (core if part == 0 else 1 - core), ROWS)
        side, cross = rows_of(part, 0, ROWS)
        dst[at, 0:CELLS, :] = ref[:, :, lanes]
        dst[at, CELLS : CELLS + 2, :] = near[f, side, :, lanes]
        dst[at, CELLS + 2 : CELLS + 4, :] = far[f, cross, :, lanes]
    if rows is None:
        dst[0:2] = jnp.zeros((2, SLOTS, width), bf16)
        dst[34:36] = jnp.zeros((2, SLOTS, width), bf16)
    else:
        dst[pl.ds(34 * (1 - xl), 2), 0:36, :] = rows[f, :, 0:36, lanes]
        dst[pl.ds(34 * xl, 2)] = jnp.zeros((2, SLOTS, width), bf16)


def over(index, divisor):
    return ((index.astype(f32) + 0.5) * (1.0 / divisor)).astype(jnp.int32)


def split_taps(index):
    k = over(index, 25)
    tap = index - 25 * k
    b = over(tap, 5)
    return k, b, tap - 5 * b


def iota(shape, axis):
    return lax.broadcasted_iota(jnp.int32, shape, axis)


def band_masks(lanes):
    _, core = here()
    cell = iota((CELLS, lanes), 0)
    lane = iota((CELLS, lanes), 1)
    slot = lane - SLOTS * over(lane, SLOTS)
    side = jnp.where(slot < CELLS + 2, slot - 34 * (1 - core), slot - 2 - 34 * core)
    place = jnp.where(slot < CELLS, slot, jnp.where(slot < CELLS + 4, side, 1000))
    return [(place - cell + 2) == s for s in range(BAND)]


def band(block, masks, lanes, row):
    total = jnp.zeros((CELLS, lanes), f32)
    for s in range(BAND):
        line = block[pl.ds(row, 1), s * lanes : (s + 1) * lanes]
        total = jnp.where(masks[s], jnp.broadcast_to(line, (CELLS, lanes)), total)
    return total.astype(bf16)


def one_hot(row, group, offset, count, total):
    column = iota((total, count), 1)
    return (over(row, group) == column + offset).astype(f32).astype(bf16)


def spread(rep, keep, row_key, lanes, inner):
    lane = iota((1, BAND * lanes), 1)
    s = over(lane, lanes)
    o = over(lane - lanes * s, SLOTS)
    lane_key = jnp.where(o < inner, o * BAND + s, -2)
    table = jnp.where(row_key == lane_key, 1.0, 0.0).astype(bf16)
    kept = jnp.where(keep, rep, 0.0).astype(bf16)
    return jnp.dot(kept, table, preferred_element_type=f32)


def band_table():
    lane = iota((1, BAND * CHAN), 1)
    s = over(lane, CHAN)
    b = over(lane - CHAN * s, SLOTS)
    key = jnp.where(b < BAND, b * BAND + s, -1)
    return jnp.where(iota((25, 1), 0) == key, 1.0, 0.0).astype(bf16)


def tap_lines(taps, lines):
    lines[...] = jnp.dot(
        taps[...].reshape(BASIS * ROWS, 25), band_table(), preferred_element_type=f32
    )


def all_bands(taps, bands, lines):
    tap_lines(taps, lines)
    masks = band_masks(CHAN)

    def step(n, carry):
        for k in range(BASIS):
            line = band(lines, masks, CHAN, k * ROWS + n)
            bands[n, k * CELLS : (k + 1) * CELLS, :] = line
        return carry

    lax.fori_loop(0, ROWS, step, 0, unroll=4)


def own_band_kernel(mo, own, after, bo, cot_t, to, lines):
    to[...] = flat_taps(mo)
    all_bands(mo, bo, lines)
    cot_t[...] = own[1].reshape(512, CHAN).T


def other_band_kernel(mx, cx, after, bx, cot_t, tx, lines):
    tx[...] = flat_taps(mx)
    all_bands(mx, bx, lines)
    cot_t[...] = cx[...].reshape(512, CHAN).T


def flat_taps(taps):
    total = jnp.zeros((ROWS, CHAN), f32)
    for k in range(BASIS):
        at = iota((25, CHAN), 1) == iota((25, CHAN), 0) + 25 * k
        total += jnp.dot(taps[k], at.astype(f32).astype(bf16), preferred_element_type=f32)
    return total.astype(bf16)


def weight_kernel(own, fx, near, far, bo, bx, ct_o, ct_x, grad, field, basis):
    xl, core = here()
    lanes = pl.ds(pl.multiple_of(core * HALF, HALF), HALF)
    padded(field, 0, xl, core, own.at[0], fx, near, far, None, lanes)

    for part, bands in enumerate((bo, bx)):
        begin = ROWS * (core if part == 0 else 1 - core)

        def step(n, carry):
            window = field[pl.ds(begin + n, BAND)].reshape(BAND * SLOTS, HALF)
            out = jnp.dot(
                bands[n, :, 0 : BAND * SLOTS], window, preferred_element_type=f32
            ).astype(bf16)
            at = pl.ds(pl.multiple_of((part * ROWS + n) * CELLS, CELLS), CELLS)
            for k in range(BASIS):
                basis[at, k * HALF : (k + 1) * HALF] = out[k * CELLS : (k + 1) * CELLS]
            return carry

        lax.fori_loop(0, ROWS, step, 0, unroll=16)
    for chosen, part, first in boundary(xl, core):

        @pl.when(chosen)
        def _():
            at = (part * ROWS + first) * CELLS
            basis[at : at + 2 * CELLS, :] = jnp.zeros((2 * CELLS, BASIS * HALF), bf16)

    total = jnp.dot(ct_o[...], basis[0:512, :], preferred_element_type=f32)
    total += jnp.dot(ct_x[...], basis[512:1024, :], preferred_element_type=f32)
    for k in range(BASIS):
        grad[k] = total[:, k * HALF : (k + 1) * HALF].T


def runs(k, side, half):
    begin, at = half * 288 + side * 144 + k * 16, 0
    while at < 16:
        slot, j = divmod(begin + at, 64)
        count = min(16 - at, 64 - j)
        yield at, slot, j, count
        at += count


def weight_end_kernel(
    own, fx, cx, near, far, rows, bo, bx, grad, parts, token, field, cot, tile
):
    mark(token)
    xl, core = here()
    lanes = pl.ds(pl.multiple_of(core * HALF, HALF), HALF)
    field[:, 36:SLOTS, :] = jnp.zeros((6, SLOTS - 36, HALF), bf16)
    field[pl.ds(4 * (1 - xl), 2), 0:36, :] = rows[0, :, 0:36, lanes]
    for chosen, part, first in boundary(xl, core):

        @pl.when(chosen)
        def _():
            ref = (own.at[0], fx)[part]
            at = 2 if first == 0 else 0
            begin = 0 if first == 0 else 12
            side, cross = rows_of(part, begin, 4)
            field[at : at + 4, 0:CELLS, :] = ref[begin : begin + 4, :, lanes]
            field[at : at + 4, CELLS : CELLS + 2, :] = near[0, side, :, lanes]
            field[at : at + 4, CELLS + 2 : CELLS + 4, :] = far[0, cross, :, lanes]
            cot[...] = (own.at[1], cx)[part][first : first + 2].reshape(2 * CELLS, CHAN)
            tile[...] = (bo, bx)[part][first : first + 2]

    basis = []
    for r in range(2):
        window = field[r : r + BAND].reshape(BAND * SLOTS, HALF)
        basis.append(
            jnp.dot(tile[r, :, 0 : BAND * SLOTS], window, preferred_element_type=f32)
        )
    for k in range(BASIS):
        cells = jnp.concatenate([x[k * CELLS : (k + 1) * CELLS] for x in basis], 0)
        total = grad[k] + jnp.dot(cells.T.astype(bf16), cot[...], preferred_element_type=f32)
        for side in range(2):
            tiles = total[:, side * HALF : (side + 1) * HALF].reshape(16, 8, HALF)
            for half in range(2):
                piece = tiles[:, half * 4 : (half + 1) * 4, :].astype(bf16)
                for at, slot, j, count in runs(k, side, half):
                    parts[j : j + count, slot] = piece[at : at + count]


def sum_kernel(scale, parts, after, out, token, copies, sems):
    mark(token)
    total = jnp.sum(parts[...].astype(f32), axis=0) * scale
    copies[...] = jnp.broadcast_to(total.astype(bf16)[None], copies.shape)
    sends = [
        pltpu.make_async_copy(copies, out.at[i * 8 : (i + 1) * 8], sems.at[i]) for i in range(8)
    ]
    for x in sends:
        x.start()
    for x in sends:
        x.wait()


def half_kernel(half_of, tiles_ref, out, stage, sems):
    first = half_of() * 16
    copies = []
    for k in range(BASIS):
        for side in range(2):
            for half in range(2):
                for at, slot, j, count in runs(k, side, half):
                    stage[
                        k,
                        at : at + count,
                        half * 4 : (half + 1) * 4,
                        side * HALF : (side + 1) * HALF,
                    ] = tiles_ref[j : j + count, slot].astype(f32)
        copies.append(
            pltpu.make_async_copy(stage.at[k], out.at[k, pl.ds(first, 16)], sems.at[k])
        )
        copies[-1].start()
    for copy in copies:
        copy.wait()


def own_half_kernel(mine, out, stage, sems):
    half_kernel(lambda: here()[1], mine, out, stage, sems)


def other_half_kernel(theirs, before, out, stage, sems):
    half_kernel(lambda: 1 - here()[1], theirs, out, stage, sems)


def mixed_kernel(
    fo, fx, near, far, rows, mo, w_hbm, after, out, token,
    field, basis, weight, bands, lines, sems
):
    mark(token)
    xl, core = here()
    copy = pltpu.make_async_copy(w_hbm, weight, sems)
    copy.start()
    padded(field, 0, xl, core, fo, fx, near, far, rows, slice(None))
    tap_lines(mo, lines)
    masks = band_masks(CHAN)
    for n in range(ROWS):
        for k in range(BASIS):
            line = band(lines, masks, CHAN, k * ROWS + n)
            bands[n, k * CELLS : (k + 1) * CELLS, :] = line
        window = field[pl.ds(core * ROWS + n, BAND)].reshape(BAND * SLOTS, CHAN)
        part = jnp.dot(
            bands[n, :, 0 : BAND * SLOTS], window, preferred_element_type=f32
        ).astype(bf16)
        for k in range(BASIS):
            basis[n * CELLS : (n + 1) * CELLS, k * CHAN : (k + 1) * CHAN] = part[
                k * CELLS : (k + 1) * CELLS
            ]
    copy.wait()
    out[...] = (
        jnp.dot(basis[...], weight[...], preferred_element_type=f32)
        .astype(bf16)
        .reshape(ROWS, CELLS, CHAN)
    )


def feature_kernel(
    co, cx, near, far, rows, to, tx, w_hbm, after, out, token, field, lines, grads, bands, total,
    weight, sems
):
    mark(token)
    copy = pltpu.make_async_copy(w_hbm, weight, sems)
    copy.start()
    xl, core = here()
    lanes = 512
    around = ROWS + 4
    padded(field, 1, xl, core, co, cx, near, far, rows, slice(None))

    count = around * 8
    row = iota((count, 1), 0)
    beyond = 34 * (1 - xl) - core * ROWS
    other = 2 + (1 - 2 * core) * ROWS
    rep = jnp.dot(one_hot(row, 8, 2, 16, count), to[...], preferred_element_type=f32)
    rep += jnp.dot(one_hot(row, 8, other, 16, count), tx[...], preferred_element_type=f32)
    rep += jnp.dot(
        one_hot(row, 8, beyond, 2, count), rows[1, 0, 38:40, :], preferred_element_type=f32
    )
    _, b, _ = split_taps(iota((1, CHAN), 1))
    k, _, s = split_taps(iota((CHAN, 1), 0))
    lines[...] = spread(rep, b == row - 8 * over(row, 8), k * BAND + 4 - s, lanes, BASIS)
    masks = band_masks(lanes)
    copy.wait()
    for k in range(BASIS):
        for h in range(2):
            upstream = field[pl.ds(core * ROWS + h * 10, 10)].reshape(10 * SLOTS, CHAN)
            back = lax.dot_general(
                upstream,
                weight[k * CHAN : (k + 1) * CHAN, :],
                (((1,), (1,)), ((), ())),
                preferred_element_type=f32,
            )
            grads[h * 10 : (h + 1) * 10, k * SLOTS : (k + 1) * SLOTS, :] = back.astype(
                bf16
            ).reshape(10, SLOTS, CHAN)
    total[...] = jnp.zeros_like(total)

    def step(i, carry):
        for b in range(BAND):
            bands[b * CELLS : (b + 1) * CELLS, :] = band(lines, masks, lanes, i * 8 + b)
        part = jnp.dot(
            bands[:, 0 : BASIS * SLOTS], grads[i], preferred_element_type=f32
        ).reshape(BAND, CELLS, CHAN)
        total[pl.ds(i, BAND)] += part
        return carry

    lax.fori_loop(0, around, step, 0, unroll=4)
    out[...] = total[4 : 4 + ROWS].astype(bf16)


def shards(feature, filters, start, length, weight, cotangent):
    fx = send(feature, core=True)
    cx = send(cotangent, core=True)
    own = jnp.stack([feature, cotangent])

    block = ((ROWS, CELLS, CHAN), bf16)
    tiles = ((ROWS, BASIS * CELLS, CHAN), bf16)
    flat = ((ROWS, CHAN), bf16)
    lines = pltpu.VMEM((BASIS * ROWS, BAND * CHAN), f32)
    (edge,) = call(
        column_kernel,
        [((2, 2 * ROWS, 2, CHAN), bf16)],
        (own, fx, cx),
        traffic=2**20,
        limit=8,
    )
    edge, start = lax.optimization_barrier((edge, start))
    near = send(edge, lon=(1, -1))
    lat = lax.axis_index("xl") * 2 + lax.axis_index("core")
    source = lat * ROWS + jnp.arange(ROWS, dtype=jnp.int32)[:, None] - 2
    source = source + jnp.arange(25, dtype=jnp.int32)[None, :] // BAND - start[:, None]
    inside = (source >= 0) & (source < length[:, None])
    mo = jnp.where(inside[None], filters.transpose(1, 0, 2), jnp.zeros((), bf16))
    mx = send(mo, core=True)

    turned = ((CHAN, 512), bf16)
    bo, ct_o, to = call(
        own_band_kernel,
        [tiles, turned, flat],
        (mo, own, edge),
        scratch=[lines],
        flops=2 * 144 * 256 * 1280,
        traffic=4 * 2**20,
        limit=16,
    )
    bx, ct_x, tx = call(
        other_band_kernel,
        [tiles, turned, flat],
        (mx, cx, to),
        scratch=[lines],
        flops=2 * 144 * 256 * 1280,
        traffic=4 * 2**20,
        limit=16,
    )
    near, bx = lax.optimization_barrier((near, bx))
    far = send(near, core=True)
    halo = (near, far)

    (rows,) = call(
        row_kernel,
        [((2, 2, 40, CHAN), bf16)],
        (own, fx, cx, *halo, to, tx),
        traffic=2**20,
    )
    rows = send(rows, lat=True)
    (grad,) = call(
        weight_kernel,
        [((BASIS, HALF, CHAN), f32)],
        (own, fx, *halo, bo, bx, ct_o, ct_x),
        scratch=[
            pltpu.VMEM((36, SLOTS, HALF), bf16),
            pltpu.VMEM((1024, BASIS * HALF), bf16),
        ],
        flops=2 * 32 * 288 * 256 * 256 + 2 * 1024 * 1152 * 256,
        traffic=7 * 2**20,
    )
    parts, after = call(
        weight_end_kernel,
        [((64, *CHUNK), bf16), TOKEN],
        (own, fx, cx, *halo, rows, bo, bx, grad),
        scratch=[
            pltpu.VMEM((6, SLOTS, HALF), bf16),
            pltpu.VMEM((2 * CELLS, CHAN), bf16),
            pltpu.VMEM((2, BASIS * CELLS, CHAN), bf16),
        ],
        flops=2 * 64 * 1152 * 256,
        traffic=3 * 2**20,
    )
    mixing = weight.reshape(BASIS * CHAN, CHAN)

    swapped = lax.all_to_all(parts, RING, 0, 0, tiled=True)
    mixed, after = call(
        mixed_kernel,
        [block, TOKEN],
        (feature, fx, *halo, rows, mo, mixing, after),
        scratch=[
            pltpu.VMEM((36, SLOTS, CHAN), bf16),
            pltpu.VMEM((512, BASIS * CHAN), bf16),
            pltpu.VMEM((BASIS * CHAN, CHAN), bf16),
            pltpu.VMEM((ROWS, BASIS * CELLS, CHAN), bf16),
            lines,
            pltpu.SemaphoreType.DMA,
        ],
        hbm=(6,),
        flops=2 * 16 * 288 * 256 * 256 + 2 * 512 * 2304 * 256,
        traffic=8 * 2**20,
    )
    shared, after = call(
        functools.partial(sum_kernel, 1.0 / math.sqrt(64 * 1024)),
        [((64, *CHUNK), bf16), TOKEN],
        (swapped, after),
        scratch=[pltpu.VMEM((8, *CHUNK), bf16), pltpu.SemaphoreType.DMA((8,))],
        to=(0,),
        traffic=2**20,
    )

    mine = lax.all_to_all(shared, RING, 0, 0, tiled=True)
    grad_feature, after = call(
        feature_kernel,
        [block, TOKEN],
        (cotangent, cx, *halo, rows, to, tx, mixing, after),
        scratch=[
            pltpu.VMEM((36, SLOTS, CHAN), bf16),
            pltpu.VMEM(((ROWS + 4) * 8, BAND * 512), f32),
            pltpu.VMEM((ROWS + 4, BASIS * SLOTS, CHAN), bf16),
            pltpu.VMEM((BAND * CELLS, 512), bf16),
            pltpu.VMEM((ROWS + 8, CELLS, CHAN), f32),
            pltpu.VMEM((BASIS * CHAN, CHAN), bf16),
            pltpu.SemaphoreType.DMA,
        ],
        hbm=(7,),
        flops=2 * 960 * 2304 * 256 + 2 * 20 * 160 * 512 * 256,
        traffic=8 * 2**20,
    )
    mine, grad_feature = lax.optimization_barrier((mine, grad_feature))
    theirs = send(mine, core=True)
    whole = ((BASIS, 32, 8, CHAN), f32)
    stage = [pltpu.VMEM((BASIS, 16, 8, CHAN), f32), pltpu.SemaphoreType.DMA((BASIS,))]
    (grad_weight,) = call(
        own_half_kernel, [whole], (mine,), scratch=stage, to=(0,), traffic=2 * 2**20, limit=8
    )
    (grad_weight,) = call(
        other_half_kernel,
        [whole],
        (theirs, grad_weight),
        scratch=stage,
        hbm=(1,),
        to=(0,),
        alias={1: 0},
        traffic=2 * 2**20,
        limit=8,
    )
    return (mixed, grad_feature, grad_weight.reshape(BASIS, CHAN, CHAN))


def solution(mesh):
    fine = Mesh(mesh.devices.reshape(SIZES), AXES)
    lat, lon = ("xl", "core"), ("y", "xh", "z")
    return jax.shard_map(
        shards,
        mesh=fine,
        in_specs=(P(lat, lon, None), P(lat, None, None), P(lat), P(lat), P(), P(lat, lon, None)),
        out_specs=(P(lat, lon, None), P(lat, lon, None), P()),
        check_vma=False,
    )
```

```python
import functools
import math

import jax
import jax.numpy as jnp
from jax import lax
from jax.experimental import pallas as pl
from jax.experimental.pallas import tpu as pltpu
from jax.sharding import Mesh, PartitionSpec as P

AXES = ("xl", "core", "y", "xh", "z")
SIZES = (2, 2, 4, 2, 4)
RING = ("xl", "y", "xh", "z")

ROWS = 16
CELLS = 32
SLOTS = 48
BASIS = 9
CHAN = 256
HALF = 128
BAND = 5
CHUNK = (9, 4, 128)
bf16 = jnp.bfloat16
f32 = jnp.float32


def moves(lat=False, core=False, lon=(0, 0)):
    pairs = []
    for xl in range(2):
        for c in range(2):
            for cell in range(32):
                source = (xl * 2 + c) * 32 + cell
                row = (xl ^ int(lat)) * 2 + (c ^ int(core))
                pairs.append((source, row * 32 + (cell + lon[c]) % 32))
    return pairs


def send(x, **way):
    return lax.ppermute(x, AXES, moves(**way))


def vmem(count):
    return [pl.BlockSpec(memory_space=pltpu.VMEM)] * count


HBM = pl.BlockSpec(memory_space=pltpu.HBM)


def mark(token):
    token[...] = jnp.zeros(token.shape, f32)


TOKEN = ((8, 128), jnp.float32)


def here():
    return lax.axis_index("xl"), lax.axis_index("core")


def call(kernel, outs, operands, scratch=(), flops=0, traffic=0, limit=24, hbm=(), to=(), alias=None):
    return pl.pallas_call(
        kernel,
        out_shape=[jax.ShapeDtypeStruct(*o) for o in outs],
        in_specs=[HBM if i in hbm else vmem(1)[0] for i in range(len(operands))],
        out_specs=[HBM if i in to else vmem(1)[0] for i in range(len(outs))],
        scratch_shapes=list(scratch),
        input_output_aliases=alias or {},
        compiler_params=pltpu.CompilerParams(vmem_limit_bytes=limit * 1024 * 1024),
        cost_estimate=pl.CostEstimate(flops=flops, bytes_accessed=traffic, transcendentals=0),
    )(*operands)


def column_kernel(own, fx, cx, edge):
    _, core = here()
    for side in range(2):

        @pl.when(core == side)
        def _():
            cells = slice(CELLS - 2, CELLS) if side == 0 else slice(0, 2)
            for f, other in enumerate((fx, cx)):
                edge[f, 0:ROWS] = own[f, :, cells, :]
                edge[f, ROWS : 2 * ROWS] = other[:, cells, :]


def boundary(xl, core):
    return [
        ((xl == side) & (core == (1 - side if part == 0 else side)), part, 14 * (1 - side))
        for side in range(2)
        for part in range(2)
    ]


def rows_of(part, first, count):
    return [slice(p * ROWS + first, p * ROWS + first + count) for p in (part, 1 - part)]


def row_kernel(own, fx, cx, near, far, to, tx, rows):
    xl, core = here()
    rows[:, :, 36:40, :] = jnp.zeros((2, 2, 4, CHAN), bf16)
    for chosen, part, first in boundary(xl, core):

        @pl.when(chosen)
        def _():
            span = slice(first, first + 2)
            side, cross = rows_of(part, first, 2)
            for f, pair in enumerate(((own.at[0], fx), (own.at[1], cx))):
                rows[f, :, 0:CELLS, :] = pair[part][span]
                rows[f, :, CELLS : CELLS + 2, :] = near[f, side]
                rows[f, :, CELLS + 2 : CELLS + 4, :] = far[f, cross]
            rows[1, 0, 38:40, :] = (to, tx)[part][span]


def padded(dst, f, xl, core, own, other, near, far, rows, lanes):
    width = dst.shape[-1]
    dst[:, 36:SLOTS, :] = jnp.zeros((36, SLOTS - 36, width), bf16)
    for part, ref in enumerate((own, other)):
        at = pl.ds(2 + ROWS * (core if part == 0 else 1 - core), ROWS)
        side, cross = rows_of(part, 0, ROWS)
        dst[at, 0:CELLS, :] = ref[:, :, lanes]
        dst[at, CELLS : CELLS + 2, :] = near[f, side, :, lanes]
        dst[at, CELLS + 2 : CELLS + 4, :] = far[f, cross, :, lanes]
    if rows is None:
        dst[0:2] = jnp.zeros((2, SLOTS, width), bf16)
        dst[34:36] = jnp.zeros((2, SLOTS, width), bf16)
    else:
        dst[pl.ds(34 * (1 - xl), 2), 0:36, :] = rows[f, :, 0:36, lanes]
        dst[pl.ds(34 * xl, 2)] = jnp.zeros((2, SLOTS, width), bf16)


def over(index, divisor):
    return ((index.astype(f32) + 0.5) * (1.0 / divisor)).astype(jnp.int32)


def split_taps(index):
    k = over(index, 25)
    tap = index - 25 * k
    b = over(tap, 5)
    return k, b, tap - 5 * b


def iota(shape, axis):
    return lax.broadcasted_iota(jnp.int32, shape, axis)


def band_masks(lanes):
    _, core = here()
    cell = iota((CELLS, lanes), 0)
    lane = iota((CELLS, lanes), 1)
    slot = lane - SLOTS * over(lane, SLOTS)
    side = jnp.where(slot < CELLS + 2, slot - 34 * (1 - core), slot - 2 - 34 * core)
    place = jnp.where(slot < CELLS, slot, jnp.where(slot < CELLS + 4, side, 1000))
    return [(place - cell + 2) == s for s in range(BAND)]


def band(block, masks, lanes, row):
    total = jnp.zeros((CELLS, lanes), f32)
    for s in range(BAND):
        line = block[pl.ds(row, 1), s * lanes : (s + 1) * lanes]
        total = jnp.where(masks[s], jnp.broadcast_to(line, (CELLS, lanes)), total)
    return total.astype(bf16)


def one_hot(row, group, offset, count, total):
    column = iota((total, count), 1)
    return (over(row, group) == column + offset).astype(f32).astype(bf16)


def spread(rep, keep, row_key, lanes, inner):
    lane = iota((1, BAND * lanes), 1)
    s = over(lane, lanes)
    o = over(lane - lanes * s, SLOTS)
    lane_key = jnp.where(o < inner, o * BAND + s, -2)
    table = jnp.where(row_key == lane_key, 1.0, 0.0).astype(bf16)
    kept = jnp.where(keep, rep, 0.0).astype(bf16)
    return jnp.dot(kept, table, preferred_element_type=f32)


def band_table():
    lane = iota((1, BAND * CHAN), 1)
    s = over(lane, CHAN)
    b = over(lane - CHAN * s, SLOTS)
    key = jnp.where(b < BAND, b * BAND + s, -1)
    return jnp.where(iota((25, 1), 0) == key, 1.0, 0.0).astype(bf16)


def tap_lines(taps, lines):
    lines[...] = jnp.dot(
        taps[...].reshape(BASIS * ROWS, 25), band_table(), preferred_element_type=f32
    )


def all_bands(taps, bands, lines):
    tap_lines(taps, lines)
    masks = band_masks(CHAN)

    def step(n, carry):
        for k in range(BASIS):
            line = band(lines, masks, CHAN, k * ROWS + n)
            bands[n, k * CELLS : (k + 1) * CELLS, :] = line
        return carry

    lax.fori_loop(0, ROWS, step, 0, unroll=4)


def own_band_kernel(mo, own, after, bo, cot_t, to, lines):
    to[...] = flat_taps(mo)
    all_bands(mo, bo, lines)
    cot_t[...] = own[1].reshape(512, CHAN).T


def other_band_kernel(mx, cx, after, bx, cot_t, tx, lines):
    tx[...] = flat_taps(mx)
    all_bands(mx, bx, lines)
    cot_t[...] = cx[...].reshape(512, CHAN).T


def flat_taps(taps):
    total = jnp.zeros((ROWS, CHAN), f32)
    for k in range(BASIS):
        at = iota((25, CHAN), 1) == iota((25, CHAN), 0) + 25 * k
        total += jnp.dot(taps[k], at.astype(f32).astype(bf16), preferred_element_type=f32)
    return total.astype(bf16)


def weight_kernel(own, fx, near, far, bo, bx, ct_o, ct_x, grad, field, basis):
    xl, core = here()
    lanes = pl.ds(pl.multiple_of(core * HALF, HALF), HALF)
    padded(field, 0, xl, core, own.at[0], fx, near, far, None, lanes)

    for part, bands in enumerate((bo, bx)):
        begin = ROWS * (core if part == 0 else 1 - core)

        def step(n, carry):
            window = field[pl.ds(begin + n, BAND)].reshape(BAND * SLOTS, HALF)
            out = jnp.dot(
                bands[n, :, 0 : BAND * SLOTS], window, preferred_element_type=f32
            ).astype(bf16)
            at = pl.ds(pl.multiple_of((part * ROWS + n) * CELLS, CELLS), CELLS)
            for k in range(BASIS):
                basis[at, k * HALF : (k + 1) * HALF] = out[k * CELLS : (k + 1) * CELLS]
            return carry

        lax.fori_loop(0, ROWS, step, 0, unroll=16)
    for chosen, part, first in boundary(xl, core):

        @pl.when(chosen)
        def _():
            at = (part * ROWS + first) * CELLS
            basis[at : at + 2 * CELLS, :] = jnp.zeros((2 * CELLS, BASIS * HALF), bf16)

    total = jnp.dot(ct_o[...], basis[0:512, :], preferred_element_type=f32)
    total += jnp.dot(ct_x[...], basis[512:1024, :], preferred_element_type=f32)
    for k in range(BASIS):
        grad[k] = total[:, k * HALF : (k + 1) * HALF].T


def quarters():
    for side in range(2):
        for half in range(2):
            first = (half * 2 + side) * 16
            lanes = slice(side * HALF, (side + 1) * HALF)
            yield slice(first, first + 16), slice(half * 4, (half + 1) * 4), lanes


def weight_end_kernel(
    own, fx, cx, near, far, rows, bo, bx, grad, out, token,
    field, cot, tile, parts, sems
):
    mark(token)
    xl, core = here()
    lanes = pl.ds(pl.multiple_of(core * HALF, HALF), HALF)
    field[:, 36:SLOTS, :] = jnp.zeros((6, SLOTS - 36, HALF), bf16)
    field[pl.ds(4 * (1 - xl), 2), 0:36, :] = rows[0, :, 0:36, lanes]
    for chosen, part, first in boundary(xl, core):

        @pl.when(chosen)
        def _():
            ref = (own.at[0], fx)[part]
            at = 2 if first == 0 else 0
            begin = 0 if first == 0 else 12
            side, cross = rows_of(part, begin, 4)
            field[at : at + 4, 0:CELLS, :] = ref[begin : begin + 4, :, lanes]
            field[at : at + 4, CELLS : CELLS + 2, :] = near[0, side, :, lanes]
            field[at : at + 4, CELLS + 2 : CELLS + 4, :] = far[0, cross, :, lanes]
            cot[...] = (own.at[1], cx)[part][first : first + 2].reshape(2 * CELLS, CHAN)
            tile[...] = (bo, bx)[part][first : first + 2]

    basis = []
    for r in range(2):
        window = field[r : r + BAND].reshape(BAND * SLOTS, HALF)
        basis.append(
            jnp.dot(tile[r, :, 0 : BAND * SLOTS], window, preferred_element_type=f32)
        )
    sends = []
    for k in range(BASIS):
        cells = jnp.concatenate([x[k * CELLS : (k + 1) * CELLS] for x in basis], 0)
        total = grad[k] + jnp.dot(cells.T.astype(bf16), cot[...], preferred_element_type=f32)
        tiles = total.reshape(16, 8, CHAN)
        for chunks, rows_, columns in quarters():
            parts[chunks, k] = tiles[:, rows_, columns].astype(bf16)
        sends.append(pltpu.make_async_copy(parts.at[:, k], out.at[:, k], sems.at[k]))
        sends[-1].start()
    for x in sends:
        x.wait()


def sum_kernel(scale, parts, after, out, token, copies, sems):
    mark(token)
    total = jnp.sum(parts[...].astype(f32), axis=0) * scale
    copies[...] = jnp.broadcast_to(total.astype(bf16)[None], copies.shape)
    sends = [
        pltpu.make_async_copy(copies, out.at[i * 8 : (i + 1) * 8], sems.at[i]) for i in range(8)
    ]
    for x in sends:
        x.start()
    for x in sends:
        x.wait()


def half_kernel(half_of, tiles_ref, out, stage, sems):
    first = half_of() * 16
    copies = []
    for k in range(BASIS):
        for chunks, rows_, columns in quarters():
            stage[k, :, rows_, columns] = tiles_ref[chunks, k].astype(f32)
        copies.append(
            pltpu.make_async_copy(stage.at[k], out.at[k, pl.ds(first, 16)], sems.at[k])
        )
        copies[-1].start()
    for copy in copies:
        copy.wait()


def own_half_kernel(mine, out, stage, sems):
    half_kernel(lambda: here()[1], mine, out, stage, sems)


def other_half_kernel(theirs, before, out, stage, sems):
    half_kernel(lambda: 1 - here()[1], theirs, out, stage, sems)


def mixed_kernel(
    fo, fx, near, far, rows, mo, w_hbm, after, out, token,
    field, basis, weight, bands, lines, sems
):
    mark(token)
    xl, core = here()
    copy = pltpu.make_async_copy(w_hbm, weight, sems)
    copy.start()
    padded(field, 0, xl, core, fo, fx, near, far, rows, slice(None))
    tap_lines(mo, lines)
    masks = band_masks(CHAN)
    for n in range(ROWS):
        for k in range(BASIS):
            line = band(lines, masks, CHAN, k * ROWS + n)
            bands[n, k * CELLS : (k + 1) * CELLS, :] = line
        window = field[pl.ds(core * ROWS + n, BAND)].reshape(BAND * SLOTS, CHAN)
        part = jnp.dot(
            bands[n, :, 0 : BAND * SLOTS], window, preferred_element_type=f32
        ).astype(bf16)
        for k in range(BASIS):
            basis[n * CELLS : (n + 1) * CELLS, k * CHAN : (k + 1) * CHAN] = part[
                k * CELLS : (k + 1) * CELLS
            ]
    copy.wait()
    out[...] = (
        jnp.dot(basis[...], weight[...], preferred_element_type=f32)
        .astype(bf16)
        .reshape(ROWS, CELLS, CHAN)
    )


def feature_kernel(
    co, cx, near, far, rows, to, tx, w_hbm, after, out, token, field, lines, grads, bands, total,
    weight, sems
):
    mark(token)
    copy = pltpu.make_async_copy(w_hbm, weight, sems)
    copy.start()
    xl, core = here()
    lanes = 512
    around = ROWS + 4
    padded(field, 1, xl, core, co, cx, near, far, rows, slice(None))

    count = around * 8
    row = iota((count, 1), 0)
    beyond = 34 * (1 - xl) - core * ROWS
    other = 2 + (1 - 2 * core) * ROWS
    rep = jnp.dot(one_hot(row, 8, 2, 16, count), to[...], preferred_element_type=f32)
    rep += jnp.dot(one_hot(row, 8, other, 16, count), tx[...], preferred_element_type=f32)
    rep += jnp.dot(
        one_hot(row, 8, beyond, 2, count), rows[1, 0, 38:40, :], preferred_element_type=f32
    )
    _, b, _ = split_taps(iota((1, CHAN), 1))
    k, _, s = split_taps(iota((CHAN, 1), 0))
    lines[...] = spread(rep, b == row - 8 * over(row, 8), k * BAND + 4 - s, lanes, BASIS)
    masks = band_masks(lanes)
    copy.wait()
    for k in range(BASIS):
        for h in range(2):
            upstream = field[pl.ds(core * ROWS + h * 10, 10)].reshape(10 * SLOTS, CHAN)
            back = lax.dot_general(
                upstream,
                weight[k * CHAN : (k + 1) * CHAN, :],
                (((1,), (1,)), ((), ())),
                preferred_element_type=f32,
            )
            grads[h * 10 : (h + 1) * 10, k * SLOTS : (k + 1) * SLOTS, :] = back.astype(
                bf16
            ).reshape(10, SLOTS, CHAN)
    total[...] = jnp.zeros_like(total)

    def step(i, carry):
        for b in range(BAND):
            bands[b * CELLS : (b + 1) * CELLS, :] = band(lines, masks, lanes, i * 8 + b)
        part = jnp.dot(
            bands[:, 0 : BASIS * SLOTS], grads[i], preferred_element_type=f32
        ).reshape(BAND, CELLS, CHAN)
        total[pl.ds(i, BAND)] += part
        return carry

    lax.fori_loop(0, around, step, 0, unroll=4)
    out[...] = total[4 : 4 + ROWS].astype(bf16)


def shards(feature, filters, start, length, weight, cotangent):
    fx = send(feature, core=True)
    cx = send(cotangent, core=True)
    own = jnp.stack([feature, cotangent])

    block = ((ROWS, CELLS, CHAN), bf16)
    tiles = ((ROWS, BASIS * CELLS, CHAN), bf16)
    flat = ((ROWS, CHAN), bf16)
    lines = pltpu.VMEM((BASIS * ROWS, BAND * CHAN), f32)
    (edge,) = call(
        column_kernel,
        [((2, 2 * ROWS, 2, CHAN), bf16)],
        (own, fx, cx),
        traffic=2**20,
        limit=8,
    )
    edge, start = lax.optimization_barrier((edge, start))
    near = send(edge, lon=(1, -1))
    lat = lax.axis_index("xl") * 2 + lax.axis_index("core")
    source = lat * ROWS + jnp.arange(ROWS, dtype=jnp.int32)[:, None] - 2
    source = source + jnp.arange(25, dtype=jnp.int32)[None, :] // BAND - start[:, None]
    inside = (source >= 0) & (source < length[:, None])
    mo = jnp.where(inside[None], filters.transpose(1, 0, 2), jnp.zeros((), bf16))
    mx = send(mo, core=True)

    turned = ((CHAN, 512), bf16)
    bo, ct_o, to = call(
        own_band_kernel,
        [tiles, turned, flat],
        (mo, own, edge),
        scratch=[lines],
        flops=2 * 144 * 256 * 1280,
        traffic=4 * 2**20,
        limit=16,
    )
    bx, ct_x, tx = call(
        other_band_kernel,
        [tiles, turned, flat],
        (mx, cx, to),
        scratch=[lines],
        flops=2 * 144 * 256 * 1280,
        traffic=4 * 2**20,
        limit=16,
    )
    near, bx = lax.optimization_barrier((near, bx))
    far = send(near, core=True)
    halo = (near, far)

    (rows,) = call(
        row_kernel,
        [((2, 2, 40, CHAN), bf16)],
        (own, fx, cx, *halo, to, tx),
        traffic=2**20,
    )
    rows = send(rows, lat=True)
    (grad,) = call(
        weight_kernel,
        [((BASIS, HALF, CHAN), f32)],
        (own, fx, *halo, bo, bx, ct_o, ct_x),
        scratch=[
            pltpu.VMEM((36, SLOTS, HALF), bf16),
            pltpu.VMEM((1024, BASIS * HALF), bf16),
        ],
        flops=2 * 32 * 288 * 256 * 256 + 2 * 1024 * 1152 * 256,
        traffic=7 * 2**20,
    )
    parts, after = call(
        weight_end_kernel,
        [((64, *CHUNK), bf16), TOKEN],
        (own, fx, cx, *halo, rows, bo, bx, grad),
        scratch=[
            pltpu.VMEM((6, SLOTS, HALF), bf16),
            pltpu.VMEM((2 * CELLS, CHAN), bf16),
            pltpu.VMEM((2, BASIS * CELLS, CHAN), bf16),
            pltpu.VMEM((64, *CHUNK), bf16),
            pltpu.SemaphoreType.DMA((BASIS,)),
        ],
        to=(0,),
        flops=2 * 64 * 1152 * 256,
        traffic=3 * 2**20,
    )
    mixing = weight.reshape(BASIS * CHAN, CHAN)

    swapped = lax.all_to_all(parts, RING, 0, 0, tiled=True)
    mixed, after = call(
        mixed_kernel,
        [block, TOKEN],
        (feature, fx, *halo, rows, mo, mixing, after),
        scratch=[
            pltpu.VMEM((36, SLOTS, CHAN), bf16),
            pltpu.VMEM((512, BASIS * CHAN), bf16),
            pltpu.VMEM((BASIS * CHAN, CHAN), bf16),
            pltpu.VMEM((ROWS, BASIS * CELLS, CHAN), bf16),
            lines,
            pltpu.SemaphoreType.DMA,
        ],
        hbm=(6,),
        flops=2 * 16 * 288 * 256 * 256 + 2 * 512 * 2304 * 256,
        traffic=8 * 2**20,
    )
    shared, after = call(
        functools.partial(sum_kernel, 1.0 / math.sqrt(64 * 1024)),
        [((64, *CHUNK), bf16), TOKEN],
        (swapped, after),
        scratch=[pltpu.VMEM((8, *CHUNK), bf16), pltpu.SemaphoreType.DMA((8,))],
        to=(0,),
        traffic=2**20,
    )

    mine = lax.all_to_all(shared, RING, 0, 0, tiled=True)
    grad_feature, after = call(
        feature_kernel,
        [block, TOKEN],
        (cotangent, cx, *halo, rows, to, tx, mixing, after),
        scratch=[
            pltpu.VMEM((36, SLOTS, CHAN), bf16),
            pltpu.VMEM(((ROWS + 4) * 8, BAND * 512), f32),
            pltpu.VMEM((ROWS + 4, BASIS * SLOTS, CHAN), bf16),
            pltpu.VMEM((BAND * CELLS, 512), bf16),
            pltpu.VMEM((ROWS + 8, CELLS, CHAN), f32),
            pltpu.VMEM((BASIS * CHAN, CHAN), bf16),
            pltpu.SemaphoreType.DMA,
        ],
        hbm=(7,),
        flops=2 * 960 * 2304 * 256 + 2 * 20 * 160 * 512 * 256,
        traffic=8 * 2**20,
    )
    mine, grad_feature = lax.optimization_barrier((mine, grad_feature))
    theirs = send(mine, core=True)
    whole = ((BASIS, 32, 8, CHAN), f32)
    stage = [pltpu.VMEM((BASIS, 16, 8, CHAN), f32), pltpu.SemaphoreType.DMA((BASIS,))]
    (grad_weight,) = call(
        own_half_kernel, [whole], (mine,), scratch=stage, to=(0,), traffic=2 * 2**20, limit=8
    )
    (grad_weight,) = call(
        other_half_kernel,
        [whole],
        (theirs, grad_weight),
        scratch=stage,
        hbm=(1,),
        to=(0,),
        alias={1: 0},
        traffic=2 * 2**20,
        limit=8,
    )
    return (mixed, grad_feature, grad_weight.reshape(BASIS, CHAN, CHAN))


def solution(mesh):
    fine = Mesh(mesh.devices.reshape(SIZES), AXES)
    lat, lon = ("xl", "core"), ("y", "xh", "z")
    return jax.shard_map(
        shards,
        mesh=fine,
        in_specs=(P(lat, lon, None), P(lat, None, None), P(lat), P(lat), P(), P(lat, lon, None)),
        out_specs=(P(lat, lon, None), P(lat, lon, None), P()),
        check_vma=False,
    )
```

```python
import functools
import math

import jax
import jax.numpy as jnp
from jax import lax
from jax.experimental import pallas as pl
from jax.experimental.pallas import tpu as pltpu
from jax.sharding import Mesh, PartitionSpec as P

AXES = ("xl", "core", "y", "xh", "z")
SIZES = (2, 2, 4, 2, 4)
RING = ("xl", "y", "xh", "z")

ROWS = 16
CELLS = 32
SLOTS = 48
BASIS = 9
CHAN = 256
HALF = 128
BAND = 5
CHUNK = (9, 4, 128)
bf16 = jnp.bfloat16
f32 = jnp.float32


def moves(lat=False, core=False, lon=(0, 0)):
    pairs = []
    for xl in range(2):
        for c in range(2):
            for cell in range(32):
                source = (xl * 2 + c) * 32 + cell
                row = (xl ^ int(lat)) * 2 + (c ^ int(core))
                pairs.append((source, row * 32 + (cell + lon[c]) % 32))
    return pairs


def send(x, **way):
    return lax.ppermute(x, AXES, moves(**way))


def vmem(count):
    return [pl.BlockSpec(memory_space=pltpu.VMEM)] * count


HBM = pl.BlockSpec(memory_space=pltpu.HBM)


def mark(token):
    token[...] = jnp.zeros(token.shape, f32)


TOKEN = ((8, 128), jnp.float32)


def here():
    return lax.axis_index("xl"), lax.axis_index("core")


def call(kernel, outs, operands, scratch=(), flops=0, traffic=0, limit=24, hbm=(), to=(), alias=None):
    return pl.pallas_call(
        kernel,
        out_shape=[jax.ShapeDtypeStruct(*o) for o in outs],
        in_specs=[HBM if i in hbm else vmem(1)[0] for i in range(len(operands))],
        out_specs=[HBM if i in to else vmem(1)[0] for i in range(len(outs))],
        scratch_shapes=list(scratch),
        input_output_aliases=alias or {},
        compiler_params=pltpu.CompilerParams(vmem_limit_bytes=limit * 1024 * 1024),
        cost_estimate=pl.CostEstimate(flops=flops, bytes_accessed=traffic, transcendentals=0),
    )(*operands)


def column_kernel(f, own, other, edge):
    _, core = here()
    for side in range(2):

        @pl.when(core == side)
        def _():
            cells = slice(CELLS - 2, CELLS) if side == 0 else slice(0, 2)
            edge[0:ROWS] = own[f, :, cells, :]
            edge[ROWS : 2 * ROWS] = other[:, cells, :]


def boundary(xl, core):
    return [
        ((xl == side) & (core == (1 - side if part == 0 else side)), part, 14 * (1 - side))
        for side in range(2)
        for part in range(2)
    ]


def rows_of(part, first, count):
    return [slice(p * ROWS + first, p * ROWS + first + count) for p in (part, 1 - part)]


def row_kernel(f, own, other, near, far, to, tx, rows):
    xl, core = here()
    rows[:, 36:40, :] = jnp.zeros((2, 4, CHAN), bf16)
    for chosen, part, first in boundary(xl, core):

        @pl.when(chosen)
        def _():
            span = slice(first, first + 2)
            side, cross = rows_of(part, first, 2)
            rows[:, 0:CELLS, :] = (own.at[f], other)[part][span]
            rows[:, CELLS : CELLS + 2, :] = near[side]
            rows[:, CELLS + 2 : CELLS + 4, :] = far[cross]
            rows[0, 38:40, :] = (to, tx)[part][span]


def padded(dst, xl, core, own, other, near, far, rows, lanes):
    width = dst.shape[-1]
    dst[:, 36:SLOTS, :] = jnp.zeros((36, SLOTS - 36, width), bf16)
    for part, ref in enumerate((own, other)):
        at = pl.ds(2 + ROWS * (core if part == 0 else 1 - core), ROWS)
        side, cross = rows_of(part, 0, ROWS)
        dst[at, 0:CELLS, :] = ref[:, :, lanes]
        dst[at, CELLS : CELLS + 2, :] = near[side, :, lanes]
        dst[at, CELLS + 2 : CELLS + 4, :] = far[cross, :, lanes]
    if rows is None:
        dst[0:2] = jnp.zeros((2, SLOTS, width), bf16)
        dst[34:36] = jnp.zeros((2, SLOTS, width), bf16)
    else:
        dst[pl.ds(34 * (1 - xl), 2), 0:36, :] = rows[:, 0:36, lanes]
        dst[pl.ds(34 * xl, 2)] = jnp.zeros((2, SLOTS, width), bf16)


def over(index, divisor):
    return ((index.astype(f32) + 0.5) * (1.0 / divisor)).astype(jnp.int32)


def split_taps(index):
    k = over(index, 25)
    tap = index - 25 * k
    b = over(tap, 5)
    return k, b, tap - 5 * b


def iota(shape, axis):
    return lax.broadcasted_iota(jnp.int32, shape, axis)


def band_masks(lanes):
    _, core = here()
    cell = iota((CELLS, lanes), 0)
    lane = iota((CELLS, lanes), 1)
    slot = lane - SLOTS * over(lane, SLOTS)
    side = jnp.where(slot < CELLS + 2, slot - 34 * (1 - core), slot - 2 - 34 * core)
    place = jnp.where(slot < CELLS, slot, jnp.where(slot < CELLS + 4, side, 1000))
    return [(place - cell + 2) == s for s in range(BAND)]


def band(block, masks, lanes, row):
    total = jnp.zeros((CELLS, lanes), f32)
    for s in range(BAND):
        line = block[pl.ds(row, 1), s * lanes : (s + 1) * lanes]
        total = jnp.where(masks[s], jnp.broadcast_to(line, (CELLS, lanes)), total)
    return total.astype(bf16)


def one_hot(row, group, offset, count, total):
    column = iota((total, count), 1)
    return (over(row, group) == column + offset).astype(f32).astype(bf16)


def spread(rep, keep, row_key, lanes, inner):
    lane = iota((1, BAND * lanes), 1)
    s = over(lane, lanes)
    o = over(lane - lanes * s, SLOTS)
    lane_key = jnp.where(o < inner, o * BAND + s, -2)
    table = jnp.where(row_key == lane_key, 1.0, 0.0).astype(bf16)
    kept = jnp.where(keep, rep, 0.0).astype(bf16)
    return jnp.dot(kept, table, preferred_element_type=f32)


def band_table():
    lane = iota((1, BAND * CHAN), 1)
    s = over(lane, CHAN)
    b = over(lane - CHAN * s, SLOTS)
    key = jnp.where(b < BAND, b * BAND + s, -1)
    return jnp.where(iota((25, 1), 0) == key, 1.0, 0.0).astype(bf16)


def tap_lines(taps, lines):
    lines[...] = jnp.dot(
        taps[...].reshape(BASIS * ROWS, 25), band_table(), preferred_element_type=f32
    )


def all_bands(taps, bands, lines):
    tap_lines(taps, lines)
    masks = band_masks(CHAN)

    def step(n, carry):
        for k in range(BASIS):
            line = band(lines, masks, CHAN, k * ROWS + n)
            bands[n, k * CELLS : (k + 1) * CELLS, :] = line
        return carry

    lax.fori_loop(0, ROWS, step, 0, unroll=4)


def own_band_kernel(mo, own, after, bo, cot_t, to, lines):
    to[...] = flat_taps(mo)
    all_bands(mo, bo, lines)
    cot_t[...] = own[1].reshape(512, CHAN).T


def other_band_kernel(mx, cx, after, bx, cot_t, tx, lines):
    tx[...] = flat_taps(mx)
    all_bands(mx, bx, lines)
    cot_t[...] = cx[...].reshape(512, CHAN).T


def flat_taps(taps):
    total = jnp.zeros((ROWS, CHAN), f32)
    for k in range(BASIS):
        at = iota((25, CHAN), 1) == iota((25, CHAN), 0) + 25 * k
        total += jnp.dot(taps[k], at.astype(f32).astype(bf16), preferred_element_type=f32)
    return total.astype(bf16)


def weight_kernel(own, fx, near, far, bo, bx, ct_o, ct_x, grad, field, basis):
    xl, core = here()
    lanes = pl.ds(pl.multiple_of(core * HALF, HALF), HALF)
    padded(field, xl, core, own.at[0], fx, near, far, None, lanes)

    for part, bands in enumerate((bo, bx)):
        begin = ROWS * (core if part == 0 else 1 - core)

        def step(n, carry):
            window = field[pl.ds(begin + n, BAND)].reshape(BAND * SLOTS, HALF)
            out = jnp.dot(
                bands[n, :, 0 : BAND * SLOTS], window, preferred_element_type=f32
            ).astype(bf16)
            at = pl.ds(pl.multiple_of((part * ROWS + n) * CELLS, CELLS), CELLS)
            for k in range(BASIS):
                basis[at, k * HALF : (k + 1) * HALF] = out[k * CELLS : (k + 1) * CELLS]
            return carry

        lax.fori_loop(0, ROWS, step, 0, unroll=16)
    for chosen, part, first in boundary(xl, core):

        @pl.when(chosen)
        def _():
            at = (part * ROWS + first) * CELLS
            basis[at : at + 2 * CELLS, :] = jnp.zeros((2 * CELLS, BASIS * HALF), bf16)

    total = jnp.dot(ct_o[...], basis[0:512, :], preferred_element_type=f32)
    total += jnp.dot(ct_x[...], basis[512:1024, :], preferred_element_type=f32)
    for k in range(BASIS):
        grad[k] = total[:, k * HALF : (k + 1) * HALF].T


def quarters():
    for side in range(2):
        for half in range(2):
            first = (half * 2 + side) * 16
            lanes = slice(side * HALF, (side + 1) * HALF)
            yield slice(first, first + 16), slice(half * 4, (half + 1) * 4), lanes


def weight_end_kernel(
    own, fx, cx, near, far, rows, after, bo, bx, grad, out, token,
    field, cot, tile, parts, sems
):
    mark(token)
    xl, core = here()
    lanes = pl.ds(pl.multiple_of(core * HALF, HALF), HALF)
    field[:, 36:SLOTS, :] = jnp.zeros((6, SLOTS - 36, HALF), bf16)
    field[pl.ds(4 * (1 - xl), 2), 0:36, :] = rows[:, 0:36, lanes]
    for chosen, part, first in boundary(xl, core):

        @pl.when(chosen)
        def _():
            ref = (own.at[0], fx)[part]
            at = 2 if first == 0 else 0
            begin = 0 if first == 0 else 12
            side, cross = rows_of(part, begin, 4)
            field[at : at + 4, 0:CELLS, :] = ref[begin : begin + 4, :, lanes]
            field[at : at + 4, CELLS : CELLS + 2, :] = near[side, :, lanes]
            field[at : at + 4, CELLS + 2 : CELLS + 4, :] = far[cross, :, lanes]
            cot[...] = (own.at[1], cx)[part][first : first + 2].reshape(2 * CELLS, CHAN)
            tile[...] = (bo, bx)[part][first : first + 2]

    basis = []
    for r in range(2):
        window = field[r : r + BAND].reshape(BAND * SLOTS, HALF)
        basis.append(
            jnp.dot(tile[r, :, 0 : BAND * SLOTS], window, preferred_element_type=f32)
        )
    sends = []
    for k in range(BASIS):
        cells = jnp.concatenate([x[k * CELLS : (k + 1) * CELLS] for x in basis], 0)
        total = grad[k] + jnp.dot(cells.T.astype(bf16), cot[...], preferred_element_type=f32)
        tiles = total.reshape(16, 8, CHAN)
        for chunks, rows_, columns in quarters():
            parts[chunks, k] = tiles[:, rows_, columns].astype(bf16)
        sends.append(pltpu.make_async_copy(parts.at[:, k], out.at[:, k], sems.at[k]))
        sends[-1].start()
    for x in sends:
        x.wait()


def sum_kernel(scale, parts, after, out, token, copies, sems):
    mark(token)
    total = jnp.sum(parts[...].astype(f32), axis=0) * scale
    copies[...] = jnp.broadcast_to(total.astype(bf16)[None], copies.shape)
    sends = [
        pltpu.make_async_copy(copies, out.at[i * 8 : (i + 1) * 8], sems.at[i]) for i in range(8)
    ]
    for x in sends:
        x.start()
    for x in sends:
        x.wait()


def half_kernel(half_of, tiles_ref, out, stage, sems):
    first = half_of() * 16
    copies = []
    for k in range(BASIS):
        for chunks, rows_, columns in quarters():
            stage[k, :, rows_, columns] = tiles_ref[chunks, k].astype(f32)
        copies.append(
            pltpu.make_async_copy(stage.at[k], out.at[k, pl.ds(first, 16)], sems.at[k])
        )
        copies[-1].start()
    for copy in copies:
        copy.wait()


def own_half_kernel(mine, out, stage, sems):
    half_kernel(lambda: here()[1], mine, out, stage, sems)


def other_half_kernel(theirs, before, out, stage, sems):
    half_kernel(lambda: 1 - here()[1], theirs, out, stage, sems)


def mixed_kernel(
    fo, fx, near, far, rows, mo, w_hbm, after, out, token,
    field, basis, weight, bands, lines, sems
):
    mark(token)
    xl, core = here()
    copy = pltpu.make_async_copy(w_hbm, weight, sems)
    copy.start()
    padded(field, xl, core, fo, fx, near, far, rows, slice(None))
    tap_lines(mo, lines)
    masks = band_masks(CHAN)
    for n in range(ROWS):
        for k in range(BASIS):
            line = band(lines, masks, CHAN, k * ROWS + n)
            bands[n, k * CELLS : (k + 1) * CELLS, :] = line
        window = field[pl.ds(core * ROWS + n, BAND)].reshape(BAND * SLOTS, CHAN)
        part = jnp.dot(
            bands[n, :, 0 : BAND * SLOTS], window, preferred_element_type=f32
        ).astype(bf16)
        for k in range(BASIS):
            basis[n * CELLS : (n + 1) * CELLS, k * CHAN : (k + 1) * CHAN] = part[
                k * CELLS : (k + 1) * CELLS
            ]
    copy.wait()
    out[...] = (
        jnp.dot(basis[...], weight[...], preferred_element_type=f32)
        .astype(bf16)
        .reshape(ROWS, CELLS, CHAN)
    )


def feature_kernel(
    co, cx, near, far, rows, to, tx, w_hbm, after, out, token, field, lines, grads, bands, total,
    weight, sems
):
    mark(token)
    copy = pltpu.make_async_copy(w_hbm, weight, sems)
    copy.start()
    xl, core = here()
    lanes = 512
    around = ROWS + 4
    padded(field, xl, core, co, cx, near, far, rows, slice(None))

    count = around * 8
    row = iota((count, 1), 0)
    beyond = 34 * (1 - xl) - core * ROWS
    other = 2 + (1 - 2 * core) * ROWS
    rep = jnp.dot(one_hot(row, 8, 2, 16, count), to[...], preferred_element_type=f32)
    rep += jnp.dot(one_hot(row, 8, other, 16, count), tx[...], preferred_element_type=f32)
    rep += jnp.dot(
        one_hot(row, 8, beyond, 2, count), rows[0, 38:40, :], preferred_element_type=f32
    )
    _, b, _ = split_taps(iota((1, CHAN), 1))
    k, _, s = split_taps(iota((CHAN, 1), 0))
    lines[...] = spread(rep, b == row - 8 * over(row, 8), k * BAND + 4 - s, lanes, BASIS)
    masks = band_masks(lanes)
    copy.wait()
    for k in range(BASIS):
        for h in range(2):
            upstream = field[pl.ds(core * ROWS + h * 10, 10)].reshape(10 * SLOTS, CHAN)
            back = lax.dot_general(
                upstream,
                weight[k * CHAN : (k + 1) * CHAN, :],
                (((1,), (1,)), ((), ())),
                preferred_element_type=f32,
            )
            grads[h * 10 : (h + 1) * 10, k * SLOTS : (k + 1) * SLOTS, :] = back.astype(
                bf16
            ).reshape(10, SLOTS, CHAN)
    total[...] = jnp.zeros_like(total)

    def step(i, carry):
        for b in range(BAND):
            bands[b * CELLS : (b + 1) * CELLS, :] = band(lines, masks, lanes, i * 8 + b)
        part = jnp.dot(
            bands[:, 0 : BASIS * SLOTS], grads[i], preferred_element_type=f32
        ).reshape(BAND, CELLS, CHAN)
        total[pl.ds(i, BAND)] += part
        return carry

    lax.fori_loop(0, around, step, 0, unroll=4)
    out[...] = total[4 : 4 + ROWS].astype(bf16)


def shards(feature, filters, start, length, weight, cotangent):
    fx = send(feature, core=True)
    cx = send(cotangent, core=True)
    own = jnp.stack([feature, cotangent])

    block = ((ROWS, CELLS, CHAN), bf16)
    tiles = ((ROWS, BASIS * CELLS, CHAN), bf16)
    flat = ((ROWS, CHAN), bf16)
    lines = pltpu.VMEM((BASIS * ROWS, BAND * CHAN), f32)
    column = ((2 * ROWS, 2, CHAN), bf16)
    edges = [
        call(functools.partial(column_kernel, f), [column], (own, other), traffic=2**20, limit=8)[0]
        for f, other in enumerate((fx, cx))
    ]
    near_f = send(edges[0], lon=(1, -1))
    near_c = send(edges[1], lon=(1, -1))
    edge, start = lax.optimization_barrier((edges[0], start))
    lat = lax.axis_index("xl") * 2 + lax.axis_index("core")
    source = lat * ROWS + jnp.arange(ROWS, dtype=jnp.int32)[:, None] - 2
    source = source + jnp.arange(25, dtype=jnp.int32)[None, :] // BAND - start[:, None]
    inside = (source >= 0) & (source < length[:, None])
    mo = jnp.where(inside[None], filters.transpose(1, 0, 2), jnp.zeros((), bf16))
    mx = send(mo, core=True)

    turned = ((CHAN, 512), bf16)
    bo, ct_o, to = call(
        own_band_kernel,
        [tiles, turned, flat],
        (mo, own, edge),
        scratch=[lines],
        flops=2 * 144 * 256 * 1280,
        traffic=4 * 2**20,
        limit=16,
    )
    bx, ct_x, tx = call(
        other_band_kernel,
        [tiles, turned, flat],
        (mx, cx, to),
        scratch=[lines],
        flops=2 * 144 * 256 * 1280,
        traffic=4 * 2**20,
        limit=16,
    )
    near_f, bx = lax.optimization_barrier((near_f, bx))
    far_f = send(near_f, core=True)
    far_c = send(near_c, core=True)

    sides = ((near_f, far_f), (near_c, far_c))
    rows_f, rows_c = [
        send(
            call(
                functools.partial(row_kernel, f),
                [((2, 40, CHAN), bf16)],
                (own, other, *sides[f], to, tx),
                traffic=2**20,
            )[0],
            lat=True,
        )
        for f, other in enumerate((fx, cx))
    ]
    (grad,) = call(
        weight_kernel,
        [((BASIS, HALF, CHAN), f32)],
        (own, fx, *sides[0], bo, bx, ct_o, ct_x),
        scratch=[
            pltpu.VMEM((36, SLOTS, HALF), bf16),
            pltpu.VMEM((1024, BASIS * HALF), bf16),
        ],
        flops=2 * 32 * 288 * 256 * 256 + 2 * 1024 * 1152 * 256,
        traffic=7 * 2**20,
    )
    parts, after = call(
        weight_end_kernel,
        [((64, *CHUNK), bf16), TOKEN],
        (own, fx, cx, *sides[0], rows_f, rows_c, bo, bx, grad),
        scratch=[
            pltpu.VMEM((6, SLOTS, HALF), bf16),
            pltpu.VMEM((2 * CELLS, CHAN), bf16),
            pltpu.VMEM((2, BASIS * CELLS, CHAN), bf16),
            pltpu.VMEM((64, *CHUNK), bf16),
            pltpu.SemaphoreType.DMA((BASIS,)),
        ],
        to=(0,),
        flops=2 * 64 * 1152 * 256,
        traffic=3 * 2**20,
    )
    mixing = weight.reshape(BASIS * CHAN, CHAN)

    swapped = lax.all_to_all(parts, RING, 0, 0, tiled=True)
    mixed, after = call(
        mixed_kernel,
        [block, TOKEN],
        (feature, fx, *sides[0], rows_f, mo, mixing, after),
        scratch=[
            pltpu.VMEM((36, SLOTS, CHAN), bf16),
            pltpu.VMEM((512, BASIS * CHAN), bf16),
            pltpu.VMEM((BASIS * CHAN, CHAN), bf16),
            pltpu.VMEM((ROWS, BASIS * CELLS, CHAN), bf16),
            lines,
            pltpu.SemaphoreType.DMA,
        ],
        hbm=(6,),
        flops=2 * 16 * 288 * 256 * 256 + 2 * 512 * 2304 * 256,
        traffic=8 * 2**20,
    )
    shared, after = call(
        functools.partial(sum_kernel, 1.0 / math.sqrt(64 * 1024)),
        [((64, *CHUNK), bf16), TOKEN],
        (swapped, after),
        scratch=[pltpu.VMEM((8, *CHUNK), bf16), pltpu.SemaphoreType.DMA((8,))],
        to=(0,),
        traffic=2**20,
    )

    mine = lax.all_to_all(shared, RING, 0, 0, tiled=True)
    grad_feature, after = call(
        feature_kernel,
        [block, TOKEN],
        (cotangent, cx, *sides[1], rows_c, to, tx, mixing, after),
        scratch=[
            pltpu.VMEM((36, SLOTS, CHAN), bf16),
            pltpu.VMEM(((ROWS + 4) * 8, BAND * 512), f32),
            pltpu.VMEM((ROWS + 4, BASIS * SLOTS, CHAN), bf16),
            pltpu.VMEM((BAND * CELLS, 512), bf16),
            pltpu.VMEM((ROWS + 8, CELLS, CHAN), f32),
            pltpu.VMEM((BASIS * CHAN, CHAN), bf16),
            pltpu.SemaphoreType.DMA,
        ],
        hbm=(7,),
        flops=2 * 960 * 2304 * 256 + 2 * 20 * 160 * 512 * 256,
        traffic=8 * 2**20,
    )
    mine, grad_feature = lax.optimization_barrier((mine, grad_feature))
    theirs = send(mine, core=True)
    whole = ((BASIS, 32, 8, CHAN), f32)
    stage = [pltpu.VMEM((BASIS, 16, 8, CHAN), f32), pltpu.SemaphoreType.DMA((BASIS,))]
    (grad_weight,) = call(
        own_half_kernel, [whole], (mine,), scratch=stage, to=(0,), traffic=2 * 2**20, limit=8
    )
    (grad_weight,) = call(
        other_half_kernel,
        [whole],
        (theirs, grad_weight),
        scratch=stage,
        hbm=(1,),
        to=(0,),
        alias={1: 0},
        traffic=2 * 2**20,
        limit=8,
    )
    return (mixed, grad_feature, grad_weight.reshape(BASIS, CHAN, CHAN))


def solution(mesh):
    fine = Mesh(mesh.devices.reshape(SIZES), AXES)
    lat, lon = ("xl", "core"), ("y", "xh", "z")
    return jax.shard_map(
        shards,
        mesh=fine,
        in_specs=(P(lat, lon, None), P(lat, None, None), P(lat), P(lat), P(), P(lat, lon, None)),
        out_specs=(P(lat, lon, None), P(lat, lon, None), P()),
        check_vma=False,
    )
```

```python
import functools
import math

import jax
import jax.numpy as jnp
from jax import lax
from jax.experimental import pallas as pl
from jax.experimental.pallas import tpu as pltpu
from jax.sharding import Mesh, PartitionSpec as P

AXES = ("xl", "core", "y", "xh", "z")
SIZES = (2, 2, 4, 2, 4)
RING = ("xl", "y", "xh", "z")

ROWS = 16
CELLS = 32
SLOTS = 48
BASIS = 9
CHAN = 256
HALF = 128
BAND = 5
CHUNK = (9, 4, 128)
bf16 = jnp.bfloat16
f32 = jnp.float32


def moves(lat=False, core=False, lon=(0, 0)):
    pairs = []
    for xl in range(2):
        for c in range(2):
            for cell in range(32):
                source = (xl * 2 + c) * 32 + cell
                row = (xl ^ int(lat)) * 2 + (c ^ int(core))
                pairs.append((source, row * 32 + (cell + lon[c]) % 32))
    return pairs


def send(x, **way):
    return lax.ppermute(x, AXES, moves(**way))


def vmem(count):
    return [pl.BlockSpec(memory_space=pltpu.VMEM)] * count


HBM = pl.BlockSpec(memory_space=pltpu.HBM)


def mark(token):
    token[...] = jnp.zeros(token.shape, f32)


TOKEN = ((8, 128), jnp.float32)


def here():
    return lax.axis_index("xl"), lax.axis_index("core")


def call(kernel, outs, operands, scratch=(), flops=0, traffic=0, limit=24, hbm=(), to=(), alias=None):
    return pl.pallas_call(
        kernel,
        out_shape=[jax.ShapeDtypeStruct(*o) for o in outs],
        in_specs=[HBM if i in hbm else vmem(1)[0] for i in range(len(operands))],
        out_specs=[HBM if i in to else vmem(1)[0] for i in range(len(outs))],
        scratch_shapes=list(scratch),
        input_output_aliases=alias or {},
        compiler_params=pltpu.CompilerParams(vmem_limit_bytes=limit * 1024 * 1024),
        cost_estimate=pl.CostEstimate(flops=flops, bytes_accessed=traffic, transcendentals=0),
    )(*operands)


def column_kernel(f, own, other, edge):
    _, core = here()
    for side in range(2):

        @pl.when(core == side)
        def _():
            cells = slice(CELLS - 2, CELLS) if side == 0 else slice(0, 2)
            edge[0:ROWS] = own[f, :, cells, :]
            edge[ROWS : 2 * ROWS] = other[:, cells, :]


def boundary(xl, core):
    return [
        ((xl == side) & (core == (1 - side if part == 0 else side)), part, 14 * (1 - side))
        for side in range(2)
        for part in range(2)
    ]


def rows_of(part, first, count):
    return [slice(p * ROWS + first, p * ROWS + first + count) for p in (part, 1 - part)]


def row_kernel(f, own, other, near, far, to, tx, rows):
    xl, core = here()
    rows[:, 36:40, :] = jnp.zeros((2, 4, CHAN), bf16)
    for chosen, part, first in boundary(xl, core):

        @pl.when(chosen)
        def _():
            span = slice(first, first + 2)
            side, cross = rows_of(part, first, 2)
            rows[:, 0:CELLS, :] = (own.at[f], other)[part][span]
            rows[:, CELLS : CELLS + 2, :] = near[side]
            rows[:, CELLS + 2 : CELLS + 4, :] = far[cross]
            rows[0, 38:40, :] = (to, tx)[part][span]


def padded(dst, xl, core, own, other, near, far, rows, lanes):
    width = dst.shape[-1]
    dst[:, 36:SLOTS, :] = jnp.zeros((36, SLOTS - 36, width), bf16)
    for part, ref in enumerate((own, other)):
        at = pl.ds(2 + ROWS * (core if part == 0 else 1 - core), ROWS)
        side, cross = rows_of(part, 0, ROWS)
        dst[at, 0:CELLS, :] = ref[:, :, lanes]
        dst[at, CELLS : CELLS + 2, :] = near[side, :, lanes]
        dst[at, CELLS + 2 : CELLS + 4, :] = far[cross, :, lanes]
    if rows is None:
        dst[0:2] = jnp.zeros((2, SLOTS, width), bf16)
        dst[34:36] = jnp.zeros((2, SLOTS, width), bf16)
    else:
        dst[pl.ds(34 * (1 - xl), 2), 0:36, :] = rows[:, 0:36, lanes]
        dst[pl.ds(34 * xl, 2)] = jnp.zeros((2, SLOTS, width), bf16)


def over(index, divisor):
    return ((index.astype(f32) + 0.5) * (1.0 / divisor)).astype(jnp.int32)


def split_taps(index):
    k = over(index, 25)
    tap = index - 25 * k
    b = over(tap, 5)
    return k, b, tap - 5 * b


def iota(shape, axis):
    return lax.broadcasted_iota(jnp.int32, shape, axis)


def band_masks(lanes):
    _, core = here()
    cell = iota((CELLS, lanes), 0)
    lane = iota((CELLS, lanes), 1)
    slot = lane - SLOTS * over(lane, SLOTS)
    side = jnp.where(slot < CELLS + 2, slot - 34 * (1 - core), slot - 2 - 34 * core)
    place = jnp.where(slot < CELLS, slot, jnp.where(slot < CELLS + 4, side, 1000))
    return [(place - cell + 2) == s for s in range(BAND)]


def band(block, masks, lanes, row):
    total = jnp.zeros((CELLS, lanes), f32)
    for s in range(BAND):
        line = block[pl.ds(row, 1), s * lanes : (s + 1) * lanes]
        total = jnp.where(masks[s], jnp.broadcast_to(line, (CELLS, lanes)), total)
    return total.astype(bf16)


def one_hot(row, group, offset, count, total):
    column = iota((total, count), 1)
    return (over(row, group) == column + offset).astype(f32).astype(bf16)


def spread(rep, keep, row_key, lanes, inner):
    lane = iota((1, BAND * lanes), 1)
    s = over(lane, lanes)
    o = over(lane - lanes * s, SLOTS)
    lane_key = jnp.where(o < inner, o * BAND + s, -2)
    table = jnp.where(row_key == lane_key, 1.0, 0.0).astype(bf16)
    kept = jnp.where(keep, rep, 0.0).astype(bf16)
    return jnp.dot(kept, table, preferred_element_type=f32)


def band_table():
    lane = iota((1, BAND * CHAN), 1)
    s = over(lane, CHAN)
    b = over(lane - CHAN * s, SLOTS)
    key = jnp.where(b < BAND, b * BAND + s, -1)
    return jnp.where(iota((25, 1), 0) == key, 1.0, 0.0).astype(bf16)


def tap_lines(taps, lines):
    lines[...] = jnp.dot(
        taps[...].reshape(BASIS * ROWS, 25), band_table(), preferred_element_type=f32
    )


def all_bands(taps, bands, lines):
    tap_lines(taps, lines)
    masks = band_masks(CHAN)

    def step(n, carry):
        for k in range(BASIS):
            line = band(lines, masks, CHAN, k * ROWS + n)
            bands[n, k * CELLS : (k + 1) * CELLS, :] = line
        return carry

    lax.fori_loop(0, ROWS, step, 0, unroll=4)


def own_band_kernel(mo, own, after, bo, cot_t, to, lines):
    to[...] = flat_taps(mo)
    all_bands(mo, bo, lines)
    cot_t[...] = own[1].reshape(512, CHAN).T


def other_band_kernel(mx, cx, after, bx, cot_t, tx, lines):
    tx[...] = flat_taps(mx)
    all_bands(mx, bx, lines)
    cot_t[...] = cx[...].reshape(512, CHAN).T


def flat_taps(taps):
    total = jnp.zeros((ROWS, CHAN), f32)
    for k in range(BASIS):
        at = iota((25, CHAN), 1) == iota((25, CHAN), 0) + 25 * k
        total += jnp.dot(taps[k], at.astype(f32).astype(bf16), preferred_element_type=f32)
    return total.astype(bf16)


def weight_kernel(own, fx, near, far, bo, bx, ct_o, ct_x, grad, field, basis):
    xl, core = here()
    lanes = pl.ds(pl.multiple_of(core * HALF, HALF), HALF)
    padded(field, xl, core, own.at[0], fx, near, far, None, lanes)

    for part, bands in enumerate((bo, bx)):
        begin = ROWS * (core if part == 0 else 1 - core)

        def step(n, carry):
            window = field[pl.ds(begin + n, BAND)].reshape(BAND * SLOTS, HALF)
            out = jnp.dot(
                bands[n, :, 0 : BAND * SLOTS], window, preferred_element_type=f32
            ).astype(bf16)
            at = pl.ds(pl.multiple_of((part * ROWS + n) * CELLS, CELLS), CELLS)
            for k in range(BASIS):
                basis[at, k * HALF : (k + 1) * HALF] = out[k * CELLS : (k + 1) * CELLS]
            return carry

        lax.fori_loop(0, ROWS, step, 0, unroll=16)
    for chosen, part, first in boundary(xl, core):

        @pl.when(chosen)
        def _():
            at = (part * ROWS + first) * CELLS
            basis[at : at + 2 * CELLS, :] = jnp.zeros((2 * CELLS, BASIS * HALF), bf16)

    total = jnp.dot(ct_o[...], basis[0:512, :], preferred_element_type=f32)
    total += jnp.dot(ct_x[...], basis[512:1024, :], preferred_element_type=f32)
    for k in range(BASIS):
        grad[k] = total[:, k * HALF : (k + 1) * HALF].T


def quarters():
    for side in range(2):
        for half in range(2):
            first = (half * 2 + side) * 16
            lanes = slice(side * HALF, (side + 1) * HALF)
            yield slice(first, first + 16), slice(half * 4, (half + 1) * 4), lanes


def weight_end_kernel(
    own, fx, cx, near, far, rows, bo, bx, grad, out, token,
    field, cot, tile, parts, sems
):
    mark(token)
    xl, core = here()
    lanes = pl.ds(pl.multiple_of(core * HALF, HALF), HALF)
    field[:, 36:SLOTS, :] = jnp.zeros((6, SLOTS - 36, HALF), bf16)
    field[pl.ds(4 * (1 - xl), 2), 0:36, :] = rows[:, 0:36, lanes]
    for chosen, part, first in boundary(xl, core):

        @pl.when(chosen)
        def _():
            ref = (own.at[0], fx)[part]
            at = 2 if first == 0 else 0
            begin = 0 if first == 0 else 12
            side, cross = rows_of(part, begin, 4)
            field[at : at + 4, 0:CELLS, :] = ref[begin : begin + 4, :, lanes]
            field[at : at + 4, CELLS : CELLS + 2, :] = near[side, :, lanes]
            field[at : at + 4, CELLS + 2 : CELLS + 4, :] = far[cross, :, lanes]
            cot[...] = (own.at[1], cx)[part][first : first + 2].reshape(2 * CELLS, CHAN)
            tile[...] = (bo, bx)[part][first : first + 2]

    basis = []
    for r in range(2):
        window = field[r : r + BAND].reshape(BAND * SLOTS, HALF)
        basis.append(
            jnp.dot(tile[r, :, 0 : BAND * SLOTS], window, preferred_element_type=f32)
        )
    sends = []
    for k in range(BASIS):
        cells = jnp.concatenate([x[k * CELLS : (k + 1) * CELLS] for x in basis], 0)
        total = grad[k] + jnp.dot(cells.T.astype(bf16), cot[...], preferred_element_type=f32)
        tiles = total.reshape(16, 8, CHAN)
        for chunks, rows_, columns in quarters():
            parts[chunks, k] = tiles[:, rows_, columns].astype(bf16)
        sends.append(pltpu.make_async_copy(parts.at[:, k], out.at[:, k], sems.at[k]))
        sends[-1].start()
    for x in sends:
        x.wait()


def sum_kernel(scale, parts, after, out, token, copies, sems):
    mark(token)
    total = jnp.sum(parts[...].astype(f32), axis=0) * scale
    copies[...] = jnp.broadcast_to(total.astype(bf16)[None], copies.shape)
    sends = [
        pltpu.make_async_copy(copies, out.at[i * 8 : (i + 1) * 8], sems.at[i]) for i in range(8)
    ]
    for x in sends:
        x.start()
    for x in sends:
        x.wait()


def half_kernel(half_of, tiles_ref, out, stage, sems):
    first = half_of() * 16
    copies = []
    for k in range(BASIS):
        for chunks, rows_, columns in quarters():
            stage[k, :, rows_, columns] = tiles_ref[chunks, k].astype(f32)
        copies.append(
            pltpu.make_async_copy(stage.at[k], out.at[k, pl.ds(first, 16)], sems.at[k])
        )
        copies[-1].start()
    for copy in copies:
        copy.wait()


def own_half_kernel(mine, out, stage, sems):
    half_kernel(lambda: here()[1], mine, out, stage, sems)


def other_half_kernel(theirs, before, out, stage, sems):
    half_kernel(lambda: 1 - here()[1], theirs, out, stage, sems)


def mixed_kernel(
    fo, fx, near, far, rows, mo, w_hbm, after, out, token,
    field, basis, weight, bands, lines, sems
):
    mark(token)
    xl, core = here()
    copy = pltpu.make_async_copy(w_hbm, weight, sems)
    copy.start()
    padded(field, xl, core, fo, fx, near, far, rows, slice(None))
    tap_lines(mo, lines)
    masks = band_masks(CHAN)
    for n in range(ROWS):
        for k in range(BASIS):
            line = band(lines, masks, CHAN, k * ROWS + n)
            bands[n, k * CELLS : (k + 1) * CELLS, :] = line
        window = field[pl.ds(core * ROWS + n, BAND)].reshape(BAND * SLOTS, CHAN)
        part = jnp.dot(
            bands[n, :, 0 : BAND * SLOTS], window, preferred_element_type=f32
        ).astype(bf16)
        for k in range(BASIS):
            basis[n * CELLS : (n + 1) * CELLS, k * CHAN : (k + 1) * CHAN] = part[
                k * CELLS : (k + 1) * CELLS
            ]
    copy.wait()
    out[...] = (
        jnp.dot(basis[...], weight[...], preferred_element_type=f32)
        .astype(bf16)
        .reshape(ROWS, CELLS, CHAN)
    )


def feature_kernel(
    co, cx, near, far, rows, to, tx, w_hbm, after, out, token, field, lines, grads, bands, total,
    weight, sems
):
    mark(token)
    copy = pltpu.make_async_copy(w_hbm, weight, sems)
    copy.start()
    xl, core = here()
    lanes = 512
    around = ROWS + 4
    padded(field, xl, core, co, cx, near, far, rows, slice(None))

    count = around * 8
    row = iota((count, 1), 0)
    beyond = 34 * (1 - xl) - core * ROWS
    other = 2 + (1 - 2 * core) * ROWS
    rep = jnp.dot(one_hot(row, 8, 2, 16, count), to[...], preferred_element_type=f32)
    rep += jnp.dot(one_hot(row, 8, other, 16, count), tx[...], preferred_element_type=f32)
    rep += jnp.dot(
        one_hot(row, 8, beyond, 2, count), rows[0, 38:40, :], preferred_element_type=f32
    )
    _, b, _ = split_taps(iota((1, CHAN), 1))
    k, _, s = split_taps(iota((CHAN, 1), 0))
    lines[...] = spread(rep, b == row - 8 * over(row, 8), k * BAND + 4 - s, lanes, BASIS)
    masks = band_masks(lanes)
    copy.wait()
    for k in range(BASIS):
        for h in range(2):
            upstream = field[pl.ds(core * ROWS + h * 10, 10)].reshape(10 * SLOTS, CHAN)
            back = lax.dot_general(
                upstream,
                weight[k * CHAN : (k + 1) * CHAN, :],
                (((1,), (1,)), ((), ())),
                preferred_element_type=f32,
            )
            grads[h * 10 : (h + 1) * 10, k * SLOTS : (k + 1) * SLOTS, :] = back.astype(
                bf16
            ).reshape(10, SLOTS, CHAN)
    total[...] = jnp.zeros_like(total)

    def step(i, carry):
        for b in range(BAND):
            bands[b * CELLS : (b + 1) * CELLS, :] = band(lines, masks, lanes, i * 8 + b)
        part = jnp.dot(
            bands[:, 0 : BASIS * SLOTS], grads[i], preferred_element_type=f32
        ).reshape(BAND, CELLS, CHAN)
        total[pl.ds(i, BAND)] += part
        return carry

    lax.fori_loop(0, around, step, 0, unroll=4)
    out[...] = total[4 : 4 + ROWS].astype(bf16)


def shards(feature, filters, start, length, weight, cotangent):
    fx = send(feature, core=True)
    cx = send(cotangent, core=True)
    own = jnp.stack([feature, cotangent])

    block = ((ROWS, CELLS, CHAN), bf16)
    tiles = ((ROWS, BASIS * CELLS, CHAN), bf16)
    flat = ((ROWS, CHAN), bf16)
    lines = pltpu.VMEM((BASIS * ROWS, BAND * CHAN), f32)
    column = ((2 * ROWS, 2, CHAN), bf16)
    edges = [
        call(functools.partial(column_kernel, f), [column], (own, other), traffic=2**20, limit=8)[0]
        for f, other in enumerate((fx, cx))
    ]
    near_f = send(edges[0], lon=(1, -1))
    near_c = send(edges[1], lon=(1, -1))
    edge, start = lax.optimization_barrier((edges[0], start))
    lat = lax.axis_index("xl") * 2 + lax.axis_index("core")
    source = lat * ROWS + jnp.arange(ROWS, dtype=jnp.int32)[:, None] - 2
    source = source + jnp.arange(25, dtype=jnp.int32)[None, :] // BAND - start[:, None]
    inside = (source >= 0) & (source < length[:, None])
    mo = jnp.where(inside[None], filters.transpose(1, 0, 2), jnp.zeros((), bf16))
    mx = send(mo, core=True)

    turned = ((CHAN, 512), bf16)
    bo, ct_o, to = call(
        own_band_kernel,
        [tiles, turned, flat],
        (mo, own, edge),
        scratch=[lines],
        flops=2 * 144 * 256 * 1280,
        traffic=4 * 2**20,
        limit=16,
    )
    bx, ct_x, tx = call(
        other_band_kernel,
        [tiles, turned, flat],
        (mx, cx, to),
        scratch=[lines],
        flops=2 * 144 * 256 * 1280,
        traffic=4 * 2**20,
        limit=16,
    )
    near_f, bx = lax.optimization_barrier((near_f, bx))
    far_f = send(near_f, core=True)
    far_c = send(near_c, core=True)

    sides = ((near_f, far_f), (near_c, far_c))
    rows_f, rows_c = [
        send(
            call(
                functools.partial(row_kernel, f),
                [((2, 40, CHAN), bf16)],
                (own, other, *sides[f], to, tx),
                traffic=2**20,
            )[0],
            lat=True,
        )
        for f, other in enumerate((fx, cx))
    ]
    (grad,) = call(
        weight_kernel,
        [((BASIS, HALF, CHAN), f32)],
        (own, fx, *sides[0], bo, bx, ct_o, ct_x),
        scratch=[
            pltpu.VMEM((36, SLOTS, HALF), bf16),
            pltpu.VMEM((1024, BASIS * HALF), bf16),
        ],
        flops=2 * 32 * 288 * 256 * 256 + 2 * 1024 * 1152 * 256,
        traffic=7 * 2**20,
    )
    parts, after = call(
        weight_end_kernel,
        [((64, *CHUNK), bf16), TOKEN],
        (own, fx, cx, *sides[0], rows_f, bo, bx, grad),
        scratch=[
            pltpu.VMEM((6, SLOTS, HALF), bf16),
            pltpu.VMEM((2 * CELLS, CHAN), bf16),
            pltpu.VMEM((2, BASIS * CELLS, CHAN), bf16),
            pltpu.VMEM((64, *CHUNK), bf16),
            pltpu.SemaphoreType.DMA((BASIS,)),
        ],
        to=(0,),
        flops=2 * 64 * 1152 * 256,
        traffic=3 * 2**20,
    )
    mixing = weight.reshape(BASIS * CHAN, CHAN)

    parts, rows_c = lax.optimization_barrier((parts, rows_c))
    swapped = lax.all_to_all(parts, RING, 0, 0, tiled=True)
    mixed, after = call(
        mixed_kernel,
        [block, TOKEN],
        (feature, fx, *sides[0], rows_f, mo, mixing, after),
        scratch=[
            pltpu.VMEM((36, SLOTS, CHAN), bf16),
            pltpu.VMEM((512, BASIS * CHAN), bf16),
            pltpu.VMEM((BASIS * CHAN, CHAN), bf16),
            pltpu.VMEM((ROWS, BASIS * CELLS, CHAN), bf16),
            lines,
            pltpu.SemaphoreType.DMA,
        ],
        hbm=(6,),
        flops=2 * 16 * 288 * 256 * 256 + 2 * 512 * 2304 * 256,
        traffic=8 * 2**20,
    )
    shared, after = call(
        functools.partial(sum_kernel, 1.0 / math.sqrt(64 * 1024)),
        [((64, *CHUNK), bf16), TOKEN],
        (swapped, after),
        scratch=[pltpu.VMEM((8, *CHUNK), bf16), pltpu.SemaphoreType.DMA((8,))],
        to=(0,),
        traffic=2**20,
    )

    mine = lax.all_to_all(shared, RING, 0, 0, tiled=True)
    grad_feature, after = call(
        feature_kernel,
        [block, TOKEN],
        (cotangent, cx, *sides[1], rows_c, to, tx, mixing, after),
        scratch=[
            pltpu.VMEM((36, SLOTS, CHAN), bf16),
            pltpu.VMEM(((ROWS + 4) * 8, BAND * 512), f32),
            pltpu.VMEM((ROWS + 4, BASIS * SLOTS, CHAN), bf16),
            pltpu.VMEM((BAND * CELLS, 512), bf16),
            pltpu.VMEM((ROWS + 8, CELLS, CHAN), f32),
            pltpu.VMEM((BASIS * CHAN, CHAN), bf16),
            pltpu.SemaphoreType.DMA,
        ],
        hbm=(7,),
        flops=2 * 960 * 2304 * 256 + 2 * 20 * 160 * 512 * 256,
        traffic=8 * 2**20,
    )
    mine, grad_feature = lax.optimization_barrier((mine, grad_feature))
    theirs = send(mine, core=True)
    whole = ((BASIS, 32, 8, CHAN), f32)
    stage = [pltpu.VMEM((BASIS, 16, 8, CHAN), f32), pltpu.SemaphoreType.DMA((BASIS,))]
    (grad_weight,) = call(
        own_half_kernel, [whole], (mine,), scratch=stage, to=(0,), traffic=2 * 2**20, limit=8
    )
    (grad_weight,) = call(
        other_half_kernel,
        [whole],
        (theirs, grad_weight),
        scratch=stage,
        hbm=(1,),
        to=(0,),
        alias={1: 0},
        traffic=2 * 2**20,
        limit=8,
    )
    return (mixed, grad_feature, grad_weight.reshape(BASIS, CHAN, CHAN))


def solution(mesh):
    fine = Mesh(mesh.devices.reshape(SIZES), AXES)
    lat, lon = ("xl", "core"), ("y", "xh", "z")
    return jax.shard_map(
        shards,
        mesh=fine,
        in_specs=(P(lat, lon, None), P(lat, None, None), P(lat), P(lat), P(), P(lat, lon, None)),
        out_specs=(P(lat, lon, None), P(lat, lon, None), P()),
        check_vma=False,
    )
```

```python
import functools
import math

import jax
import jax.numpy as jnp
from jax import lax
from jax.experimental import pallas as pl
from jax.experimental.pallas import tpu as pltpu
from jax.sharding import Mesh, PartitionSpec as P

AXES = ("xl", "core", "y", "xh", "z")
SIZES = (2, 2, 4, 2, 4)
RING = ("xl", "y", "xh", "z")

ROWS = 16
CELLS = 32
SLOTS = 48
BASIS = 9
CHAN = 256
HALF = 128
BAND = 5
CHUNK = (9, 4, 128)
bf16 = jnp.bfloat16
f32 = jnp.float32


def moves(lat=False, core=False, lon=(0, 0)):
    pairs = []
    for xl in range(2):
        for c in range(2):
            for cell in range(32):
                source = (xl * 2 + c) * 32 + cell
                row = (xl ^ int(lat)) * 2 + (c ^ int(core))
                pairs.append((source, row * 32 + (cell + lon[c]) % 32))
    return pairs


def send(x, **way):
    return lax.ppermute(x, AXES, moves(**way))


def vmem(count):
    return [pl.BlockSpec(memory_space=pltpu.VMEM)] * count


HBM = pl.BlockSpec(memory_space=pltpu.HBM)


def mark(token):
    token[...] = jnp.zeros(token.shape, f32)


TOKEN = ((8, 128), jnp.float32)


def here():
    return lax.axis_index("xl"), lax.axis_index("core")


def call(kernel, outs, operands, scratch=(), flops=0, traffic=0, limit=24, hbm=(), to=(), alias=None):
    return pl.pallas_call(
        kernel,
        out_shape=[jax.ShapeDtypeStruct(*o) for o in outs],
        in_specs=[HBM if i in hbm else vmem(1)[0] for i in range(len(operands))],
        out_specs=[HBM if i in to else vmem(1)[0] for i in range(len(outs))],
        scratch_shapes=list(scratch),
        input_output_aliases=alias or {},
        compiler_params=pltpu.CompilerParams(vmem_limit_bytes=limit * 1024 * 1024),
        cost_estimate=pl.CostEstimate(flops=flops, bytes_accessed=traffic, transcendentals=0),
    )(*operands)


def column_kernel(f, own, other, edge):
    _, core = here()
    for side in range(2):

        @pl.when(core == side)
        def _():
            cells = slice(CELLS - 2, CELLS) if side == 0 else slice(0, 2)
            edge[0:ROWS] = own[f, :, cells, :]
            edge[ROWS : 2 * ROWS] = other[:, cells, :]


def boundary(xl, core):
    return [
        ((xl == side) & (core == (1 - side if part == 0 else side)), part, 14 * (1 - side))
        for side in range(2)
        for part in range(2)
    ]


def rows_of(part, first, count):
    return [slice(p * ROWS + first, p * ROWS + first + count) for p in (part, 1 - part)]


def row_kernel(f, own, other, near, far, to, tx, rows):
    xl, core = here()
    rows[:, 36:40, :] = jnp.zeros((2, 4, CHAN), bf16)
    for chosen, part, first in boundary(xl, core):

        @pl.when(chosen)
        def _():
            span = slice(first, first + 2)
            side, cross = rows_of(part, first, 2)
            rows[:, 0:CELLS, :] = (own.at[f], other)[part][span]
            rows[:, CELLS : CELLS + 2, :] = near[side]
            rows[:, CELLS + 2 : CELLS + 4, :] = far[cross]
            rows[0, 38:40, :] = (to, tx)[part][span]


def padded(dst, xl, core, own, other, near, far, rows, lanes):
    width = dst.shape[-1]
    dst[:, 36:SLOTS, :] = jnp.zeros((36, SLOTS - 36, width), bf16)
    for part, ref in enumerate((own, other)):
        at = pl.ds(2 + ROWS * (core if part == 0 else 1 - core), ROWS)
        side, cross = rows_of(part, 0, ROWS)
        dst[at, 0:CELLS, :] = ref[:, :, lanes]
        dst[at, CELLS : CELLS + 2, :] = near[side, :, lanes]
        dst[at, CELLS + 2 : CELLS + 4, :] = far[cross, :, lanes]
    if rows is None:
        dst[0:2] = jnp.zeros((2, SLOTS, width), bf16)
        dst[34:36] = jnp.zeros((2, SLOTS, width), bf16)
    else:
        dst[pl.ds(34 * (1 - xl), 2), 0:36, :] = rows[:, 0:36, lanes]
        dst[pl.ds(34 * xl, 2)] = jnp.zeros((2, SLOTS, width), bf16)


def over(index, divisor):
    return ((index.astype(f32) + 0.5) * (1.0 / divisor)).astype(jnp.int32)


def split_taps(index):
    k = over(index, 25)
    tap = index - 25 * k
    b = over(tap, 5)
    return k, b, tap - 5 * b


def iota(shape, axis):
    return lax.broadcasted_iota(jnp.int32, shape, axis)


def band_masks(lanes):
    _, core = here()
    cell = iota((CELLS, lanes), 0)
    lane = iota((CELLS, lanes), 1)
    slot = lane - SLOTS * over(lane, SLOTS)
    side = jnp.where(slot < CELLS + 2, slot - 34 * (1 - core), slot - 2 - 34 * core)
    place = jnp.where(slot < CELLS, slot, jnp.where(slot < CELLS + 4, side, 1000))
    return [(place - cell + 2) == s for s in range(BAND)]


def band(block, masks, lanes, row):
    total = jnp.zeros((CELLS, lanes), f32)
    for s in range(BAND):
        line = block[pl.ds(row, 1), s * lanes : (s + 1) * lanes]
        total = jnp.where(masks[s], jnp.broadcast_to(line, (CELLS, lanes)), total)
    return total.astype(bf16)


def one_hot(row, group, offset, count, total):
    column = iota((total, count), 1)
    return (over(row, group) == column + offset).astype(f32).astype(bf16)


def spread(rep, keep, row_key, lanes, inner):
    lane = iota((1, BAND * lanes), 1)
    s = over(lane, lanes)
    o = over(lane - lanes * s, SLOTS)
    lane_key = jnp.where(o < inner, o * BAND + s, -2)
    table = jnp.where(row_key == lane_key, 1.0, 0.0).astype(bf16)
    kept = jnp.where(keep, rep, 0.0).astype(bf16)
    return jnp.dot(kept, table, preferred_element_type=f32)


def band_table():
    lane = iota((1, BAND * CHAN), 1)
    s = over(lane, CHAN)
    b = over(lane - CHAN * s, SLOTS)
    key = jnp.where(b < BAND, b * BAND + s, -1)
    return jnp.where(iota((25, 1), 0) == key, 1.0, 0.0).astype(bf16)


def tap_lines(taps, lines):
    lines[...] = jnp.dot(
        taps[...].reshape(BASIS * ROWS, 25), band_table(), preferred_element_type=f32
    )


def all_bands(taps, bands, lines):
    tap_lines(taps, lines)
    masks = band_masks(CHAN)

    def step(n, carry):
        for k in range(BASIS):
            line = band(lines, masks, CHAN, k * ROWS + n)
            bands[n, k * CELLS : (k + 1) * CELLS, :] = line
        return carry

    lax.fori_loop(0, ROWS, step, 0, unroll=4)


def own_band_kernel(mo, own, after, bo, cot_t, to, lines):
    to[...] = flat_taps(mo)
    all_bands(mo, bo, lines)
    cot_t[...] = own[1].reshape(512, CHAN).T


def other_band_kernel(mx, cx, after, bx, cot_t, tx, lines):
    tx[...] = flat_taps(mx)
    all_bands(mx, bx, lines)
    cot_t[...] = cx[...].reshape(512, CHAN).T


def flat_taps(taps):
    total = jnp.zeros((ROWS, CHAN), f32)
    for k in range(BASIS):
        at = iota((25, CHAN), 1) == iota((25, CHAN), 0) + 25 * k
        total += jnp.dot(taps[k], at.astype(f32).astype(bf16), preferred_element_type=f32)
    return total.astype(bf16)


def weight_kernel(own, fx, near, far, bo, bx, ct_o, ct_x, grad, field, basis):
    xl, core = here()
    lanes = pl.ds(pl.multiple_of(core * HALF, HALF), HALF)
    padded(field, xl, core, own.at[0], fx, near, far, None, lanes)

    for part, bands in enumerate((bo, bx)):
        begin = ROWS * (core if part == 0 else 1 - core)

        def step(n, carry):
            window = field[pl.ds(begin + n, BAND)].reshape(BAND * SLOTS, HALF)
            out = jnp.dot(
                bands[n, :, 0 : BAND * SLOTS], window, preferred_element_type=f32
            ).astype(bf16)
            at = pl.ds(pl.multiple_of((part * ROWS + n) * CELLS, CELLS), CELLS)
            for k in range(BASIS):
                basis[at, k * HALF : (k + 1) * HALF] = out[k * CELLS : (k + 1) * CELLS]
            return carry

        lax.fori_loop(0, ROWS, step, 0, unroll=16)
    for chosen, part, first in boundary(xl, core):

        @pl.when(chosen)
        def _():
            at = (part * ROWS + first) * CELLS
            basis[at : at + 2 * CELLS, :] = jnp.zeros((2 * CELLS, BASIS * HALF), bf16)

    total = jnp.dot(ct_o[...], basis[0:512, :], preferred_element_type=f32)
    total += jnp.dot(ct_x[...], basis[512:1024, :], preferred_element_type=f32)
    for k in range(BASIS):
        grad[k] = total[:, k * HALF : (k + 1) * HALF].T


def quarters():
    for side in range(2):
        for half in range(2):
            first = (half * 2 + side) * 16
            lanes = slice(side * HALF, (side + 1) * HALF)
            yield slice(first, first + 16), slice(half * 4, (half + 1) * 4), lanes


def weight_end_kernel(
    own, fx, cx, near, far, rows, bo, bx, grad, out, token,
    field, cot, tile, parts, sems
):
    mark(token)
    xl, core = here()
    lanes = pl.ds(pl.multiple_of(core * HALF, HALF), HALF)
    field[:, 36:SLOTS, :] = jnp.zeros((6, SLOTS - 36, HALF), bf16)
    field[pl.ds(4 * (1 - xl), 2), 0:36, :] = rows[:, 0:36, lanes]
    for chosen, part, first in boundary(xl, core):

        @pl.when(chosen)
        def _():
            ref = (own.at[0], fx)[part]
            at = 2 if first == 0 else 0
            begin = 0 if first == 0 else 12
            side, cross = rows_of(part, begin, 4)
            field[at : at + 4, 0:CELLS, :] = ref[begin : begin + 4, :, lanes]
            field[at : at + 4, CELLS : CELLS + 2, :] = near[side, :, lanes]
            field[at : at + 4, CELLS + 2 : CELLS + 4, :] = far[cross, :, lanes]
            cot[...] = (own.at[1], cx)[part][first : first + 2].reshape(2 * CELLS, CHAN)
            tile[...] = (bo, bx)[part][first : first + 2]

    basis = []
    for r in range(2):
        window = field[r : r + BAND].reshape(BAND * SLOTS, HALF)
        basis.append(
            jnp.dot(tile[r, :, 0 : BAND * SLOTS], window, preferred_element_type=f32)
        )
    sends = []
    for k in range(BASIS):
        cells = jnp.concatenate([x[k * CELLS : (k + 1) * CELLS] for x in basis], 0)
        total = grad[k] + jnp.dot(cells.T.astype(bf16), cot[...], preferred_element_type=f32)
        tiles = total.reshape(16, 8, CHAN)
        for chunks, rows_, columns in quarters():
            parts[chunks, k] = tiles[:, rows_, columns].astype(bf16)
        sends.append(pltpu.make_async_copy(parts.at[:, k], out.at[:, k], sems.at[k]))
        sends[-1].start()
    for x in sends:
        x.wait()


def sum_kernel(scale, parts, after, out, token, copies, sems):
    mark(token)
    total = jnp.sum(parts[...].astype(f32), axis=0) * scale
    copies[...] = jnp.broadcast_to(total.astype(bf16)[None], copies.shape)
    sends = [
        pltpu.make_async_copy(copies, out.at[i * 8 : (i + 1) * 8], sems.at[i]) for i in range(8)
    ]
    for x in sends:
        x.start()
    for x in sends:
        x.wait()


def half_kernel(half_of, tiles_ref, out, stage, sems):
    first = half_of() * 16
    copies = []
    for k in range(BASIS):
        for chunks, rows_, columns in quarters():
            stage[k, :, rows_, columns] = tiles_ref[chunks, k].astype(f32)
        copies.append(
            pltpu.make_async_copy(stage.at[k], out.at[k, pl.ds(first, 16)], sems.at[k])
        )
        copies[-1].start()
    for copy in copies:
        copy.wait()


def own_half_kernel(mine, out, stage, sems):
    half_kernel(lambda: here()[1], mine, out, stage, sems)


def other_half_kernel(theirs, before, out, stage, sems):
    half_kernel(lambda: 1 - here()[1], theirs, out, stage, sems)


def mixed_kernel(
    fo, fx, near, far, rows, mo, w_hbm, after, out, token,
    field, basis, weight, bands, lines, sems
):
    mark(token)
    xl, core = here()
    copy = pltpu.make_async_copy(w_hbm, weight, sems)
    copy.start()
    padded(field, xl, core, fo, fx, near, far, rows, slice(None))
    tap_lines(mo, lines)
    masks = band_masks(CHAN)
    for n in range(ROWS):
        for k in range(BASIS):
            line = band(lines, masks, CHAN, k * ROWS + n)
            bands[n, k * CELLS : (k + 1) * CELLS, :] = line
        window = field[pl.ds(core * ROWS + n, BAND)].reshape(BAND * SLOTS, CHAN)
        part = jnp.dot(
            bands[n, :, 0 : BAND * SLOTS], window, preferred_element_type=f32
        ).astype(bf16)
        for k in range(BASIS):
            basis[n * CELLS : (n + 1) * CELLS, k * CHAN : (k + 1) * CHAN] = part[
                k * CELLS : (k + 1) * CELLS
            ]
    copy.wait()
    out[...] = (
        jnp.dot(basis[...], weight[...], preferred_element_type=f32)
        .astype(bf16)
        .reshape(ROWS, CELLS, CHAN)
    )


def feature_kernel(
    co, cx, near, far, rows, to, tx, w_hbm, after, out, token, field, lines, grads, bands, total,
    weight, sems
):
    mark(token)
    copy = pltpu.make_async_copy(w_hbm, weight, sems)
    copy.start()
    xl, core = here()
    lanes = 512
    around = ROWS + 4
    padded(field, xl, core, co, cx, near, far, rows, slice(None))

    count = around * 8
    row = iota((count, 1), 0)
    beyond = 34 * (1 - xl) - core * ROWS
    other = 2 + (1 - 2 * core) * ROWS
    rep = jnp.dot(one_hot(row, 8, 2, 16, count), to[...], preferred_element_type=f32)
    rep += jnp.dot(one_hot(row, 8, other, 16, count), tx[...], preferred_element_type=f32)
    rep += jnp.dot(
        one_hot(row, 8, beyond, 2, count), rows[0, 38:40, :], preferred_element_type=f32
    )
    _, b, _ = split_taps(iota((1, CHAN), 1))
    k, _, s = split_taps(iota((CHAN, 1), 0))
    lines[...] = spread(rep, b == row - 8 * over(row, 8), k * BAND + 4 - s, lanes, BASIS)
    masks = band_masks(lanes)
    copy.wait()
    for k in range(BASIS):
        for h in range(2):
            upstream = field[pl.ds(core * ROWS + h * 10, 10)].reshape(10 * SLOTS, CHAN)
            back = lax.dot_general(
                upstream,
                weight[k * CHAN : (k + 1) * CHAN, :],
                (((1,), (1,)), ((), ())),
                preferred_element_type=f32,
            )
            grads[h * 10 : (h + 1) * 10, k * SLOTS : (k + 1) * SLOTS, :] = back.astype(
                bf16
            ).reshape(10, SLOTS, CHAN)
    total[...] = jnp.zeros_like(total)

    def step(i, carry):
        for b in range(BAND):
            bands[b * CELLS : (b + 1) * CELLS, :] = band(lines, masks, lanes, i * 8 + b)
        part = jnp.dot(
            bands[:, 0 : BASIS * SLOTS], grads[i], preferred_element_type=f32
        ).reshape(BAND, CELLS, CHAN)
        total[pl.ds(i, BAND)] += part
        return carry

    lax.fori_loop(0, around, step, 0, unroll=4)
    out[...] = total[4 : 4 + ROWS].astype(bf16)


def shards(feature, filters, start, length, weight, cotangent):
    fx = send(feature, core=True)
    cx = send(cotangent, core=True)
    own = jnp.stack([feature, cotangent])

    block = ((ROWS, CELLS, CHAN), bf16)
    tiles = ((ROWS, BASIS * CELLS, CHAN), bf16)
    flat = ((ROWS, CHAN), bf16)
    lines = pltpu.VMEM((BASIS * ROWS, BAND * CHAN), f32)
    column = ((2 * ROWS, 2, CHAN), bf16)
    edges = [
        call(functools.partial(column_kernel, f), [column], (own, other), traffic=2**20, limit=8)[0]
        for f, other in enumerate((fx, cx))
    ]
    near_f = send(edges[0], lon=(1, -1))
    near_c = send(edges[1], lon=(1, -1))
    edge, start = lax.optimization_barrier((edges[0], start))
    lat = lax.axis_index("xl") * 2 + lax.axis_index("core")
    source = lat * ROWS + jnp.arange(ROWS, dtype=jnp.int32)[:, None] - 2
    source = source + jnp.arange(25, dtype=jnp.int32)[None, :] // BAND - start[:, None]
    inside = (source >= 0) & (source < length[:, None])
    mo = jnp.where(inside[None], filters.transpose(1, 0, 2), jnp.zeros((), bf16))
    mx = send(mo, core=True)

    turned = ((CHAN, 512), bf16)
    bo, ct_o, to = call(
        own_band_kernel,
        [tiles, turned, flat],
        (mo, own, edge),
        scratch=[lines],
        flops=2 * 144 * 256 * 1280,
        traffic=4 * 2**20,
        limit=16,
    )
    bx, ct_x, tx = call(
        other_band_kernel,
        [tiles, turned, flat],
        (mx, cx, to),
        scratch=[lines],
        flops=2 * 144 * 256 * 1280,
        traffic=4 * 2**20,
        limit=16,
    )
    near_f, bx = lax.optimization_barrier((near_f, bx))
    far_f = send(near_f, core=True)
    far_c = send(near_c, core=True)

    sides = ((near_f, far_f), (near_c, far_c))
    rows_f, rows_c = [
        send(
            call(
                functools.partial(row_kernel, f),
                [((2, 40, CHAN), bf16)],
                (own, other, *sides[f], to, tx),
                traffic=2**20,
            )[0],
            lat=True,
        )
        for f, other in enumerate((fx, cx))
    ]
    (grad,) = call(
        weight_kernel,
        [((BASIS, HALF, CHAN), f32)],
        (own, fx, *sides[0], bo, bx, ct_o, ct_x),
        scratch=[
            pltpu.VMEM((36, SLOTS, HALF), bf16),
            pltpu.VMEM((1024, BASIS * HALF), bf16),
        ],
        flops=2 * 32 * 288 * 256 * 256 + 2 * 1024 * 1152 * 256,
        traffic=7 * 2**20,
    )
    parts, after = call(
        weight_end_kernel,
        [((64, *CHUNK), bf16), TOKEN],
        (own, fx, cx, *sides[0], rows_f, bo, bx, grad),
        scratch=[
            pltpu.VMEM((6, SLOTS, HALF), bf16),
            pltpu.VMEM((2 * CELLS, CHAN), bf16),
            pltpu.VMEM((2, BASIS * CELLS, CHAN), bf16),
            pltpu.VMEM((64, *CHUNK), bf16),
            pltpu.SemaphoreType.DMA((BASIS,)),
        ],
        to=(0,),
        flops=2 * 64 * 1152 * 256,
        traffic=3 * 2**20,
    )
    mixing = weight.reshape(BASIS * CHAN, CHAN)

    parts, rows_c = lax.optimization_barrier((parts, rows_c))
    swapped = lax.all_to_all(parts, RING, 0, 0, tiled=True)
    grad_feature, after = call(
        feature_kernel,
        [block, TOKEN],
        (cotangent, cx, *sides[1], rows_c, to, tx, mixing, after),
        scratch=[
            pltpu.VMEM((36, SLOTS, CHAN), bf16),
            pltpu.VMEM(((ROWS + 4) * 8, BAND * 512), f32),
            pltpu.VMEM((ROWS + 4, BASIS * SLOTS, CHAN), bf16),
            pltpu.VMEM((BAND * CELLS, 512), bf16),
            pltpu.VMEM((ROWS + 8, CELLS, CHAN), f32),
            pltpu.VMEM((BASIS * CHAN, CHAN), bf16),
            pltpu.SemaphoreType.DMA,
        ],
        hbm=(7,),
        flops=2 * 960 * 2304 * 256 + 2 * 20 * 160 * 512 * 256,
        traffic=8 * 2**20,
    )
    shared, after = call(
        functools.partial(sum_kernel, 1.0 / math.sqrt(64 * 1024)),
        [((64, *CHUNK), bf16), TOKEN],
        (swapped, after),
        scratch=[pltpu.VMEM((8, *CHUNK), bf16), pltpu.SemaphoreType.DMA((8,))],
        to=(0,),
        traffic=2**20,
    )

    mine = lax.all_to_all(shared, RING, 0, 0, tiled=True)
    mixed, after = call(
        mixed_kernel,
        [block, TOKEN],
        (feature, fx, *sides[0], rows_f, mo, mixing, after),
        scratch=[
            pltpu.VMEM((36, SLOTS, CHAN), bf16),
            pltpu.VMEM((512, BASIS * CHAN), bf16),
            pltpu.VMEM((BASIS * CHAN, CHAN), bf16),
            pltpu.VMEM((ROWS, BASIS * CELLS, CHAN), bf16),
            lines,
            pltpu.SemaphoreType.DMA,
        ],
        hbm=(6,),
        flops=2 * 16 * 288 * 256 * 256 + 2 * 512 * 2304 * 256,
        traffic=8 * 2**20,
    )
    mine, mixed = lax.optimization_barrier((mine, mixed))
    theirs = send(mine, core=True)
    whole = ((BASIS, 32, 8, CHAN), f32)
    stage = [pltpu.VMEM((BASIS, 16, 8, CHAN), f32), pltpu.SemaphoreType.DMA((BASIS,))]
    (grad_weight,) = call(
        own_half_kernel, [whole], (mine,), scratch=stage, to=(0,), traffic=2 * 2**20, limit=8
    )
    (grad_weight,) = call(
        other_half_kernel,
        [whole],
        (theirs, grad_weight),
        scratch=stage,
        hbm=(1,),
        to=(0,),
        alias={1: 0},
        traffic=2 * 2**20,
        limit=8,
    )
    return (mixed, grad_feature, grad_weight.reshape(BASIS, CHAN, CHAN))


def solution(mesh):
    fine = Mesh(mesh.devices.reshape(SIZES), AXES)
    lat, lon = ("xl", "core"), ("y", "xh", "z")
    return jax.shard_map(
        shards,
        mesh=fine,
        in_specs=(P(lat, lon, None), P(lat, None, None), P(lat), P(lat), P(), P(lat, lon, None)),
        out_specs=(P(lat, lon, None), P(lat, lon, None), P()),
        check_vma=False,
    )
```

```python
import functools
import math

import jax
import jax.numpy as jnp
from jax import lax
from jax.experimental import pallas as pl
from jax.experimental.pallas import tpu as pltpu
from jax.sharding import Mesh, PartitionSpec as P

AXES = ("xl", "core", "y", "xh", "z")
SIZES = (2, 2, 4, 2, 4)
RING = ("xl", "y", "xh", "z")

ROWS = 16
CELLS = 32
SLOTS = 48
BASIS = 9
CHAN = 256
HALF = 128
BAND = 5
CHUNK = (9, 4, 128)
bf16 = jnp.bfloat16
f32 = jnp.float32


def moves(lat=False, core=False, lon=(0, 0)):
    pairs = []
    for xl in range(2):
        for c in range(2):
            for cell in range(32):
                source = (xl * 2 + c) * 32 + cell
                row = (xl ^ int(lat)) * 2 + (c ^ int(core))
                pairs.append((source, row * 32 + (cell + lon[c]) % 32))
    return pairs


def send(x, **way):
    return lax.ppermute(x, AXES, moves(**way))


def vmem(count):
    return [pl.BlockSpec(memory_space=pltpu.VMEM)] * count


HBM = pl.BlockSpec(memory_space=pltpu.HBM)


def mark(token):
    token[...] = jnp.zeros(token.shape, f32)


TOKEN = ((8, 128), jnp.float32)


def here():
    return lax.axis_index("xl"), lax.axis_index("core")


def call(kernel, outs, operands, scratch=(), flops=0, traffic=0, limit=24, hbm=(), to=(), alias=None):
    return pl.pallas_call(
        kernel,
        out_shape=[jax.ShapeDtypeStruct(*o) for o in outs],
        in_specs=[HBM if i in hbm else vmem(1)[0] for i in range(len(operands))],
        out_specs=[HBM if i in to else vmem(1)[0] for i in range(len(outs))],
        scratch_shapes=list(scratch),
        input_output_aliases=alias or {},
        compiler_params=pltpu.CompilerParams(vmem_limit_bytes=limit * 1024 * 1024),
        cost_estimate=pl.CostEstimate(flops=flops, bytes_accessed=traffic, transcendentals=0),
    )(*operands)


def column_kernel(f, own, other, edge):
    _, core = here()
    for side in range(2):

        @pl.when(core == side)
        def _():
            cells = slice(CELLS - 2, CELLS) if side == 0 else slice(0, 2)
            edge[0:ROWS] = own[f, :, cells, :]
            edge[ROWS : 2 * ROWS] = other[:, cells, :]


def boundary(xl, core):
    return [
        ((xl == side) & (core == (1 - side if part == 0 else side)), part, 14 * (1 - side))
        for side in range(2)
        for part in range(2)
    ]


def rows_of(part, first, count):
    return [slice(p * ROWS + first, p * ROWS + first + count) for p in (part, 1 - part)]


def row_kernel(f, own, other, near, far, to, tx, rows):
    xl, core = here()
    rows[:, 36:40, :] = jnp.zeros((2, 4, CHAN), bf16)
    for chosen, part, first in boundary(xl, core):

        @pl.when(chosen)
        def _():
            span = slice(first, first + 2)
            side, cross = rows_of(part, first, 2)
            rows[:, 0:CELLS, :] = (own.at[f], other)[part][span]
            rows[:, CELLS : CELLS + 2, :] = near[side]
            rows[:, CELLS + 2 : CELLS + 4, :] = far[cross]
            rows[0, 38:40, :] = (to, tx)[part][span]


def padded(dst, xl, core, own, other, near, far, rows, lanes):
    width = dst.shape[-1]
    dst[:, 36:SLOTS, :] = jnp.zeros((36, SLOTS - 36, width), bf16)
    for part, ref in enumerate((own, other)):
        at = pl.ds(2 + ROWS * (core if part == 0 else 1 - core), ROWS)
        side, cross = rows_of(part, 0, ROWS)
        dst[at, 0:CELLS, :] = ref[:, :, lanes]
        dst[at, CELLS : CELLS + 2, :] = near[side, :, lanes]
        dst[at, CELLS + 2 : CELLS + 4, :] = far[cross, :, lanes]
    if rows is None:
        dst[0:2] = jnp.zeros((2, SLOTS, width), bf16)
        dst[34:36] = jnp.zeros((2, SLOTS, width), bf16)
    else:
        dst[pl.ds(34 * (1 - xl), 2), 0:36, :] = rows[:, 0:36, lanes]
        dst[pl.ds(34 * xl, 2)] = jnp.zeros((2, SLOTS, width), bf16)


def over(index, divisor):
    return ((index.astype(f32) + 0.5) * (1.0 / divisor)).astype(jnp.int32)


def split_taps(index):
    k = over(index, 25)
    tap = index - 25 * k
    b = over(tap, 5)
    return k, b, tap - 5 * b


def iota(shape, axis):
    return lax.broadcasted_iota(jnp.int32, shape, axis)


def band_masks(lanes):
    _, core = here()
    cell = iota((CELLS, lanes), 0)
    lane = iota((CELLS, lanes), 1)
    slot = lane - SLOTS * over(lane, SLOTS)
    side = jnp.where(slot < CELLS + 2, slot - 34 * (1 - core), slot - 2 - 34 * core)
    place = jnp.where(slot < CELLS, slot, jnp.where(slot < CELLS + 4, side, 1000))
    return [(place - cell + 2) == s for s in range(BAND)]


def band(block, masks, lanes, row):
    total = jnp.zeros((CELLS, lanes), f32)
    for s in range(BAND):
        line = block[pl.ds(row, 1), s * lanes : (s + 1) * lanes]
        total = jnp.where(masks[s], jnp.broadcast_to(line, (CELLS, lanes)), total)
    return total.astype(bf16)


def one_hot(row, group, offset, count, total):
    column = iota((total, count), 1)
    return (over(row, group) == column + offset).astype(f32).astype(bf16)


def spread(rep, keep, row_key, lanes, inner):
    lane = iota((1, BAND * lanes), 1)
    s = over(lane, lanes)
    o = over(lane - lanes * s, SLOTS)
    lane_key = jnp.where(o < inner, o * BAND + s, -2)
    table = jnp.where(row_key == lane_key, 1.0, 0.0).astype(bf16)
    kept = jnp.where(keep, rep, 0.0).astype(bf16)
    return jnp.dot(kept, table, preferred_element_type=f32)


def band_table():
    lane = iota((1, BAND * CHAN), 1)
    s = over(lane, CHAN)
    b = over(lane - CHAN * s, SLOTS)
    key = jnp.where(b < BAND, b * BAND + s, -1)
    return jnp.where(iota((25, 1), 0) == key, 1.0, 0.0).astype(bf16)


def tap_lines(taps, lines):
    lines[...] = jnp.dot(
        taps[...].reshape(BASIS * ROWS, 25), band_table(), preferred_element_type=f32
    )


def all_bands(taps, bands, lines):
    tap_lines(taps, lines)
    masks = band_masks(CHAN)

    def step(n, carry):
        for k in range(BASIS):
            line = band(lines, masks, CHAN, k * ROWS + n)
            bands[n, k * CELLS : (k + 1) * CELLS, :] = line
        return carry

    lax.fori_loop(0, ROWS, step, 0, unroll=4)


def own_band_kernel(mo, own, after, bo, cot_t, to, lines):
    to[...] = flat_taps(mo)
    all_bands(mo, bo, lines)
    cot_t[...] = own[1].reshape(512, CHAN).T


def other_band_kernel(mx, cx, after, bx, cot_t, tx, lines):
    tx[...] = flat_taps(mx)
    all_bands(mx, bx, lines)
    cot_t[...] = cx[...].reshape(512, CHAN).T


def flat_taps(taps):
    total = jnp.zeros((ROWS, CHAN), f32)
    for k in range(BASIS):
        at = iota((25, CHAN), 1) == iota((25, CHAN), 0) + 25 * k
        total += jnp.dot(taps[k], at.astype(f32).astype(bf16), preferred_element_type=f32)
    return total.astype(bf16)


def weight_kernel(own, fx, near, far, bo, bx, ct_o, ct_x, grad, field, basis):
    xl, core = here()
    lanes = pl.ds(pl.multiple_of(core * HALF, HALF), HALF)
    padded(field, xl, core, own.at[0], fx, near, far, None, lanes)

    for part, bands in enumerate((bo, bx)):
        begin = ROWS * (core if part == 0 else 1 - core)

        def step(n, carry):
            window = field[pl.ds(begin + n, BAND)].reshape(BAND * SLOTS, HALF)
            out = jnp.dot(
                bands[n, :, 0 : BAND * SLOTS], window, preferred_element_type=f32
            ).astype(bf16)
            at = pl.ds(pl.multiple_of((part * ROWS + n) * CELLS, CELLS), CELLS)
            for k in range(BASIS):
                basis[at, k * HALF : (k + 1) * HALF] = out[k * CELLS : (k + 1) * CELLS]
            return carry

        lax.fori_loop(0, ROWS, step, 0, unroll=16)
    for chosen, part, first in boundary(xl, core):

        @pl.when(chosen)
        def _():
            at = (part * ROWS + first) * CELLS
            basis[at : at + 2 * CELLS, :] = jnp.zeros((2 * CELLS, BASIS * HALF), bf16)

    total = jnp.dot(ct_o[...], basis[0:512, :], preferred_element_type=f32)
    total += jnp.dot(ct_x[...], basis[512:1024, :], preferred_element_type=f32)
    for k in range(BASIS):
        grad[k] = total[:, k * HALF : (k + 1) * HALF].T


def quarters():
    for side in range(2):
        for half in range(2):
            first = (half * 2 + side) * 16
            lanes = slice(side * HALF, (side + 1) * HALF)
            yield slice(first, first + 16), slice(half * 4, (half + 1) * 4), lanes


def weight_end_kernel(
    own, fx, cx, near, far, rows, after, bo, bx, grad, out, token,
    field, cot, tile, parts, sems
):
    mark(token)
    xl, core = here()
    lanes = pl.ds(pl.multiple_of(core * HALF, HALF), HALF)
    field[:, 36:SLOTS, :] = jnp.zeros((6, SLOTS - 36, HALF), bf16)
    field[pl.ds(4 * (1 - xl), 2), 0:36, :] = rows[:, 0:36, lanes]
    for chosen, part, first in boundary(xl, core):

        @pl.when(chosen)
        def _():
            ref = (own.at[0], fx)[part]
            at = 2 if first == 0 else 0
            begin = 0 if first == 0 else 12
            side, cross = rows_of(part, begin, 4)
            field[at : at + 4, 0:CELLS, :] = ref[begin : begin + 4, :, lanes]
            field[at : at + 4, CELLS : CELLS + 2, :] = near[side, :, lanes]
            field[at : at + 4, CELLS + 2 : CELLS + 4, :] = far[cross, :, lanes]
            cot[...] = (own.at[1], cx)[part][first : first + 2].reshape(2 * CELLS, CHAN)
            tile[...] = (bo, bx)[part][first : first + 2]

    basis = []
    for r in range(2):
        window = field[r : r + BAND].reshape(BAND * SLOTS, HALF)
        basis.append(
            jnp.dot(tile[r, :, 0 : BAND * SLOTS], window, preferred_element_type=f32)
        )
    sends = []
    for k in range(BASIS):
        cells = jnp.concatenate([x[k * CELLS : (k + 1) * CELLS] for x in basis], 0)
        total = grad[k] + jnp.dot(cells.T.astype(bf16), cot[...], preferred_element_type=f32)
        tiles = total.reshape(16, 8, CHAN)
        for chunks, rows_, columns in quarters():
            parts[chunks, k] = tiles[:, rows_, columns].astype(bf16)
        sends.append(pltpu.make_async_copy(parts.at[:, k], out.at[:, k], sems.at[k]))
        sends[-1].start()
    for x in sends:
        x.wait()


def sum_kernel(scale, parts, after, out, token, copies, sems):
    mark(token)
    for k in range(BASIS):
        total = parts[0, k].astype(f32)
        for j in range(1, 64):
            total = total + parts[j, k].astype(f32)
        copies[:, k] = jnp.broadcast_to((total * scale).astype(bf16)[None], (16, 4, HALF))
    sends = [
        pltpu.make_async_copy(copies, out.at[i * 16 : (i + 1) * 16], sems.at[i]) for i in range(4)
    ]
    for x in sends:
        x.start()
    for x in sends:
        x.wait()


def half_kernel(half_of, tiles_ref, out, stage, sems):
    first = half_of() * 16
    copies = []
    for k in range(BASIS):
        for chunks, rows_, columns in quarters():
            stage[k, :, rows_, columns] = tiles_ref[chunks, k].astype(f32)
        copies.append(
            pltpu.make_async_copy(stage.at[k], out.at[k, pl.ds(first, 16)], sems.at[k])
        )
        copies[-1].start()
    for copy in copies:
        copy.wait()


def own_half_kernel(mine, out, stage, sems):
    half_kernel(lambda: here()[1], mine, out, stage, sems)


def other_half_kernel(theirs, before, out, stage, sems):
    half_kernel(lambda: 1 - here()[1], theirs, out, stage, sems)


def mixed_kernel(
    fo, fx, near, far, rows, mo, w_hbm, after, out, token,
    field, basis, weight, bands, lines, sems
):
    mark(token)
    xl, core = here()
    copy = pltpu.make_async_copy(w_hbm, weight, sems)
    copy.start()
    padded(field, xl, core, fo, fx, near, far, rows, slice(None))
    tap_lines(mo, lines)
    masks = band_masks(CHAN)
    for n in range(ROWS):
        for k in range(BASIS):
            line = band(lines, masks, CHAN, k * ROWS + n)
            bands[n, k * CELLS : (k + 1) * CELLS, :] = line
        window = field[pl.ds(core * ROWS + n, BAND)].reshape(BAND * SLOTS, CHAN)
        part = jnp.dot(
            bands[n, :, 0 : BAND * SLOTS], window, preferred_element_type=f32
        ).astype(bf16)
        for k in range(BASIS):
            basis[n * CELLS : (n + 1) * CELLS, k * CHAN : (k + 1) * CHAN] = part[
                k * CELLS : (k + 1) * CELLS
            ]
    copy.wait()
    out[...] = (
        jnp.dot(basis[...], weight[...], preferred_element_type=f32)
        .astype(bf16)
        .reshape(ROWS, CELLS, CHAN)
    )


def feature_kernel(
    co, cx, near, far, rows, to, tx, w_hbm, after, out, token, field, lines, grads, bands, total,
    weight, sems
):
    mark(token)
    copy = pltpu.make_async_copy(w_hbm, weight, sems)
    copy.start()
    xl, core = here()
    lanes = 512
    around = ROWS + 4
    padded(field, xl, core, co, cx, near, far, rows, slice(None))

    count = around * 8
    row = iota((count, 1), 0)
    beyond = 34 * (1 - xl) - core * ROWS
    other = 2 + (1 - 2 * core) * ROWS
    rep = jnp.dot(one_hot(row, 8, 2, 16, count), to[...], preferred_element_type=f32)
    rep += jnp.dot(one_hot(row, 8, other, 16, count), tx[...], preferred_element_type=f32)
    rep += jnp.dot(
        one_hot(row, 8, beyond, 2, count), rows[0, 38:40, :], preferred_element_type=f32
    )
    _, b, _ = split_taps(iota((1, CHAN), 1))
    k, _, s = split_taps(iota((CHAN, 1), 0))
    lines[...] = spread(rep, b == row - 8 * over(row, 8), k * BAND + 4 - s, lanes, BASIS)
    masks = band_masks(lanes)
    copy.wait()
    for k in range(BASIS):
        for h in range(2):
            upstream = field[pl.ds(core * ROWS + h * 10, 10)].reshape(10 * SLOTS, CHAN)
            back = lax.dot_general(
                upstream,
                weight[k * CHAN : (k + 1) * CHAN, :],
                (((1,), (1,)), ((), ())),
                preferred_element_type=f32,
            )
            grads[h * 10 : (h + 1) * 10, k * SLOTS : (k + 1) * SLOTS, :] = back.astype(
                bf16
            ).reshape(10, SLOTS, CHAN)
    total[...] = jnp.zeros_like(total)

    def step(i, carry):
        for b in range(BAND):
            bands[b * CELLS : (b + 1) * CELLS, :] = band(lines, masks, lanes, i * 8 + b)
        part = jnp.dot(
            bands[:, 0 : BASIS * SLOTS], grads[i], preferred_element_type=f32
        ).reshape(BAND, CELLS, CHAN)
        total[pl.ds(i, BAND)] += part
        return carry

    lax.fori_loop(0, around, step, 0, unroll=4)
    out[...] = total[4 : 4 + ROWS].astype(bf16)


def shards(feature, filters, start, length, weight, cotangent):
    fx = send(feature, core=True)
    cx = send(cotangent, core=True)
    own = jnp.stack([feature, cotangent])

    block = ((ROWS, CELLS, CHAN), bf16)
    tiles = ((ROWS, BASIS * CELLS, CHAN), bf16)
    flat = ((ROWS, CHAN), bf16)
    lines = pltpu.VMEM((BASIS * ROWS, BAND * CHAN), f32)
    column = ((2 * ROWS, 2, CHAN), bf16)
    edges = [
        call(functools.partial(column_kernel, f), [column], (own, other), traffic=2**20, limit=8)[0]
        for f, other in enumerate((fx, cx))
    ]
    near_f = send(edges[0], lon=(1, -1))
    near_c = send(edges[1], lon=(1, -1))
    edge, start = lax.optimization_barrier((edges[0], start))
    lat = lax.axis_index("xl") * 2 + lax.axis_index("core")
    source = lat * ROWS + jnp.arange(ROWS, dtype=jnp.int32)[:, None] - 2
    source = source + jnp.arange(25, dtype=jnp.int32)[None, :] // BAND - start[:, None]
    inside = (source >= 0) & (source < length[:, None])
    mo = jnp.where(inside[None], filters.transpose(1, 0, 2), jnp.zeros((), bf16))
    mx = send(mo, core=True)

    turned = ((CHAN, 512), bf16)
    bo, ct_o, to = call(
        own_band_kernel,
        [tiles, turned, flat],
        (mo, own, edge),
        scratch=[lines],
        flops=2 * 144 * 256 * 1280,
        traffic=4 * 2**20,
        limit=16,
    )
    bx, ct_x, tx = call(
        other_band_kernel,
        [tiles, turned, flat],
        (mx, cx, to),
        scratch=[lines],
        flops=2 * 144 * 256 * 1280,
        traffic=4 * 2**20,
        limit=16,
    )
    near_f, bx = lax.optimization_barrier((near_f, bx))
    far_f = send(near_f, core=True)
    far_c = send(near_c, core=True)

    sides = ((near_f, far_f), (near_c, far_c))
    rows_f, rows_c = [
        send(
            call(
                functools.partial(row_kernel, f),
                [((2, 40, CHAN), bf16)],
                (own, other, *sides[f], to, tx),
                traffic=2**20,
            )[0],
            lat=True,
        )
        for f, other in enumerate((fx, cx))
    ]
    (grad,) = call(
        weight_kernel,
        [((BASIS, HALF, CHAN), f32)],
        (own, fx, *sides[0], bo, bx, ct_o, ct_x),
        scratch=[
            pltpu.VMEM((36, SLOTS, HALF), bf16),
            pltpu.VMEM((1024, BASIS * HALF), bf16),
        ],
        flops=2 * 32 * 288 * 256 * 256 + 2 * 1024 * 1152 * 256,
        traffic=7 * 2**20,
    )
    parts, after = call(
        weight_end_kernel,
        [((64, *CHUNK), bf16), TOKEN],
        (own, fx, cx, *sides[0], rows_f, rows_c, bo, bx, grad),
        scratch=[
            pltpu.VMEM((6, SLOTS, HALF), bf16),
            pltpu.VMEM((2 * CELLS, CHAN), bf16),
            pltpu.VMEM((2, BASIS * CELLS, CHAN), bf16),
            pltpu.VMEM((64, *CHUNK), bf16),
            pltpu.SemaphoreType.DMA((BASIS,)),
        ],
        to=(0,),
        flops=2 * 64 * 1152 * 256,
        traffic=3 * 2**20,
    )
    mixing = weight.reshape(BASIS * CHAN, CHAN)

    swapped = lax.all_to_all(parts, RING, 0, 0, tiled=True)
    mixed, after = call(
        mixed_kernel,
        [block, TOKEN],
        (feature, fx, *sides[0], rows_f, mo, mixing, after),
        scratch=[
            pltpu.VMEM((36, SLOTS, CHAN), bf16),
            pltpu.VMEM((512, BASIS * CHAN), bf16),
            pltpu.VMEM((BASIS * CHAN, CHAN), bf16),
            pltpu.VMEM((ROWS, BASIS * CELLS, CHAN), bf16),
            lines,
            pltpu.SemaphoreType.DMA,
        ],
        hbm=(6,),
        flops=2 * 16 * 288 * 256 * 256 + 2 * 512 * 2304 * 256,
        traffic=8 * 2**20,
    )
    shared, after = call(
        functools.partial(sum_kernel, 1.0 / math.sqrt(64 * 1024)),
        [((64, *CHUNK), bf16), TOKEN],
        (swapped, after),
        scratch=[pltpu.VMEM((16, *CHUNK), bf16), pltpu.SemaphoreType.DMA((4,))],
        to=(0,),
        traffic=2**20,
    )

    mine = lax.all_to_all(shared, RING, 0, 0, tiled=True)
    grad_feature, after = call(
        feature_kernel,
        [block, TOKEN],
        (cotangent, cx, *sides[1], rows_c, to, tx, mixing, after),
        scratch=[
            pltpu.VMEM((36, SLOTS, CHAN), bf16),
            pltpu.VMEM(((ROWS + 4) * 8, BAND * 512), f32),
            pltpu.VMEM((ROWS + 4, BASIS * SLOTS, CHAN), bf16),
            pltpu.VMEM((BAND * CELLS, 512), bf16),
            pltpu.VMEM((ROWS + 8, CELLS, CHAN), f32),
            pltpu.VMEM((BASIS * CHAN, CHAN), bf16),
            pltpu.SemaphoreType.DMA,
        ],
        hbm=(7,),
        flops=2 * 960 * 2304 * 256 + 2 * 20 * 160 * 512 * 256,
        traffic=8 * 2**20,
    )
    mine, grad_feature = lax.optimization_barrier((mine, grad_feature))
    theirs = send(mine, core=True)
    whole = ((BASIS, 32, 8, CHAN), f32)
    stage = [pltpu.VMEM((BASIS, 16, 8, CHAN), f32), pltpu.SemaphoreType.DMA((BASIS,))]
    (grad_weight,) = call(
        own_half_kernel, [whole], (mine,), scratch=stage, to=(0,), traffic=2 * 2**20, limit=8
    )
    (grad_weight,) = call(
        other_half_kernel,
        [whole],
        (theirs, grad_weight),
        scratch=stage,
        hbm=(1,),
        to=(0,),
        alias={1: 0},
        traffic=2 * 2**20,
        limit=8,
    )
    return (mixed, grad_feature, grad_weight.reshape(BASIS, CHAN, CHAN))


def solution(mesh):
    fine = Mesh(mesh.devices.reshape(SIZES), AXES)
    lat, lon = ("xl", "core"), ("y", "xh", "z")
    return jax.shard_map(
        shards,
        mesh=fine,
        in_specs=(P(lat, lon, None), P(lat, None, None), P(lat), P(lat), P(), P(lat, lon, None)),
        out_specs=(P(lat, lon, None), P(lat, lon, None), P()),
        check_vma=False,
    )
```
